32 devices in a mesh: dp: 4 (over y, x), fsdp: 8 (over z, core).
Axes of the slice: x: 2, y: 2, z: 4, core: 2. Of those that a mesh axis runs over, the one named last changes fastest.
Arguments:
- tokens: bfloat16 [2, 2048, 896], P(None, ('dp', 'fsdp')), may hold values from -6 to 6
- cotangent: bfloat16 [2, 2048, 896], P(None, ('dp', 'fsdp')), may hold values from -6 to 6
- lengths: int32 [2, 4, 8], P(None, 'dp'), may hold values from 1 to 128, 512 in all within a row
- deal: int32 [2, 4, 8], P(None, 'dp'), may hold values from 0 to 7, each once within a row
- pool: bfloat16 [2, 96, 128, 896], P(None, ('dp', 'fsdp')), may hold values from -6 to 6
- neighbour_ids: int32 [2, 64, 2], P(None, ('dp', 'fsdp')), may hold values from 0 to 2
- norm1_gain: bfloat16 [896], P(('dp', 'fsdp')), may hold values from 0.5 to 1.5
- attn_qkv: bfloat16 [896, 3072], P(('dp', 'fsdp')), may hold values from -0.1875 to 0.1875
- attn_out: bfloat16 [1024, 896], P(('dp', 'fsdp')), may hold values from -0.5 to 0.5
- attn_out_bias: bfloat16 [896], P(('dp', 'fsdp')), may hold values from -3 to 3
- rel_table: bfloat16 [1024], P(('dp', 'fsdp')), may hold values from -4 to 4
- norm2_gain: bfloat16 [896], P(('dp', 'fsdp')), may hold values from 0.5 to 1.5
- cca_query: bfloat16 [896, 1024], P(('dp', 'fsdp')), may hold values from -0.1875 to 0.1875
- cca_kv: bfloat16 [896, 2048], P(('dp', 'fsdp')), may hold values from -0.1875 to 0.1875
- cca_out: bfloat16 [1024, 896], P(('dp', 'fsdp')), may hold values from -0.5 to 0.5
- cca_out_bias: bfloat16 [896], P(('dp', 'fsdp')), may hold values from -3 to 3
- norm3_gain: bfloat16 [896], P(('dp', 'fsdp')), may hold values from 0.5 to 1.5
- ffw_up: bfloat16 [896, 3584], P(('dp', 'fsdp')), may hold values from -0.1875 to 0.1875
- ffw_up_bias: bfloat16 [3584], P(('dp', 'fsdp')), may hold values from -3 to 3
- ffw_down: bfloat16 [3584, 896], P(('dp', 'fsdp')), may hold values from -0.1875 to 0.1875
- ffw_down_bias: bfloat16 [896], P(('dp', 'fsdp')), may hold values from -3 to 3
Outputs:
- activations: bfloat16 [2, 2048, 896], P(None, ('dp', 'fsdp'))
- input_grad: bfloat16 [2, 2048, 896], P(None, ('dp', 'fsdp'))
- pool_grad: float32 [2, 96, 128, 896], P(None, ('dp', 'fsdp'))
- grad_norm1_gain: float32 [896], P(('dp', 'fsdp'))
- grad_attn_qkv: float32 [896, 3072], P(('dp', 'fsdp'))
- grad_attn_out: float32 [1024, 896], P(('dp', 'fsdp'))
- grad_attn_out_bias: float32 [896], P(('dp', 'fsdp'))
- grad_rel_table: float32 [1024], P(('dp', 'fsdp'))
- grad_norm2_gain: float32 [896], P(('dp', 'fsdp'))
- grad_cca_query: float32 [896, 1024], P(('dp', 'fsdp'))
- grad_cca_kv: float32 [896, 2048], P(('dp', 'fsdp'))
- grad_cca_out: float32 [1024, 896], P(('dp', 'fsdp'))
- grad_cca_out_bias: float32 [896], P(('dp', 'fsdp'))
- grad_norm3_gain: float32 [896], P(('dp', 'fsdp'))
- grad_ffw_up: float32 [896, 3584], P(('dp', 'fsdp'))
- grad_ffw_up_bias: float32 [3584], P(('dp', 'fsdp'))
- grad_ffw_down: float32 [3584, 896], P(('dp', 'fsdp'))
- grad_ffw_down_bias: float32 [896], P(('dp', 'fsdp'))
The draws below stay inside these ranges and needn't reach their ends.
Inputs may be any that keep to these rules, and one draw needn't show every extreme that they name: Each row's lengths sum to 64 times the devices of fsdp, and every row holds one length of exactly 128. `deal`: each row is a permutation of the fsdp indices.
All inputs are finite; a program needn't handle non-finite values.
Results may differ from the reference program's by a relative error of at most 0.018.
Values may be sent and summed in bfloat16 or wider, within the bound.
A program may use at most 256 MiB of HBM per device.

```python
import math
import jax
import jax.numpy as jnp
import numpy as np
from jax import lax

D = 896
FF = 3584
HEADS = 16
HEAD_DIM = 64
CH = 64
NL = 128
K_NB = 2
NB = 64
MB = 2
TOK_DEV = 64
ATT = 1024
SLOT = 128
NC = 2
NPOOL = 3
BW = 2
TOKENS = 2048
POOL = 96
N_DP = 4
N_FSDP = 8
DEVICES = 32


def set_ends(drawn, rng, low, largest):
    spot = [jax.random.randint(jax.random.fold_in(rng, axis), (), 0, length) for axis, length in enumerate(drawn.shape)]
    longest = drawn.shape.index(max(drawn.shape))
    next_to = spot[:longest] + [(spot[longest] + 1) % drawn.shape[longest]] + spot[longest + 1:]
    return drawn.at[tuple(spot)].set(low).at[tuple(next_to)].set(largest)


def raised(entries, rng, source, target, shards_of, factor):
    owner, partner = [(jnp.arange(entries.shape[dim]) // (entries.shape[dim] // shards_of)).reshape([-1 if axis == dim else 1 for axis in range(entries.ndim)]) for dim in (source, target)]
    chosen = jax.random.permutation(rng, shards_of)[partner]
    strong = (owner == chosen) | (owner == (partner + shards_of // 2) % shards_of)
    return jnp.where(strong, factor * entries, entries)


def block_levels(key, dims, split, smallest, top_value):
    loudness, own = 1.0, jax.random.fold_in(key, 6)
    for axis_at, blocks in split:
        heights = jnp.exp(jax.random.uniform(jax.random.fold_in(own, axis_at), (blocks,), jnp.float32, smallest / len(split), top_value / len(split)))
        loudness = loudness * jnp.repeat(heights, dims[axis_at] // blocks).reshape([-1 if axis == axis_at else 1 for axis in range(len(dims))])
    return loudness


def length_profile(count, total, limit, skew):
    loads = [(1 << 20) // math.isqrt(rank ** skew) + 1 for rank in range(2, count + 1)]
    surplus, counts = total - limit - (count - 1), [1] * (count - 1)
    while surplus > 0:
        movable = [i for i in range(count - 1) if counts[i] < limit]
        whole, remaining = sum([loads[i] for i in movable]), surplus
        for i in movable:
            more = min(limit - counts[i], max(1, remaining * loads[i] // whole), surplus)
            counts[i] = counts[i] + more
            surplus = surplus - more
    return np.array([limit] + counts)


def ragged_sizes(key, number_of, total, bound, slope):
    if number_of == 2:
        one = jax.random.randint(key, (), max(1, total - bound), min(bound, total - 1) + 1)
        return jnp.stack([one, total - one])
    sizes = jnp.asarray(length_profile(number_of, total, bound, slope), jnp.int32)
    twos = (number_of - 1) // 2
    giver, taker = sizes[1:1 + 2 * twos:2], sizes[2:2 + 2 * twos:2]
    slack = jnp.minimum(giver - 1, bound - taker)
    moved = jax.random.randint(jax.random.fold_in(key, 1), (twos,), 0, 1 << 20) % (slack + 1)
    sizes = sizes.at[1:1 + 2 * twos:2].set(giver - moved).at[2:2 + 2 * twos:2].set(taker + moved)
    return sizes[jax.random.permutation(jax.random.fold_in(key, 2), number_of)]


def centred(key, extent, scale, most, shards=(), held_as=jnp.bfloat16):
    drawn = scale * jax.random.normal(key, extent, jnp.float32)
    if shards:
        drawn = drawn * block_levels(key, extent, shards, -0.22, 0.18)
    return jnp.clip(drawn, -most, most).astype(held_as)


def noise_with(stream_key, dims, scale, bound, split, heavy, kind=jnp.bfloat16):
    result = scale * jax.random.normal(stream_key, dims, jnp.float32)
    if split:
        result = result * block_levels(stream_key, dims, split, -0.22, 0.18)
    return jnp.clip(raised(result, jax.random.fold_in(stream_key, 3), *heavy), -bound, bound).astype(kind)


def setup_inputs(seed: int = 0) -> dict:
    keys = jax.random.split(jax.random.key(seed), 22)
    tokens = noise_with(keys[0], (MB, TOKENS, D), 1.0, 6.0, ((1, 32),), (1, 2, 32, 2.75))
    cotangent = centred(keys[1], (MB, TOKENS, D), 1.0, 6.0, ((1, 32),))
    lengths = jax.vmap(lambda own: ragged_sizes(own, N_FSDP, TOK_DEV * N_FSDP, SLOT, 2))(jax.random.split(keys[2], MB * N_DP)).reshape((MB, N_DP, N_FSDP)).astype(jnp.int32)
    deal = jax.vmap(lambda own: jax.random.permutation(own, N_FSDP))(jax.random.split(keys[3], MB * N_DP)).reshape((MB, N_DP, N_FSDP)).astype(jnp.int32)
    pool = centred(keys[4], (MB, POOL, NL, D), 1.0, 6.0, ((1, 32),))
    neighbour_ids = set_ends(jax.random.randint(keys[5], (MB, NC * DEVICES, K_NB), 0, NPOOL), jax.random.fold_in(keys[5], 1), 0, NPOOL - 1).astype(jnp.int32)
    norm1_gain = jnp.clip(1.0 + 0.1 * jax.random.normal(keys[6], (D,), jnp.float32), 0.5, 1.5).astype(jnp.bfloat16)
    attn_qkv = centred(keys[7], (D, 3 * ATT), D ** -0.5, 0.1875, ((0, 32),))
    attn_out = centred(keys[8], (ATT, D), (ATT // 8) ** -0.5, 0.5, ((0, 32),))
    attn_out_bias = centred(keys[9], (D,), 0.3, 3.0, ((0, 32),))
    rel_table = centred(keys[10], (NB * HEADS,), 1.0, 4.0, ((0, 32),))
    norm2_gain = jnp.clip(1.0 + 0.1 * jax.random.normal(keys[11], (D,), jnp.float32), 0.5, 1.5).astype(jnp.bfloat16)
    cca_query = centred(keys[12], (D, ATT), D ** -0.5, 0.1875, ((0, 32),))
    cca_kv = centred(keys[13], (D, 2 * ATT), D ** -0.5, 0.1875, ((0, 32),))
    cca_out = centred(keys[14], (ATT, D), (ATT // 8) ** -0.5, 0.5, ((0, 32),))
    cca_out_bias = centred(keys[15], (D,), 0.3, 3.0, ((0, 32),))
    norm3_gain = jnp.clip(1.0 + 0.1 * jax.random.normal(keys[16], (D,), jnp.float32), 0.5, 1.5).astype(jnp.bfloat16)
    ffw_up = centred(keys[17], (D, FF), D ** -0.5, 0.1875, ((0, 32),))
    ffw_up_bias = centred(keys[18], (FF,), 0.5, 3.0, ((0, 32),))
    ffw_down = centred(keys[19], (FF, D), (FF // 4) ** -0.5, 0.1875, ((0, 32),))
    ffw_down_bias = centred(keys[20], (D,), 0.3, 3.0, ((0, 32),))
    return {"tokens": tokens, "cotangent": cotangent, "lengths": lengths, "deal": deal, "pool": pool, "neighbour_ids": neighbour_ids, "norm1_gain": norm1_gain, "attn_qkv": attn_qkv, "attn_out": attn_out, "attn_out_bias": attn_out_bias, "rel_table": rel_table, "norm2_gain": norm2_gain, "cca_query": cca_query, "cca_kv": cca_kv, "cca_out": cca_out, "cca_out_bias": cca_out_bias, "norm3_gain": norm3_gain, "ffw_up": ffw_up, "ffw_up_bias": ffw_up_bias, "ffw_down": ffw_down, "ffw_down_bias": ffw_down_bias}


epsilon = 1e-06
masked_score = -1e+30

@jax.custom_vjp
def low(v):
    return lax.optimization_barrier(v.astype(jnp.bfloat16)).astype(jnp.float32)

@jax.custom_vjp
def low_back(v):
    return v

def low_keep(v):
    return (low(v), None)

def low_pass(kept, grad):
    return (grad,)

def back_keep(v):
    return (v, None)

def back_low(kept, grad):
    return (low(grad),)
low.defvjp(low_keep, low_pass)
low_back.defvjp(back_keep, back_low)

def product(left, right):
    return jnp.dot(left, right, precision=lax.Precision.HIGHEST, preferred_element_type=jnp.float32)

def rms_norm(values, gain_vec):
    return values * lax.rsqrt(lax.optimization_barrier(jnp.mean(values * values, -1, keepdims=True)) + epsilon) * gain_vec

def softmax_rows(scores):
    return jnp.exp(scores - jax.nn.logsumexp(scores, axis=-1, keepdims=True))

def block_layer(inputs, neighbours, span_ids, weights):
    norm1_gain, attn_qkv, attn_out, attn_out_bias, rel_table, norm2_gain, cca_query, cca_kv, cca_out, cca_out_bias, norm3_gain, ffw_up, ffw_up_bias, ffw_down, ffw_down_bias = weights
    length = inputs.shape[0]
    width = inputs.shape[1]
    heads = HEADS
    inner = HEADS * HEAD_DIM
    factor = HEAD_DIM ** (-0.5)
    normed = low(rms_norm(inputs, norm1_gain))
    joined = product(normed, attn_qkv)
    query_rows = low(low_back(joined[:, :inner])).reshape(length, heads, HEAD_DIM)
    key_rows = low(low_back(joined[:, inner:2 * inner])).reshape(length, heads, HEAD_DIM)
    value_rows = low(low_back(joined[:, 2 * inner:])).reshape(length, heads, HEAD_DIM)
    scores = jnp.einsum('ihd,jhd->hij', query_rows, key_rows, precision=lax.Precision.HIGHEST) * factor
    places = jnp.arange(length, dtype=jnp.int32)
    distance = places[:, None] - places[None, :]
    bucket = jnp.clip(distance, 0, length - 1) // BW
    table = rel_table.reshape(NB, heads)
    scores = low_back(scores + jnp.transpose(table[bucket], (2, 0, 1)))
    scores = jnp.where(distance[None] >= 0, scores, masked_score)
    soft_rows = low(softmax_rows(scores))
    mixed = jnp.einsum('hij,jhd->ihd', soft_rows, value_rows, precision=lax.Precision.HIGHEST).reshape(length, inner)
    mixed = low(low_back(mixed))
    hidden_one = inputs + low_back(product(mixed, attn_out) + attn_out_bias)
    normed = low(rms_norm(hidden_one, norm2_gain))
    cross_query = low(low_back(product(normed, cca_query)))
    pairs = product(neighbours.reshape(-1, width), cca_kv).reshape(neighbours.shape[0], NL, 2 * inner)
    cross_keys = low(low_back(pairs[..., :inner]))
    cross_values = low(low_back(pairs[..., inner:]))
    spans = length // CH
    key_sets = cross_keys[span_ids].reshape(spans, K_NB * NL, heads, HEAD_DIM)
    value_sets = cross_values[span_ids].reshape(spans, K_NB * NL, heads, HEAD_DIM)
    pad_rows = jnp.zeros((CH - 1, inner), jnp.float32)
    shifted = jnp.concatenate([cross_query[CH - 1:], pad_rows], 0).reshape(spans, CH, heads, HEAD_DIM)
    cross_scores = low_back(jnp.einsum('uchd,uthd->uhct', shifted, key_sets, precision=lax.Precision.HIGHEST) * factor)
    cross_soft = low(softmax_rows(cross_scores))
    gathered = jnp.einsum('uhct,uthd->uchd', cross_soft, value_sets, precision=lax.Precision.HIGHEST).reshape(length, inner)
    attended = low(low_back(jnp.concatenate([pad_rows, gathered[:length - CH + 1]], 0)))
    hidden_two = hidden_one + low_back(product(attended, cca_out) + cca_out_bias)
    normed = low(rms_norm(hidden_two, norm3_gain))
    upward = low_back(product(normed, ffw_up) + ffw_up_bias)
    activated = low(jax.nn.gelu(upward, approximate=True))
    return hidden_two + low_back(product(activated, ffw_down) + ffw_down_bias)

def reference(tokens, cotangent, lengths, deal, pool, neighbour_ids, norm1_gain, attn_qkv, attn_out, attn_out_bias, rel_table, norm2_gain, cca_query, cca_kv, cca_out, cca_out_bias, norm3_gain, ffw_up, ffw_up_bias, ffw_down, ffw_down_bias):
    weights = tuple((item.astype(jnp.float32) for item in (norm1_gain, attn_qkv, attn_out, attn_out_bias, rel_table, norm2_gain, cca_query, cca_kv, cca_out, cca_out_bias, norm3_gain, ffw_up, ffw_up_bias, ffw_down, ffw_down_bias)))
    groups = N_DP
    members = N_FSDP
    stream = members * TOK_DEV
    width = tokens.shape[2]
    starts = (jnp.cumsum(lengths, -1) - lengths).astype(jnp.int32)
    member_ids = jnp.arange(members, dtype=jnp.int32)
    match = deal[..., :, None] == member_ids[None, None, None, :]
    seq_of = lax.optimization_barrier(jnp.sum(jnp.where(match, member_ids[:, None], 0), axis=2)).astype(jnp.int32)
    seq_start = jnp.take_along_axis(starts, seq_of, axis=-1)
    seq_len = jnp.take_along_axis(lengths, seq_of, axis=-1)
    slot_pos = jnp.arange(SLOT, dtype=jnp.int32)
    live = slot_pos[None, None, None, :] < seq_len[..., None]
    base = (jnp.arange(MB * groups, dtype=jnp.int32) * stream).reshape(MB, groups, 1, 1)
    source = (jnp.clip(seq_start[..., None] + slot_pos, 0, stream - 1) + base).reshape(-1)

    def to_slots(array):
        flat = array.astype(jnp.float32).reshape(-1, width)
        picked = jnp.take(flat, source, axis=0).reshape(MB, groups, members, SLOT, width)
        return jnp.where(live[..., None], picked, 0.0).reshape(MB * groups * members, SLOT, width)
    slot_inputs = to_slots(tokens)
    slot_cot = to_slots(cotangent)
    neighbours = pool.astype(jnp.float32).reshape(MB * groups * members, NPOOL, NL, width)
    span_ids = neighbour_ids.reshape(-1, NC, K_NB).astype(jnp.int32)

    def forward(inputs_all, neighbours_all, params):

        def one_slot(item):
            return jax.checkpoint(block_layer)(item[0], item[1], item[2], params)
        return lax.map(one_slot, (inputs_all, neighbours_all, span_ids))
    outputs, pullback = jax.vjp(forward, slot_inputs, neighbours, weights)
    d_inputs, d_neighbours, d_weights = pullback(slot_cot)
    rows = jnp.arange(stream, dtype=jnp.int32)
    holder = lax.optimization_barrier(jnp.sum((starts[..., None, :] <= rows[:, None]).astype(jnp.int32), -1)) - 1
    row_start = jnp.take_along_axis(starts, holder, axis=-1)
    row_owner = jnp.take_along_axis(deal, holder, axis=-1)
    slot_base = (jnp.arange(MB * groups, dtype=jnp.int32) * members).reshape(MB, groups, 1)
    target = ((slot_base + row_owner) * SLOT + rows[None, None, :] - row_start).reshape(-1)
    activations = jnp.take(outputs.reshape(-1, width), target, axis=0).reshape(MB, -1, width).astype(jnp.bfloat16)
    input_grad = jnp.take(d_inputs.reshape(-1, width), target, axis=0).reshape(MB, -1, width).astype(jnp.bfloat16)
    pool_grad = d_neighbours.reshape(MB, -1, NL, width)
    grad_norm1_gain, grad_attn_qkv, grad_attn_out, grad_attn_out_bias, grad_rel_table, grad_norm2_gain, grad_cca_query, grad_cca_kv, grad_cca_out, grad_cca_out_bias, grad_norm3_gain, grad_ffw_up, grad_ffw_up_bias, grad_ffw_down, grad_ffw_down_bias = d_weights
    return (activations, input_grad, pool_grad, grad_norm1_gain, grad_attn_qkv, grad_attn_out, grad_attn_out_bias, grad_rel_table, grad_norm2_gain, grad_cca_query, grad_cca_kv, grad_cca_out, grad_cca_out_bias, grad_norm3_gain, grad_ffw_up, grad_ffw_up_bias, grad_ffw_down, grad_ffw_down_bias)
```

```python
from functools import partial

import jax
import jax.numpy as jnp
from jax import lax
from jax.experimental import pallas as pl
from jax.experimental.pallas import tpu as pltpu
from jax.sharding import PartitionSpec as P

MIB = 1 << 20
F32, BF = jnp.float32, jnp.bfloat16
HEADS, HEAD_DIM, CH, NL, K_NB, NB = 16, 64, 64, 128, 2, 64
epsilon = 1e-06
masked_score = -1e30
tile = 512
low_row = 48
GROUPS = 32
SMALLS = 16
G1, G2, G3, BA, BC, BD, REL, UPB = range(8)


def mm(a, b):
    return jnp.dot(a, b, preferred_element_type=F32)
def mm_tn(a, b):
    return lax.dot_general(a, b, (((0,), (0,)), ((), ())), preferred_element_type=F32)
def mm_nt(a, b):
    return lax.dot_general(a, b, (((1,), (1,)), ((), ())), preferred_element_type=F32)
def iota(shape, dim):
    return lax.broadcasted_iota(jnp.int32, shape, dim)
def onehot(cond):
    return jnp.where(cond, 1.0, 0.0).astype(BF)
def split2(v):
    hi = v.astype(BF)
    return hi, (v - hi.astype(F32)).astype(BF)
def columns(i, size):
    return pl.ds(pl.multiple_of(i * size, size), size)
def loop(count, body):
    def step(i, carry):
        body(i)
        return carry
    lax.fori_loop(0, count, step, 0)


def spread(width):
    small = width // GROUPS
    big = (small + 15) // 16 * 16
    row, col = iota((width, GROUPS * big), 0), iota((width, GROUPS * big), 1)
    return onehot((col // big == row // small) & (col % big == row % small))


def dense(v, spread_mat):
    hi, lo = split2(v)
    return mm_nt(hi, spread_mat) + mm_nt(lo, spread_mat)


def small_rows(packed, width):
    per = width // GROUPS
    put = onehot(iota((128, width), 0) == iota((128, width), 1) % per)
    placed = mm(packed, put)
    shape = (GROUPS * SMALLS, width)
    placed = jnp.where(iota(shape, 0) // SMALLS == iota(shape, 1) // per, placed, 0.0).astype(BF)
    take = onehot(iota((SMALLS, GROUPS * SMALLS), 1) % SMALLS == iota((SMALLS, GROUPS * SMALLS), 0))
    return mm(take, placed)


def table_rows(packed, length):
    per = NB * HEADS // GROUPS // HEADS
    width = length // NB
    take = onehot(iota((GROUPS, GROUPS * SMALLS), 1) == iota((GROUPS, GROUPS * SMALLS), 0) * SMALLS + REL)
    held = mm(take, packed).astype(BF)
    far = (length - iota((GROUPS, length), 1)) % length // width
    at = mm_tn(held, onehot(far // per == iota((GROUPS, length), 0)))
    which = (length - iota((HEADS, length), 1)) % length // width % per
    out = jnp.zeros((HEADS, length), F32)
    for k in range(per):
        out = jnp.where(which == k, at[k * HEADS:(k + 1) * HEADS], out)
    return out


def biases(rows, bias):
    length = bias.shape[1]
    below = iota((length, length), 0) >= iota((length, length), 1)
    for h in range(HEADS):
        wide = jnp.broadcast_to(rows[h:h + 1], (length, length))
        bias[h] = jnp.where(below, pltpu.roll(wide, 0, 1, stride=1, stride_axis=0), masked_score)


def rms(v):
    return lax.rsqrt(jnp.mean(v * v, -1, keepdims=True) + epsilon)


def norm(v, gain):
    return (v * rms(v) * gain).astype(BF)


def norm_back(v, gain, dn):
    r = rms(v)
    unit = v * r
    gained = dn * gain
    return r * (gained - unit * jnp.mean(gained * unit, -1, keepdims=True)), jnp.sum(dn * unit, 0, keepdims=True)


def halves(v):
    first = iota(v.shape, 1) < HEAD_DIM
    zero = jnp.zeros(v.shape, v.dtype)
    return jnp.concatenate([jnp.where(first, v, zero), jnp.where(first, zero, v)], 0)


def joined(v):
    n = v.shape[0] // 2
    return jnp.where(iota((n, v.shape[1]), 1) < HEAD_DIM, v[:n], v[n:])


def head_loop(count, body):
    pairs = HEADS // 2
    def step(i, carry):
        m, p = i // pairs, i % pairs
        body(m, p, p * 2 * HEAD_DIM)
        return carry
    lax.fori_loop(0, count * pairs, step, 0, unroll=2)


class Sizes:
    def __init__(self, MB, length, width, att, ff, pool):
        self.MB, self.length, self.width, self.att, self.ff, self.pool = MB, length, width, att, ff, pool
        self.rows = MB * length
        self.win = length - low_row
        self.wide = GROUPS * ((width // GROUPS + 15) // 16 * 16)
        self.keys = pool * NL


def fwd_self(z, join, bias, ps, att):
    factor = HEAD_DIM ** -0.5
    def body(m, p, c):
        rows = pl.ds(pl.multiple_of(m * z.length, 128), z.length)
        at = lambda part: pl.ds(pl.multiple_of(part * z.att + c, 128), 128)
        q, k, v = join[rows, at(0)], join[rows, at(1)], join[rows, at(2)]
        s = mm_nt(halves(q), k) * factor + jnp.concatenate([bias[2 * p], bias[2 * p + 1]], 0)
        e = jnp.exp(s - jnp.max(s, -1, keepdims=True))
        soft = e * (1.0 / jnp.sum(e, -1, keepdims=True))
        ps[m, p] = soft
        att[rows, at(0)] = joined(mm(soft.astype(BF), v)).astype(BF)
    head_loop(z.MB, body)


def fwd_cross(z, cq, ckv, times, pc, c_out):
    factor = HEAD_DIM ** -0.5
    for m in range(z.MB):
        c_out[m * z.length:m * z.length + low_row] = jnp.zeros((low_row, z.att), BF)
    def body(m, p, c):
        rows = pl.ds(pl.multiple_of(m * z.length + low_row, 16), z.win)
        keys = pl.ds(pl.multiple_of(m * z.keys, 128), z.keys)
        at = lambda part: pl.ds(pl.multiple_of(part * z.att + c, 128), 128)
        q, k, v = cq[rows, at(0)], ckv[keys, at(0)], ckv[keys, at(1)]
        cnt = times[m]
        cnt = jnp.concatenate([cnt, cnt], 0)
        s = jnp.where(cnt > 0, mm_nt(halves(q), k) * factor, masked_score)
        e = jnp.exp(s - jnp.max(s, -1, keepdims=True))
        total = jnp.sum(e * cnt, -1, keepdims=True)
        soft = e * (1.0 / jnp.where(total > 0, total, 1.0))
        pc[m, p] = soft
        c_out[rows, at(0)] = joined(mm((soft.astype(BF).astype(F32) * cnt).astype(BF), v)).astype(BF)
    head_loop(z.MB, body)


def gelu_parts(u):
    k = 0.7978845608028654
    t = jnp.tanh(k * (u + 0.044715 * u * u * u))
    half = 0.5 * (1.0 + t)
    return u * half, half + 0.5 * u * (1.0 - t * t) * k * (1.0 + 3 * 0.044715 * u * u)


def fwd_up(z, n3, up, upb, gl, slope):
    def body(i):
        at = columns(i, tile)
        u = mm(n3[...], up[:, at]) + upb[:, at]
        value, d = gelu_parts(u)
        gl[:, at] = value.astype(BF)
        slope[:, at] = d
    loop(z.ff // tile, body)


def project(left, weight, out, size=tile):
    def body(i):
        at = columns(i, size)
        out[:, at] = mm(left[...], weight[:, at]).astype(out.dtype)
    loop(out.shape[1] // size, body)


def project_nt(left, weight, out, size=tile):
    def body(i):
        at = columns(i, size)
        out[:, at] = mm_nt(left[...], weight[at, :]).astype(out.dtype)
    loop(out.shape[1] // size, body)


def outer(left, right, out, size=256):
    def body(i):
        at = columns(i, size)
        out[at, :] = mm_tn(left[:, at], right[...]).astype(out.dtype)
    loop(out.shape[0] // size, body)


def bwd_self(z, join, ps, da, dq, table_sum):
    factor = HEAD_DIM ** -0.5
    def body(m, p, c):
        rows = pl.ds(pl.multiple_of(m * z.length, 128), z.length)
        at = lambda part: pl.ds(pl.multiple_of(part * z.att + c, 128), 128)
        q, k, v = join[rows, at(0)], join[rows, at(1)], join[rows, at(2)]
        d = halves(da[rows, at(0)])
        soft = ps[m, p]
        dp = mm_nt(d, v)
        ds = (soft * (dp - jnp.sum(dp * soft, -1, keepdims=True))).astype(BF)
        dq[rows, at(0)] = (joined(mm(ds, k)) * factor).astype(BF)
        dq[rows, at(1)] = (mm_tn(ds, halves(q)) * factor).astype(BF)
        dq[rows, at(2)] = mm_tn(soft.astype(BF), d).astype(BF)
        wide = ds.astype(F32)
        for k in range(2):
            heads = pl.ds(pl.multiple_of((2 * p + k) * z.length, 128), z.length)
            table_sum[:, heads] += wide[k * z.length:(k + 1) * z.length]
    head_loop(z.MB, body)


def bwd_cross(z, cq, ckv, times, pc, dc, dcq, dckv):
    factor = HEAD_DIM ** -0.5
    for m in range(z.MB):
        dcq[m * z.length:m * z.length + low_row] = jnp.zeros((low_row, z.att), BF)
    def body(m, p, c):
        rows = pl.ds(pl.multiple_of(m * z.length + low_row, 16), z.win)
        keys = pl.ds(pl.multiple_of(m * z.keys, 128), z.keys)
        at = lambda part: pl.ds(pl.multiple_of(part * z.att + c, 128), 128)
        q, k, v = cq[rows, at(0)], ckv[keys, at(0)], ckv[keys, at(1)]
        d = halves(dc[rows, at(0)])
        cnt = times[m]
        cnt = jnp.concatenate([cnt, cnt], 0)
        soft = pc[m, p]
        dp = mm_nt(d, v)
        ds = (soft * (dp - jnp.sum(dp * soft * cnt, -1, keepdims=True))).astype(BF)
        ds = (ds.astype(F32) * cnt).astype(BF)
        pb = (soft.astype(BF).astype(F32) * cnt).astype(BF)
        dcq[rows, at(0)] = (joined(mm(ds, k)) * factor).astype(BF)
        dckv[keys, at(0)] = (mm_tn(ds, halves(q)) * factor).astype(BF)
        dckv[keys, at(1)] = mm_tn(pb, d).astype(BF)
    head_loop(z.MB, body)


def exact(a, b, dims):
    return lax.dot_general(a, b, (dims, ((), ())), precision=lax.Precision.HIGHEST, preferred_element_type=F32)


def table_grad(table_sum):
    length = table_sum.shape[0]
    flip = onehot(iota((length, length), 0) + iota((length, length), 1) == length - 1)
    hi, lo = split2(table_sum)
    flipped = mm(flip, hi) + mm(flip, lo)
    rows = []
    for h in range(HEADS):
        turned = pltpu.roll(flipped[:, h * length:(h + 1) * length], 0, 1, stride=1, stride_axis=0)
        rows.append(jnp.sum(turned, 0, keepdims=True))
    return jnp.concatenate(rows, 0)


WEIGHTS = ("qkv", "ao", "cq", "kv", "co", "up", "dn")


def forward_steps(z, ready, r):
    sp = spread(z.width)
    r.sp[...] = sp
    packed = ready("small")[...]
    r.vec[...] = small_rows(packed, z.width)
    def upb(i):
        at = columns(i, tile)
        per = z.ff // GROUPS
        put = onehot(iota((128, tile), 0) == (iota((128, tile), 1) + i * tile) % per)
        placed = mm(packed, put)
        shape = (GROUPS * SMALLS, tile)
        mine = (iota(shape, 0) // SMALLS == (iota(shape, 1) + i * tile) // per) & (iota(shape, 0) % SMALLS == UPB)
        r.upb[:, at] = jnp.sum(jnp.where(mine, placed, 0.0), 0, keepdims=True)
    loop(z.ff // tile, upb)
    biases(table_rows(packed, z.length), r.bias)
    kv = ready("kv")
    half = z.keys // 2
    def pool_part(i):
        rows = pl.ds(pl.multiple_of(i * half, 64), half)
        r.ep[rows, :] = mm(r.pool[rows, :], r.sp[...]).astype(BF)
    loop(z.MB * 2, pool_part)
    project(r.ep, kv, r.ckv, 256)
    tok = ready("tok")
    stream = tok.shape[1]
    for m in range(z.MB):
        rows = slice(m * z.length, (m + 1) * z.length)
        pick = onehot(r.wanted[rows, :1] == iota((z.length, stream), 1))
        r.x[rows] = mm(pick, tok[m])
    x = r.x[...]
    r.n1[...] = mm(norm(x, r.vec[G1:G1 + 1]), r.sp[...]).astype(BF)
    project(r.n1, ready("qkv"), r.join)
    fwd_self(z, r.join, r.bias, r.ps, r.a)
    h1 = x + (mm(r.a[...], ready("ao")[...]) + r.vec[BA:BA + 1])
    r.h1[...] = h1
    r.n2[...] = mm(norm(h1, r.vec[G2:G2 + 1]), r.sp[...]).astype(BF)
    project(r.n2, ready("cq"), r.cq)
    fwd_cross(z, r.cq, r.ckv, r.times, r.pc, r.c)
    h2 = r.h1[...] + (mm(r.c[...], ready("co")[...]) + r.vec[BC:BC + 1])
    r.h2[...] = h2
    r.n3[...] = mm(norm(h2, r.vec[G3:G3 + 1]), r.sp[...]).astype(BF)
    fwd_up(z, r.n3, ready("up"), r.upb, r.gl, r.slope)
    y = (r.h2[...] + (mm(r.gl[...], ready("dn")[...]) + r.vec[BD:BD + 1])).astype(BF)
    ct = ready("ct")
    for m in range(z.MB):
        rows = slice(m * z.length, (m + 1) * z.length)
        pick = onehot(r.wanted[rows, :1] == iota((z.length, stream), 1))
        r.back_y[m] = mm_tn(pick, y[rows]).astype(BF)
        r.ct[rows] = mm(pick, ct[m]).astype(BF)


def backward_steps(z, ready, emit, r):
    vec, sp = r.vec, r.sp
    e3 = r.ct[...]
    small = {}
    ones = lambda v: jnp.sum(v.astype(F32), 0, keepdims=True)
    small[BD] = ones(e3)
    dn = ready("dn")
    for i in range(z.ff // tile):
        at = slice(i * tile, (i + 1) * tile)
        du = (mm_nt(e3, dn[at, :]) * r.slope_tile(i)).astype(BF)
        r.du[:, at] = du
        r.upb_sum[:, at] = ones(du)
    emit("dn", lambda out: outer(r.gl, r.ct, out))
    dw, small[G3] = norm_back(r.h2[...], vec[G3:G3 + 1], dense(mm_nt(r.du[...], ready("up")[...]), sp[...]))
    emit("up", lambda out: outer(r.n3, r.du, out))
    dh = e3.astype(F32) + dw
    r.dh[...] = dh
    r.e[...] = dh.astype(BF)
    small[BC] = ones(r.e[...])
    project_nt(r.e, ready("co"), r.dc)
    emit("co", lambda out: outer(r.c, r.e, out))
    bwd_cross(z, r.cq, r.ckv, r.times, r.pc, r.dc, r.dcq, r.dckv)
    kv = ready("kv")
    part = z.keys // 2
    for i in range(z.MB * 2):
        rows = slice(i * part, (i + 1) * part)
        r.put_pool(i, dense(mm_nt(r.dckv[rows, :], kv[...]), sp[...]))
    emit("kv", lambda out: outer(r.ep, r.dckv, out))
    dw, small[G2] = norm_back(r.h1[...], vec[G2:G2 + 1], dense(mm_nt(r.dcq[...], ready("cq")[...]), sp[...]))
    emit("cq", lambda out: outer(r.n2, r.dcq, out))
    dh = r.dh[...] + dw
    r.dh[...] = dh
    r.e[...] = dh.astype(BF)
    small[BA] = ones(r.e[...])
    project_nt(r.e, ready("ao"), r.dc)
    emit("ao", lambda out: outer(r.a, r.e, out))
    r.table[...] = jnp.zeros(r.table.shape, F32)
    bwd_self(z, r.join, r.ps, r.dc, r.dq, r.table)
    dw, small[G1] = norm_back(r.x[...], vec[G1:G1 + 1], dense(mm_nt(r.dq[...], ready("qkv")[...]), sp[...]))
    dx = (r.dh[...] + dw).astype(BF)
    stream = r.back_x.shape[1]
    for m in range(z.MB):
        rows = slice(m * z.length, (m + 1) * z.length)
        pick = onehot(r.wanted[rows, :1] == iota((z.length, stream), 1))
        r.back_x[m] = mm_tn(pick, dx[rows]).astype(BF)
    pack_smalls(z, small, r)
    emit("qkv", lambda out: outer(r.n1, r.dq, out))


def pack_smalls(z, small, r):
    rows = (GROUPS * 8, z.width)
    vecs = jnp.concatenate([small.get(i, jnp.zeros((1, z.width), F32)) for i in range(8)], 0)
    spot = lambda shape, per, off=0: iota(shape, 0) // 8 == (iota(shape, 1) + off) // per
    ask = lambda cond: jnp.where(cond, 1.0, 0.0)
    per = z.width // GROUPS
    take = ask(iota((GROUPS * 8, 8), 0) % 8 == iota((GROUPS * 8, 8), 1))
    wide = exact(take, vecs, ((1,), (0,)))
    put = ask(iota((z.width, 128), 0) % per == iota((z.width, 128), 1))
    total = exact(jnp.where(spot(rows, per), wide, 0.0), put, ((1,), (0,)))
    per = z.ff // GROUPS
    for i in range(z.ff // tile):
        part = r.upb_sum[:, i * tile:(i + 1) * tile]
        shape = (GROUPS * 8, tile)
        mine = spot(shape, per, i * tile) & (iota(shape, 0) % 8 == UPB)
        put = ask((iota((tile, 128), 0) + i * tile) % per == iota((tile, 128), 1))
        total += exact(jnp.where(mine, jnp.broadcast_to(part, shape), 0.0), put, ((1,), (0,)))
    lanes = table_grad(r.table[...])
    width = z.length // NB
    per = NB // GROUPS
    far = lambda shape, dim: (z.length - 1 - iota(shape, dim)) // width
    shape = (GROUPS * 8, z.length)
    for k in range(per):
        mine = ask((iota(shape, 0) % 8 == REL) & (far(shape, 1) == iota(shape, 0) // 8 * per + k))
        by_head = exact(mine, lanes, ((1,), (1,)))
        put = ask(iota((HEADS, 128), 0) + k * HEADS == iota((HEADS, 128), 1))
        total += exact(by_head, put, ((1,), (0,)))
    r.small_grad[...] = total


class Refs:
    def __init__(self, names, refs):
        for n, ref in zip(names, refs): setattr(self, n, ref)


def weight_shapes(z):
    return {"qkv": (z.wide, 3 * z.att), "ao": (z.att, z.width), "cq": (z.wide, z.att), "kv": (z.wide, 2 * z.att),
            "co": (z.att, z.width), "up": (z.wide, z.ff), "dn": (z.ff, z.width)}


def saved_shapes(z):
    R = z.rows
    S = jax.ShapeDtypeStruct
    pairs = HEADS // 2
    return {"sp": S((z.width, z.wide), BF), "vec": S((SMALLS, z.width), F32), "ep": S((z.MB * z.keys, z.wide), BF),
            "ckv": S((z.MB * z.keys, 2 * z.att), BF), "x": S((R, z.width), F32), "n1": S((R, z.wide), BF),
            "join": S((R, 3 * z.att), BF), "ps": S((z.MB, pairs, 2 * z.length, z.length), F32), "a": S((R, z.att), BF),
            "h1": S((R, z.width), F32), "n2": S((R, z.wide), BF), "cq": S((R, z.att), BF),
            "pc": S((z.MB, pairs, 2 * z.win, z.keys), F32), "c": S((R, z.att), BF), "h2": S((R, z.width), F32),
            "n3": S((R, z.wide), BF), "gl": S((R, z.ff), BF), "slope": S((R, z.ff), F32), "ct": S((R, z.width), BF)}


def forward_plain(z, gathered, wanted, times, pool):
    names = list(gathered)
    saved = saved_shapes(z)
    outs = {**saved, "back_y": jax.ShapeDtypeStruct(gathered["tok"].shape, BF)}
    share = {"up": "qkv", "ct": "tok"}
    room = {k: gathered[k].shape for k in names if k not in share}
    room["qkv"] = gathered["up"].shape
    def kernel(*refs):
        n = len(names)
        held = dict(zip(names, refs[:n]))
        r = Refs(["wanted", "times", "pool"], refs[n:n + 3])
        r.__dict__.update(zip(outs, refs[n + 3:n + 3 + len(outs)]))
        scratch = refs[n + 3 + len(outs):]
        sems, r.bias, r.upb = scratch[:3]
        bufs = dict(zip(room, scratch[3:]))
        def view(k):
            return bufs["qkv"].at[:, :gathered[k].shape[1]] if k in ("qkv", "up") else bufs[share.get(k, k)]
        def copy(k):
            return pltpu.make_async_copy(held[k], view(k), sems.at[names.index(k)])
        for k in room:
            copy(k).start()
        def ready(k):
            if k in share:
                copy(k).start()
            copy(k).wait()
            return view(k)
        forward_steps(z, ready, r)
    V = pl.BlockSpec(memory_space=pltpu.VMEM)
    A = pl.BlockSpec(memory_space=pl.ANY)
    return dict(zip(outs, pl.pallas_call(kernel, name="layer_forward", out_shape=list(outs.values()),
        in_specs=[A] * len(names) + [V] * 3, out_specs=[V] * len(outs),
        scratch_shapes=[pltpu.SemaphoreType.DMA((len(names),)), pltpu.VMEM((HEADS, z.length, z.length), F32), pltpu.VMEM((1, z.ff), F32)]
            + [pltpu.VMEM(v, BF) for v in room.values()],
        compiler_params=pltpu.CompilerParams(vmem_limit_bytes=63 * MIB))(*gathered.values(), wanted, times, pool)))


def backward_plain(z, weights, saved, wanted, times):
    names = list(WEIGHTS)
    shapes = weight_shapes(z)
    ins = list(saved)
    S = jax.ShapeDtypeStruct
    outs = {"pool_grad": S((z.MB * z.keys, z.width), F32), "back_x": S((z.MB, z.stream, z.width), BF), "small_grad": S((GROUPS * 8, 128), F32)}
    part = z.keys // 2
    local = {"du": ((z.rows, z.ff), BF), "upb_sum": ((1, z.ff), F32), "dh": ((z.rows, z.width), F32), "e": ((z.rows, z.width), BF),
             "dc": ((z.rows, z.att), BF), "dcq": ((z.rows, z.att), BF), "dckv": ((z.MB * z.keys, 2 * z.att), BF),
             "table": ((z.length, HEADS * z.length), F32), "tiles": ((2, z.rows, tile), F32), "pool_tiles": ((2, part, z.width), F32)}
    kept = [k for k in names if k != "qkv"]

    def kernel(*refs):
        refs = list(refs)
        take = lambda k: [refs.pop(0) for _ in range(k)]
        held = dict(zip(names, take(len(names))))
        r = Refs(ins + ["wanted", "times"], take(len(ins) + 2))
        grads = dict(zip(names, take(len(names))))
        r.__dict__.update(zip(outs, take(len(outs))))
        sems, gsem, tsem, psem = take(4)
        bufs = dict(zip(kept, take(len(kept))))
        bufs["qkv"] = bufs["up"].at[:, :shapes["qkv"][1]]
        r.__dict__.update(zip(local, take(len(local))))
        r.dq = r.du.at[:, :3 * z.att]
        load = lambda k: pltpu.make_async_copy(held[k], bufs[k], sems.at[names.index(k)])
        store = lambda k: pltpu.make_async_copy(bufs[k], grads[k], gsem.at[names.index(k)])
        slope = lambda i: pltpu.make_async_copy(r.slope.at[:, i * tile:(i + 1) * tile], r.tiles.at[i % 2], tsem.at[i % 2])
        slope(0).start()
        for k in ("dn", "up", "co", "kv", "cq", "ao"):
            load(k).start()
        def slope_tile(i):
            if i + 1 < z.ff // tile:
                slope(i + 1).start()
            slope(i).wait()
            return r.tiles[i % 2]
        pool_copy = lambda i: pltpu.make_async_copy(r.pool_tiles.at[i % 2], r.pool_grad.at[i * part:(i + 1) * part], psem.at[i % 2])
        def put_pool(i, value):
            if i >= 2:
                pool_copy(i - 2).wait()
            r.pool_tiles[i % 2] = value
            pool_copy(i).start()
        r.slope_tile, r.put_pool = slope_tile, put_pool
        def ready(k):
            load(k).wait()
            return bufs[k]
        def emit(k, write):
            write(bufs[k])
            store(k).start()
            if k == "co":
                store("up").wait()
                load("qkv").start()
        backward_steps(z, ready, emit, r)
        for k in names:
            if k != "up":
                store(k).wait()
        for i in (z.MB * 2 - 2, z.MB * 2 - 1):
            pool_copy(i).wait()
    V = pl.BlockSpec(memory_space=pltpu.VMEM)
    A = pl.BlockSpec(memory_space=pl.ANY)
    D = pltpu.SemaphoreType.DMA
    res = pl.pallas_call(kernel, name="layer_backward", out_shape=[S(shapes[k], BF) for k in names] + list(outs.values()),
        in_specs=[A] * len(names) + [A if k == "slope" else V for k in ins] + [V] * 2, out_specs=[A] * (len(names) + 1) + [V] * 2,
        scratch_shapes=[D((len(names),)), D((len(names),)), D((2,)), D((2,))] + [pltpu.VMEM(shapes[k], BF) for k in kept]
            + [pltpu.VMEM(*v) for v in local.values()],
        compiler_params=pltpu.CompilerParams(vmem_limit_bytes=63 * MIB))(*[weights[k] for k in names], *saved.values(), wanted, times)
    return dict(zip(names, res)), dict(zip(outs, res[len(names):]))


MESH = pl.DeviceIdType.MESH

def when(pred, fn):
    if pred is None: fn()
    else: pl.when(pred)(fn)

def both(a, b):
    if a is None: return b
    if b is None: return a
    return jnp.logical_and(a, b)

class Place:
    def __init__(self, nz):
        dp, fs = lax.axis_index("dp"), lax.axis_index("fsdp")
        self.nz = nz
        self.y, self.x = dp // 2, lax.rem(dp, 2)
        self.z, self.c = fs // 2, lax.rem(fs, 2)
        y, x, z, c = self.y, self.x, self.z, self.c
        self.y1, self.x1 = y + c * (1 - 2 * y), x + (1 - c) * (1 - 2 * x)
        self.y2, self.x2 = y + (1 - c) * (1 - 2 * y), x + c * (1 - 2 * x)
        self.yo, self.xo = 1 - y, 1 - x
        self.first = {"dp": self.y1 * 2 + self.x1, "fsdp": fs}
        self.second = {"dp": self.y2 * 2 + self.x2, "fsdp": fs}
        self.pair = {"dp": dp, "fsdp": z * 2 + 1 - c}
        self.up = {"dp": dp, "fsdp": fs + 2}
        self.down = {"dp": dp, "fsdp": fs - 2}
        self.has_up, self.has_down = z < nz - 1, z > 0

    def barrier(self):
        bar = pltpu.get_barrier_semaphore()
        ways = [(None, self.pair), (None, self.first), (None, self.second), (self.has_up, self.up), (self.has_down, self.down)]
        for pred, dev in ways:
            when(pred, lambda dev=dev: pl.semaphore_signal(bar, inc=1, device_id=dev, device_id_type=MESH))
        pl.semaphore_wait(bar, 3 + jnp.minimum(self.z, 1) + jnp.minimum(self.nz - 1 - self.z, 1))

class Gather:
    def __init__(self, at, block, out, sems, line_only=False):
        self.at, self.block, self.out, self.line_only = at, block, out, line_only
        self.zs, self.zr, self.ps, self.pr, self.own = sems
        self.late = []

    def cell(self, z, c):
        p = self.at
        return self.out.at[:, z, c] if self.line_only else self.out.at[p.y, p.x, z, c]
    def line(self, y, x, c):
        return self.out.at[:, :, c] if self.line_only else self.out.at[y, x, :, c]
    def copy(self, src, dst, s, r, dev):
        return pltpu.make_async_remote_copy(src_ref=src, dst_ref=dst, send_sem=s, recv_sem=r, device_id=dev, device_id_type=MESH)
    def send(self, pred, src, dst, s, r, dev):
        def go():
            self.copy(src, dst, s, r, dev).start()
        when(pred, go)
        def done():
            self.copy(src, dst, s, r, dev).wait_send()
        self.late.append((pred, done))
    def arrived(self, pred, ref, s, r):
        when(pred, lambda: self.copy(ref, ref, s, r, self.at.pair).wait_recv())

    def start(self):
        p = self.at
        mine = self.cell(p.z, p.c)
        pltpu.make_async_copy(self.block, mine, self.own).start()
        self.send(p.has_up, self.block, mine, self.zs.at[0, 0], self.zr.at[0, 0], p.up)
        self.send(p.has_down, self.block, mine, self.zs.at[1, 0], self.zr.at[1, 0], p.down)
    def along_z(self):
        p = self.at
        for j in range(1, p.nz):
            below, above = p.z >= j, p.z < p.nz - j
            ref = self.cell(p.z - j, p.c)
            self.arrived(below, ref, self.zs.at[0, j - 1], self.zr.at[0, j - 1])
            if j < p.nz - 1:
                self.send(both(below, p.has_up), ref, ref, self.zs.at[0, j], self.zr.at[0, j], p.up)
            ref = self.cell(p.z + j, p.c)
            self.arrived(above, ref, self.zs.at[1, j - 1], self.zr.at[1, j - 1])
            if j < p.nz - 1:
                self.send(both(above, p.has_down), ref, ref, self.zs.at[1, j], self.zr.at[1, j], p.down)
        pltpu.make_async_copy(self.block, self.cell(p.z, p.c), self.own).wait()
        mine = self.line(p.y, p.x, p.c)
        self.send(None, mine, mine, self.ps.at[0], self.pr.at[0], p.pair)
        if not self.line_only:
            self.send(None, mine, mine, self.ps.at[4], self.pr.at[4], p.first)
            self.send(None, mine, mine, self.ps.at[5], self.pr.at[5], p.second)
    def after_first(self):
        p = self.at
        if self.line_only: return
        got = self.line(p.y1, p.x1, p.c)
        self.arrived(None, got, self.ps.at[4], self.pr.at[4])
        self.send(None, got, got, self.ps.at[6], self.pr.at[6], p.second)
        self.send(None, got, got, self.ps.at[1], self.pr.at[1], p.pair)
    def after_second(self):
        p = self.at
        if self.line_only: return
        for k, (y, x) in enumerate(((p.y2, p.x2), (p.yo, p.xo))):
            got = self.line(y, x, p.c)
            self.arrived(None, got, self.ps.at[5 + k], self.pr.at[5 + k])
            self.send(None, got, got, self.ps.at[2 + k], self.pr.at[2 + k], p.pair)
    def whole(self):
        p = self.at
        lines = [(p.y, p.x)] if self.line_only else [(p.y, p.x), (p.y2, p.x2), (p.y1, p.x1), (p.yo, p.xo)]
        for k, (y, x) in enumerate(lines):
            self.arrived(None, self.line(y, x, 1 - p.c), self.ps.at[k], self.pr.at[k])
    def drain(self):
        for pred, done in self.late:
            when(pred, done)

def sem_shapes(n, nz):
    D = pltpu.SemaphoreType.DMA
    return [D((n, 2, nz)), D((n, 2, nz)), D((n, 8)), D((n, 8)), D((n,))]


def pad16(r):
    return (r + 15) // 16 * 16


SENDS = (("small", 1), ("kv", 2), ("tok", 1), ("qkv", 3), ("ao", 1), ("cq", 1), ("co", 1), ("up", 4), ("dn", 2), ("ct", 1))
lines_only = ("tok", "ct")


def piece(ref, name, c, cut):
    if cut == 1:
        return ref
    lead = (slice(None),) * (len(ref.shape) - 2)
    if name == "dn":
        tiles = ref.shape[-2] // 16
        return ref.at[lead + (slice(tiles * c // cut * 16, tiles * (c + 1) // cut * 16),)]
    cols = ref.shape[-1] // cut
    return ref.at[lead + (slice(None), slice(c * cols, (c + 1) * cols))]


def gather_kernel(n, nz, pieces, ahead, *refs):
    blocks, outs, stage = refs[:n], refs[n:2 * n], refs[2 * n:3 * n]
    zs, zr, ps, pr, own = refs[3 * n:]
    at = Place(nz)
    for b, s in zip(blocks, stage):
        if s.shape == b.shape:
            s[...] = b[...]
        else:
            s[...] = jnp.zeros(s.shape, s.dtype)
            s[:b.shape[0], :] = b[...]
    at.barrier()
    gs = []
    for i, (k, cut) in enumerate(pieces):
        for c in range(cut):
            part = lambda ref: piece(ref, k, c, cut)
            j = len(gs)
            gs.append(Gather(at, part(stage[i]), part(outs[i]), [s.at[j] for s in (zs, zr, ps, pr, own)], k in lines_only))
    for g in gs[:ahead]:
        g.start()
    for t in range(len(gs) + 2):
        if t + ahead < len(gs):
            gs[t + ahead].start()
        if t < len(gs):
            gs[t].along_z()
        if 1 <= t <= len(gs):
            gs[t - 1].after_first()
        if 2 <= t:
            gs[t - 2].after_second()
    for g in gs:
        g.whole()
    for g in gs:
        g.drain()


def gather_named(arrays, z, nz):
    pieces = SENDS
    names = [k for k, _ in pieces]
    n, total = len(names), sum(cut for _, cut in pieces)
    blocks = [arrays[k] for k in names]
    outs, stages = [], []
    for k, b in zip(names, blocks):
        if k in lines_only:
            outs.append(jax.ShapeDtypeStruct((b.shape[0], nz, 2) + b.shape[1:], b.dtype))
            stages.append(pltpu.VMEM(b.shape, b.dtype))
        else:
            r = pad16(b.shape[0])
            outs.append(jax.ShapeDtypeStruct((2, 2, nz, 2, r, b.shape[1]), b.dtype))
            stages.append(pltpu.VMEM((r, b.shape[1]), b.dtype))
    got = pl.pallas_call(partial(gather_kernel, n, nz, pieces, 2), name="gather_weights", out_shape=outs,
        in_specs=[pl.BlockSpec(memory_space=pltpu.VMEM)] * n, out_specs=[pl.BlockSpec(memory_space=pl.ANY)] * n,
        scratch_shapes=stages + sem_shapes(total, nz),
        compiler_params=pltpu.CompilerParams(collective_id=1, has_side_effects=True, vmem_limit_bytes=40 * MIB))(*blocks)
    flat = lambda k, v: v.reshape(v.shape[0], -1, v.shape[-1]) if k in lines_only else v.reshape(-1, v.shape[-1])
    return {k: flat(k, v) for k, v in zip(names, got)}


def scatter_named(lines, small, grads, shards, z, nz):
    S = jax.ShapeDtypeStruct
    tok = z.length // 2
    as_line = lambda v: v.reshape(z.MB, nz, 2, tok, z.width)
    as_blocks = lambda v: v.reshape(2, 2, nz, 2, v.shape[0] // GROUPS, v.shape[1])
    order = ["dn", "up", "co", "kv", "cq", "ao", "qkv"]
    srcs = [as_line(lines["y"])] + [as_blocks(grads[k]) for k in order] + [as_blocks(small), as_line(lines["x"])]
    line = [True] + [False] * 8 + [True]
    outs = [S((z.MB, tok, z.width), BF)] + [S(shards[k].shape, F32) for k in order] + [S((8, 128), F32), S((z.MB, tok, z.width), BF)]
    got = scatter_all(srcs, line, outs, nz)
    return got[0], got[-1], got[-2], dict(zip(order, got[1:-2]))


class Scatter:
    def __init__(self, at, src, out, bufs, sems, line_only=False):
        self.at, self.src, self.out, self.line_only = at, src, out, line_only
        if line_only: self.acc, self.rc, self.ru, self.rd = bufs
        else: self.acc, self.rc, self.r2, self.r1, self.ru, self.rd = bufs
        self.ps, self.pr, self.us, self.ur, self.ds, self.dr, self.own = sems
        self.late = []
    def copy(self, src, dst, s, r, dev):
        return pltpu.make_async_remote_copy(src_ref=src, dst_ref=dst, send_sem=s, recv_sem=r, device_id=dev, device_id_type=MESH)
    def send(self, pred, src, dst, s, r, dev):
        when(pred, lambda: self.copy(src, dst, s, r, dev).start())
        self.late.append((pred, lambda: self.copy(src, dst, s, r, dev).wait_send()))
    def arrived(self, ref, s, r):
        self.copy(ref, ref, s, r, self.at.pair).wait_recv()
    def add(self, mine, theirs):
        lead = mine.shape[:-2]
        count = 1
        for n in lead: count *= n
        def step(i, carry):
            at, rest = [], i
            for n in reversed(lead):
                at.append(lax.rem(rest, n)); rest = rest // n
            at = tuple(reversed(at))
            mine[at] = (mine[at].astype(F32) + theirs[at].astype(F32)).astype(mine.dtype)
            return carry
        lax.fori_loop(0, count, step, 0)
    def part(self, c):
        return self.src.at[:, :, c] if self.line_only else self.src.at[:, :, :, c]
    def start(self):
        p = self.at
        pltpu.make_async_copy(self.part(p.c), self.acc, self.own).start()
        self.send(None, self.part(1 - p.c), self.rc, self.ps.at[0], self.pr.at[0], p.pair)
    def after_pair(self):
        p = self.at
        pltpu.make_async_copy(self.part(p.c), self.acc, self.own).wait()
        self.arrived(self.rc, self.ps.at[0], self.pr.at[0])
        if self.line_only:
            self.add(self.acc, self.rc)
            return
        for k, (y, x) in enumerate(((p.y2, p.x2), (p.yo, p.xo))):
            self.add(self.acc.at[y, x], self.rc.at[y, x])
            self.send(None, self.acc.at[y, x], self.r2.at[k], self.ps.at[1 + k], self.pr.at[1 + k], p.second)
        for y, x in ((p.y1, p.x1), (p.y, p.x)):
            self.add(self.acc.at[y, x], self.rc.at[y, x])
    def after_second(self):
        p = self.at
        if self.line_only: return
        self.arrived(self.r2.at[1], self.ps.at[2], self.pr.at[2])
        self.add(self.acc.at[p.y1, p.x1], self.r2.at[1])
        self.send(None, self.acc.at[p.y1, p.x1], self.r1, self.ps.at[3], self.pr.at[3], p.first)
        self.arrived(self.r2.at[0], self.ps.at[1], self.pr.at[1])
        self.add(self.acc.at[p.y, p.x], self.r2.at[0])
    def after_first(self):
        p = self.at
        if self.line_only: return
        self.arrived(self.r1, self.ps.at[3], self.pr.at[3])
        self.add(self.acc.at[p.y, p.x], self.r1)
    def cell(self, z):
        return self.acc.at[:, z] if self.line_only else self.acc.at[self.at.y, self.at.x, z]
    def z_step(self, h):
        p, nz = self.at, self.at.nz
        for j in range(nz - h, 0, -1):
            here = p.z == h - 1
            if h > 1:
                def up():
                    self.arrived(self.ru.at[j], self.us.at[j + 1], self.ur.at[j])
                    self.add(self.cell(h - 1 + j), self.ru.at[j])
                when(here, up)
            self.send(here, self.cell(h - 1 + j), self.ru.at[j - 1], self.us.at[j], self.ur.at[j - 1], p.up)
            here = p.z == nz - h
            if h > 1:
                def down():
                    self.arrived(self.rd.at[j], self.ds.at[j + 1], self.dr.at[j])
                    self.add(self.cell(nz - h - j), self.rd.at[j])
                when(here, down)
            self.send(here, self.cell(nz - h - j), self.rd.at[j - 1], self.ds.at[j], self.dr.at[j - 1], p.down)
    def finish(self):
        p = self.at
        mine = self.cell(p.z)
        def up():
            self.arrived(self.ru.at[0], self.us.at[1], self.ur.at[0])
            self.add(mine, self.ru.at[0])
        when(p.has_down, up)
        def down():
            self.arrived(self.rd.at[0], self.ds.at[1], self.dr.at[0])
            self.add(mine, self.rd.at[0])
        when(p.has_up, down)
        if self.line_only: self.out[...] = mine[...].astype(self.out.dtype)
        else: self.out[...] = mine[...][:self.out.shape[0]].astype(self.out.dtype)
    def drain(self):
        for pred, done in self.late: when(pred, done)

def rs_bufs(src, line_only, nz):
    V = pltpu.VMEM
    if line_only:
        m, _, _, r, n = src.shape
        return [V((m, nz, r, n), src.dtype), V((m, nz, r, n), src.dtype), V((nz - 1, m, r, n), src.dtype), V((nz - 1, m, r, n), src.dtype)]
    r, n = src.shape[-2:]
    b = (r, n)
    return [V((2, 2, nz) + b, src.dtype), V((2, 2, nz) + b, src.dtype), V((2, nz) + b, src.dtype), V((nz,) + b, src.dtype), V((nz - 1,) + b, src.dtype), V((nz - 1,) + b, src.dtype)]

def scatter_kernel(n, nz, line_only, ahead, *refs):
    refs = list(refs)
    take = lambda k: [refs.pop(0) for _ in range(k)]
    srcs, outs = take(n), take(n)
    bufs = [take(4 if lo else 6) for lo in line_only]
    sems = take(7)
    at = Place(nz)
    at.barrier()
    ss = [Scatter(at, srcs[i], outs[i], bufs[i], [s.at[i] for s in sems], line_only[i]) for i in range(n)]
    for s in ss[:ahead]: s.start()
    for t in range(n + nz + 2):
        def stage(k): return ss[t - k] if 0 <= t - k < n else None
        if t + ahead < n: ss[t + ahead].start()
        if stage(0): stage(0).after_pair()
        if stage(1): stage(1).after_second()
        if stage(2):
            stage(2).after_first(); stage(2).z_step(1)
        for h in range(2, nz):
            if stage(h + 1): stage(h + 1).z_step(h)
        if stage(nz + 1): stage(nz + 1).finish()
    for s in ss: s.drain()

def scatter_all(srcs, line_only, outs, nz, ahead=2, name="scatter_grads", cid=2):
    n = len(srcs)
    D = pltpu.SemaphoreType.DMA
    scratch = [b for s, lo in zip(srcs, line_only) for b in rs_bufs(s, lo, nz)]
    return pl.pallas_call(partial(scatter_kernel, n, nz, line_only, ahead), name=name, out_shape=outs,
        in_specs=[pl.BlockSpec(memory_space=pl.ANY)] * n, out_specs=[pl.BlockSpec(memory_space=pltpu.VMEM)] * n,
        scratch_shapes=scratch + [D((n, 4)), D((n, 4)), D((n, nz + 1)), D((n, nz + 1)), D((n, nz + 1)), D((n, nz + 1)), D((n,))],
        compiler_params=pltpu.CompilerParams(collective_id=cid, has_side_effects=True, vmem_limit_bytes=63 * MIB))(*srcs)


def vectors(norm1_gain, norm2_gain, norm3_gain, attn_out_bias, cca_out_bias, ffw_down_bias, rel_table, ffw_up_bias):
    return [norm1_gain, norm2_gain, norm3_gain, attn_out_bias, cca_out_bias, ffw_down_bias, rel_table, ffw_up_bias]


def to_groups(v):
    small = v.shape[0] // GROUPS
    big = (small + 15) // 16 * 16
    return jnp.pad(v.reshape(GROUPS, small, -1), ((0, 0), (0, big - small), (0, 0))).reshape(GROUPS * big, -1)


def from_groups(v, rows):
    return v.reshape(GROUPS, v.shape[0] // GROUPS, -1)[:, :rows // GROUPS].reshape(rows, -1)


def body(tokens, cotangent, lengths, deal, pool, neighbour_ids, norm1_gain, attn_qkv, attn_out, attn_out_bias, rel_table,
         norm2_gain, cca_query, cca_kv, cca_out, cca_out_bias, norm3_gain, ffw_up, ffw_up_bias, ffw_down, ffw_down_bias):
    members, member = lax.axis_size("fsdp"), lax.axis_index("fsdp")
    devices = members * lax.axis_size("dp")
    MB, tok_rows, width = tokens.shape
    length = 2 * tok_rows
    z = Sizes(MB, length, width, HEADS * HEAD_DIM, ffw_up.shape[1], pool.shape[1])
    z.stream = members * tok_rows
    shards = {"qkv": attn_qkv, "ao": attn_out, "cq": cca_query, "kv": cca_kv, "co": cca_out, "up": ffw_up, "dn": ffw_down}
    vecs = vectors(norm1_gain, norm2_gain, norm3_gain, attn_out_bias, cca_out_bias, ffw_down_bias, rel_table, ffw_up_bias)

    ids = jnp.arange(members, dtype=jnp.int32)
    lens, dealt = lengths[:, 0], deal[:, 0]
    starts = jnp.sum(jnp.where(ids[None, :, None] > ids[None, None, :], lens[:, None, :], 0), 2)
    mine = dealt == member
    own_start = jnp.sum(jnp.where(mine, starts, 0), 1)
    own_len = jnp.sum(jnp.where(mine, lens, 0), 1)
    place = jnp.arange(length, dtype=jnp.int32)
    wanted = jnp.where(place[None] < own_len[:, None], own_start[:, None] + place[None], -1).reshape(-1)
    wanted = jnp.broadcast_to(wanted[:, None], (MB * length, 128))
    spans = length // CH
    ids3 = neighbour_ids.reshape(MB, spans, K_NB)
    held = jnp.sum((ids3[..., None] == jnp.arange(z.pool, dtype=jnp.int32)).astype(F32), 2)
    row = jnp.arange(low_row, length, dtype=jnp.int32)
    in_span = ((row[:, None] - (CH - 1)) // CH == jnp.arange(spans, dtype=jnp.int32)) & (row[:, None] >= CH - 1)
    times = jnp.sum(jnp.where(in_span[None, :, :, None], held[:, None], 0.0), 2)
    times = jnp.broadcast_to(times[..., None], times.shape + (NL,)).reshape(MB, z.win, z.keys)
    neighbours = pool.reshape(MB * z.keys, width)

    direct = lax.axis_size("dp") == 4 and members % 2 == 0 and devices == GROUPS
    nz = members // 2
    if direct:
        packed = jnp.concatenate([jnp.pad(v[None], ((0, 0), (0, 128 - v.shape[0]))) for v in vecs] + [jnp.zeros((SMALLS - 8, 128), BF)], 0)
        gathered = gather_named({"small": packed, "tok": tokens, "ct": cotangent, **shards}, z, nz)
    else:
        whole = lambda v: lax.all_gather(v, ("dp", "fsdp"), axis=0, tiled=True)
        rows = [jnp.pad(w, ((0, 0), (0, 128 - w.shape[1])))[:, None] for w in [whole(v).reshape(GROUPS, -1) for v in vecs]]
        packed = jnp.concatenate(rows + [jnp.zeros((GROUPS, SMALLS - 8, 128), BF)], 1).reshape(GROUPS * SMALLS, 128)
        gathered = {"small": packed, **{k: to_groups(whole(v)) for k, v in shards.items()},
                    "tok": lax.all_gather(tokens, "fsdp", axis=1, tiled=True), "ct": lax.all_gather(cotangent, "fsdp", axis=1, tiled=True)}
    saved = forward_plain(z, gathered, wanted, times, neighbours)
    back_y = saved.pop("back_y")
    grads, outs = backward_plain(z, {k: gathered[k] for k in WEIGHTS}, saved, wanted, times)
    back_x, small = outs["back_x"], outs["small_grad"]
    if direct:
        lines = {"y": back_y, "x": back_x}
        act, dx, small, mine = scatter_named(lines, small, grads, shards, z, nz)
        parts = [small[i, :v.shape[0]] for i, v in enumerate(vecs)]
    else:
        down = lambda v: lax.psum_scatter(v.astype(F32), ("dp", "fsdp"), scatter_dimension=0, tiled=True)
        line = lambda v: lax.psum_scatter(v, "fsdp", scatter_dimension=1, tiled=True)
        act, dx = line(back_y), line(back_x)
        mine = {k: down(from_groups(grads[k], shards[k].shape[0] * devices)) for k in shards}
        small = small.reshape(GROUPS, 8, 128)
        parts = [down(small[:, i, :v.shape[0] * devices // GROUPS].reshape(-1)) for i, v in enumerate(vecs)]
    g1, g2, g3, ba, bc, bd, rel, upb = parts
    return (act, dx, outs["pool_grad"].reshape(pool.shape), g1, mine["qkv"], mine["ao"], ba, rel, g2, mine["cq"], mine["kv"],
            mine["co"], bc, g3, mine["up"], upb, mine["dn"], bd)


def solution(mesh):
    everywhere = ("dp", "fsdp")
    rows, vec = P(everywhere, None), P(everywhere)
    slots = P(None, everywhere, None)
    return jax.shard_map(
        body,
        mesh=mesh,
        in_specs=(slots, slots, P(None, "dp", None), P(None, "dp", None), P(None, everywhere, None, None), slots,
                  vec, rows, rows, vec, vec, vec, rows, rows, rows, vec, vec, rows, vec, rows, vec),
        out_specs=(slots, slots, P(None, everywhere, None, None), vec, rows, rows, vec, vec, vec, rows, rows, rows, vec, vec,
                   rows, vec, rows, vec),
        check_vma=False,
    )
```

```python
from functools import partial

import jax
import jax.numpy as jnp
from jax import lax
from jax.experimental import pallas as pl
from jax.experimental.pallas import tpu as pltpu
from jax.sharding import PartitionSpec as P

MIB = 1 << 20
F32, BF = jnp.float32, jnp.bfloat16
HEADS, HEAD_DIM, CH, NL, K_NB, NB = 16, 64, 64, 128, 2, 64
epsilon = 1e-06
masked_score = -1e30
tile = 512
low_row = 48
GROUPS = 32
SMALLS = 16
G1, G2, G3, BA, BC, BD, REL, UPB = range(8)


def mm(a, b):
    return jnp.dot(a, b, preferred_element_type=F32)
def mm_tn(a, b):
    return lax.dot_general(a, b, (((0,), (0,)), ((), ())), preferred_element_type=F32)
def mm_nt(a, b):
    return lax.dot_general(a, b, (((1,), (1,)), ((), ())), preferred_element_type=F32)
def iota(shape, dim):
    return lax.broadcasted_iota(jnp.int32, shape, dim)
def onehot(cond):
    return jnp.where(cond, 1.0, 0.0).astype(BF)
def split2(v):
    hi = v.astype(BF)
    return hi, (v - hi.astype(F32)).astype(BF)
def columns(i, size):
    return pl.ds(pl.multiple_of(i * size, size), size)
def loop(count, body):
    def step(i, carry):
        body(i)
        return carry
    lax.fori_loop(0, count, step, 0)


def spread(width):
    small = width // GROUPS
    big = (small + 15) // 16 * 16
    row, col = iota((width, GROUPS * big), 0), iota((width, GROUPS * big), 1)
    return onehot((col // big == row // small) & (col % big == row % small))


def dense(v, spread_mat):
    hi, lo = split2(v)
    return mm_nt(hi, spread_mat) + mm_nt(lo, spread_mat)


def small_rows(packed, width):
    per = width // GROUPS
    put = onehot(iota((128, width), 0) == iota((128, width), 1) % per)
    placed = mm(packed, put)
    shape = (GROUPS * SMALLS, width)
    placed = jnp.where(iota(shape, 0) // SMALLS == iota(shape, 1) // per, placed, 0.0).astype(BF)
    take = onehot(iota((SMALLS, GROUPS * SMALLS), 1) % SMALLS == iota((SMALLS, GROUPS * SMALLS), 0))
    return mm(take, placed)


def table_rows(packed, length):
    per = NB * HEADS // GROUPS // HEADS
    width = length // NB
    take = onehot(iota((GROUPS, GROUPS * SMALLS), 1) == iota((GROUPS, GROUPS * SMALLS), 0) * SMALLS + REL)
    held = mm(take, packed).astype(BF)
    far = (length - iota((GROUPS, length), 1)) % length // width
    at = mm_tn(held, onehot(far // per == iota((GROUPS, length), 0)))
    which = (length - iota((HEADS, length), 1)) % length // width % per
    out = jnp.zeros((HEADS, length), F32)
    for k in range(per):
        out = jnp.where(which == k, at[k * HEADS:(k + 1) * HEADS], out)
    return out


def biases(rows, bias):
    length = bias.shape[1]
    below = iota((length, length), 0) >= iota((length, length), 1)
    for h in range(HEADS):
        wide = jnp.broadcast_to(rows[h:h + 1], (length, length))
        bias[h] = jnp.where(below, pltpu.roll(wide, 0, 1, stride=1, stride_axis=0), masked_score)


def rms(v):
    return lax.rsqrt(jnp.mean(v * v, -1, keepdims=True) + epsilon)


def norm(v, gain):
    return (v * rms(v) * gain).astype(BF)


def norm_back(v, gain, dn):
    r = rms(v)
    unit = v * r
    gained = dn * gain
    return r * (gained - unit * jnp.mean(gained * unit, -1, keepdims=True)), jnp.sum(dn * unit, 0, keepdims=True)


def halves(v):
    first = iota(v.shape, 1) < HEAD_DIM
    zero = jnp.zeros(v.shape, v.dtype)
    return jnp.concatenate([jnp.where(first, v, zero), jnp.where(first, zero, v)], 0)


def joined(v):
    n = v.shape[0] // 2
    return jnp.where(iota((n, v.shape[1]), 1) < HEAD_DIM, v[:n], v[n:])


def head_parts(count, parts, body):
    pairs = HEADS // 2
    total = count * pairs
    def step(i, carry):
        m, p = i // pairs, i % pairs
        body(m, p, p * 2 * HEAD_DIM)
        return carry
    for k in range(parts):
        lax.fori_loop(total * k // parts, total * (k + 1) // parts, step, 0, unroll=2)
        yield


class Sizes:
    def __init__(self, MB, length, width, att, ff, pool):
        self.MB, self.length, self.width, self.att, self.ff, self.pool = MB, length, width, att, ff, pool
        self.rows = MB * length
        self.win = length - low_row
        self.wide = GROUPS * ((width // GROUPS + 15) // 16 * 16)
        self.keys = pool * NL


def fwd_self(z, join, bias, ps, att):
    factor = HEAD_DIM ** -0.5
    def body(m, p, c):
        rows = pl.ds(pl.multiple_of(m * z.length, 128), z.length)
        at = lambda part: pl.ds(pl.multiple_of(part * z.att + c, 128), 128)
        q, k, v = join[rows, at(0)], join[rows, at(1)], join[rows, at(2)]
        s = mm_nt(halves(q), k) * factor + jnp.concatenate([bias[2 * p], bias[2 * p + 1]], 0)
        e = jnp.exp(s - jnp.max(s, -1, keepdims=True))
        soft = e * (1.0 / jnp.sum(e, -1, keepdims=True))
        ps[m, p] = soft
        att[rows, at(0)] = joined(mm(soft.astype(BF), v)).astype(BF)
    yield from head_parts(z.MB, 4, body)


def fwd_cross(z, cq, ckv, times, pc, c_out):
    factor = HEAD_DIM ** -0.5
    for m in range(z.MB):
        c_out[m * z.length:m * z.length + low_row] = jnp.zeros((low_row, z.att), BF)
    def body(m, p, c):
        rows = pl.ds(pl.multiple_of(m * z.length + low_row, 16), z.win)
        keys = pl.ds(pl.multiple_of(m * z.keys, 128), z.keys)
        at = lambda part: pl.ds(pl.multiple_of(part * z.att + c, 128), 128)
        q, k, v = cq[rows, at(0)], ckv[keys, at(0)], ckv[keys, at(1)]
        cnt = times[m]
        cnt = jnp.concatenate([cnt, cnt], 0)
        s = jnp.where(cnt > 0, mm_nt(halves(q), k) * factor, masked_score)
        e = jnp.exp(s - jnp.max(s, -1, keepdims=True))
        total = jnp.sum(e * cnt, -1, keepdims=True)
        soft = e * (1.0 / jnp.where(total > 0, total, 1.0))
        pc[m, p] = soft
        c_out[rows, at(0)] = joined(mm((soft.astype(BF).astype(F32) * cnt).astype(BF), v)).astype(BF)
    yield from head_parts(z.MB, 4, body)


def gelu_parts(u):
    k = 0.7978845608028654
    t = jnp.tanh(k * (u + 0.044715 * u * u * u))
    half = 0.5 * (1.0 + t)
    return u * half, half + 0.5 * u * (1.0 - t * t) * k * (1.0 + 3 * 0.044715 * u * u)


def fwd_up(z, n3, up, upb, gl, slope, at):
    u = mm(n3[...], up[:, at]) + upb[:, at]
    value, d = gelu_parts(u)
    gl[:, at] = value.astype(BF)
    slope[:, at] = d


def project(left, weight, out, size=tile):
    for i in range(out.shape[1] // size):
        at = slice(i * size, (i + 1) * size)
        out[:, at] = mm(left[...], weight[:, at]).astype(out.dtype)
        yield


def project_nt(left, weight, out, size=tile):
    for i in range(out.shape[1] // size):
        at = slice(i * size, (i + 1) * size)
        out[:, at] = mm_nt(left[...], weight[at, :]).astype(out.dtype)
        yield


def outer(left, right, out, size=256):
    for i in range(out.shape[0] // size):
        at = slice(i * size, (i + 1) * size)
        out[at, :] = mm_tn(left[:, at], right[...]).astype(out.dtype)
        yield


def bwd_self(z, join, ps, da, dq, table_sum):
    factor = HEAD_DIM ** -0.5
    def body(m, p, c):
        rows = pl.ds(pl.multiple_of(m * z.length, 128), z.length)
        at = lambda part: pl.ds(pl.multiple_of(part * z.att + c, 128), 128)
        q, k, v = join[rows, at(0)], join[rows, at(1)], join[rows, at(2)]
        d = halves(da[rows, at(0)])
        soft = ps[m, p]
        dp = mm_nt(d, v)
        ds = (soft * (dp - jnp.sum(dp * soft, -1, keepdims=True))).astype(BF)
        dq[rows, at(0)] = (joined(mm(ds, k)) * factor).astype(BF)
        dq[rows, at(1)] = (mm_tn(ds, halves(q)) * factor).astype(BF)
        dq[rows, at(2)] = mm_tn(soft.astype(BF), d).astype(BF)
        wide = ds.astype(F32)
        for k in range(2):
            heads = pl.ds(pl.multiple_of((2 * p + k) * z.length, 128), z.length)
            table_sum[:, heads] += wide[k * z.length:(k + 1) * z.length]
    yield from head_parts(z.MB, 4, body)


def bwd_cross(z, cq, ckv, times, pc, dc, dcq, dckv):
    factor = HEAD_DIM ** -0.5
    for m in range(z.MB):
        dcq[m * z.length:m * z.length + low_row] = jnp.zeros((low_row, z.att), BF)
    def body(m, p, c):
        rows = pl.ds(pl.multiple_of(m * z.length + low_row, 16), z.win)
        keys = pl.ds(pl.multiple_of(m * z.keys, 128), z.keys)
        at = lambda part: pl.ds(pl.multiple_of(part * z.att + c, 128), 128)
        q, k, v = cq[rows, at(0)], ckv[keys, at(0)], ckv[keys, at(1)]
        d = halves(dc[rows, at(0)])
        cnt = times[m]
        cnt = jnp.concatenate([cnt, cnt], 0)
        soft = pc[m, p]
        dp = mm_nt(d, v)
        ds = (soft * (dp - jnp.sum(dp * soft * cnt, -1, keepdims=True))).astype(BF)
        ds = (ds.astype(F32) * cnt).astype(BF)
        pb = (soft.astype(BF).astype(F32) * cnt).astype(BF)
        dcq[rows, at(0)] = (joined(mm(ds, k)) * factor).astype(BF)
        dckv[keys, at(0)] = (mm_tn(ds, halves(q)) * factor).astype(BF)
        dckv[keys, at(1)] = mm_tn(pb, d).astype(BF)
    yield from head_parts(z.MB, 4, body)


def exact(a, b, dims):
    return lax.dot_general(a, b, (dims, ((), ())), precision=lax.Precision.HIGHEST, preferred_element_type=F32)


def table_grad(table_sum):
    length = table_sum.shape[0]
    flip = onehot(iota((length, length), 0) + iota((length, length), 1) == length - 1)
    hi, lo = split2(table_sum)
    flipped = mm(flip, hi) + mm(flip, lo)
    rows = []
    for h in range(HEADS):
        turned = pltpu.roll(flipped[:, h * length:(h + 1) * length], 0, 1, stride=1, stride_axis=0)
        rows.append(jnp.sum(turned, 0, keepdims=True))
    return jnp.concatenate(rows, 0)


WEIGHTS = ("qkv", "ao", "cq", "kv", "co", "up", "dn")


def forward_steps(z, ready, r):
    yield "small"
    r.sp[...] = spread(z.width)
    r.save("sp")
    packed = ready("small")[...]
    r.vec[...] = small_rows(packed, z.width)
    r.save("vec")
    yield
    def upb(i):
        at = columns(i, tile)
        per = z.ff // GROUPS
        put = onehot(iota((128, tile), 0) == (iota((128, tile), 1) + i * tile) % per)
        placed = mm(packed, put)
        shape = (GROUPS * SMALLS, tile)
        mine = (iota(shape, 0) // SMALLS == (iota(shape, 1) + i * tile) // per) & (iota(shape, 0) % SMALLS == UPB)
        r.upb[:, at] = jnp.sum(jnp.where(mine, placed, 0.0), 0, keepdims=True)
    loop(z.ff // tile, upb)
    biases(table_rows(packed, z.length), r.bias)
    half = z.keys // 2
    for i in range(z.MB * 2):
        rows = slice(i * half, (i + 1) * half)
        r.ep[rows, :] = mm(r.pool[rows, :], r.sp[...]).astype(BF)
        yield
    r.save("ep")
    yield "kv"
    kv = ready("kv")
    yield from project(r.ep, kv, r.ckv, 256)
    r.save("ckv")
    yield "tok"
    tok = ready("tok")
    stream = tok.shape[1]
    for m in range(z.MB):
        rows = slice(m * z.length, (m + 1) * z.length)
        pick = onehot(r.wanted[rows, :1] == iota((z.length, stream), 1))
        r.x[rows] = mm(pick, tok[m])
    r.save("x")
    yield
    r.n1[...] = mm(norm(r.x[...], r.vec[G1:G1 + 1]), r.sp[...]).astype(BF)
    r.save("n1")
    yield "qkv"
    yield from project(r.n1, ready("qkv"), r.join)
    r.save("join")
    yield from fwd_self(z, r.join, r.bias, r.ps, r.a)
    r.save("ps")
    r.save("a")
    yield "ao"
    h1 = r.x[...] + (mm(r.a[...], ready("ao")[...]) + r.vec[BA:BA + 1])
    r.h1[...] = h1
    r.save("h1")
    r.n2[...] = mm(norm(h1, r.vec[G2:G2 + 1]), r.sp[...]).astype(BF)
    r.save("n2")
    yield "cq"
    yield from project(r.n2, ready("cq"), r.cq)
    r.save("cq")
    yield from fwd_cross(z, r.cq, r.ckv, r.times, r.pc, r.c)
    r.save("pc")
    r.save("c")
    yield "co"
    h2 = r.h1[...] + (mm(r.c[...], ready("co")[...]) + r.vec[BC:BC + 1])
    r.h2[...] = h2
    r.save("h2")
    r.n3[...] = mm(norm(h2, r.vec[G3:G3 + 1]), r.sp[...]).astype(BF)
    r.save("n3")
    yield "ct"
    ct = ready("ct")
    for m in range(z.MB):
        rows = slice(m * z.length, (m + 1) * z.length)
        pick = onehot(r.wanted[rows, :1] == iota((z.length, stream), 1))
        r.ct[rows] = mm(pick, ct[m]).astype(BF)
    r.save("ct")
    step = z.ff // 4
    for i in range(4):
        yield "up" + str(i)
        cut = (step // 2 + 127) // 128 * 128
        for lo, hi in ((0, cut), (cut, step)):
            fwd_up(z, r.n3, ready("up"), r.upb, r.gl, r.slope, slice(i * step + lo, i * step + hi))
            yield
    r.save("gl")
    r.save("slope")
    yield "dn"
    dn = ready("dn")
    out = mm(r.gl[...], dn[...])
    y = (r.h2[...] + (out + r.vec[BD:BD + 1])).astype(BF)
    for m in range(z.MB):
        rows = slice(m * z.length, (m + 1) * z.length)
        pick = onehot(r.wanted[rows, :1] == iota((z.length, stream), 1))
        r.back_y[m] = mm_tn(pick, y[rows]).astype(BF)
    r.save("back_y")


def backward_steps(z, ready, r):
    vec, sp = r.vec, r.sp
    small = {}
    ones = lambda v: jnp.sum(v.astype(F32), 0, keepdims=True)
    yield "saved", ("ct",)
    yield "weight", "dn"
    dn = ready("dn")
    small[BD] = ones(r.ct[...])
    for i in range(z.ff // tile):
        at = slice(i * tile, (i + 1) * tile)
        du = (mm_nt(r.ct[...], dn[at, :]) * r.slope_tile(i)).astype(BF)
        r.du[:, at] = du
        r.upb_sum[:, at] = ones(du)
        yield
    yield "saved", ("gl",)
    yield from outer(r.gl, r.ct, ready("dn"))
    yield "grad", "dn"
    yield "saved", ("sp", "vec", "h2", "n3")
    yield "weight", "up"
    dn3 = dense(mm_nt(r.du[...], ready("up")[...]), sp[...])
    dw, small[G3] = norm_back(r.h2[...], vec[G3:G3 + 1], dn3)
    dh = r.ct[...].astype(F32) + dw
    r.dh[...] = dh
    r.e[...] = dh.astype(BF)
    small[BC] = ones(dh.astype(BF))
    yield
    yield from outer(r.n3, r.du, ready("up"))
    yield "grad", "up"
    yield "weight", "co"
    yield from project_nt(r.e, ready("co"), r.dc)
    yield "saved", ("c",)
    yield from outer(r.c, r.e, ready("co"))
    yield "grad", "co"
    yield "saved", ("cq", "ckv", "pc")
    yield from bwd_cross(z, r.cq, r.ckv, r.times, r.pc, r.dc, r.dcq, r.dckv)
    yield "weight", "kv"
    kv = ready("kv")
    part = z.keys // 2
    for i in range(z.MB * 2):
        rows = slice(i * part, (i + 1) * part)
        r.put_pool(i, dense(mm_nt(r.dckv[rows, :], kv[...]), sp[...]))
        yield
    yield "saved", ("ep",)
    yield from outer(r.ep, r.dckv, kv)
    yield "grad", "kv"
    yield "weight", "cq"
    yield "saved", ("h1", "n2")
    dn2 = dense(mm_nt(r.dcq[...], ready("cq")[...]), sp[...])
    dw, small[G2] = norm_back(r.h1[...], vec[G2:G2 + 1], dn2)
    yield
    yield from outer(r.n2, r.dcq, ready("cq"))
    yield "grad", "cq"
    dh = r.dh[...] + dw
    r.dh[...] = dh
    r.e[...] = dh.astype(BF)
    small[BA] = ones(dh.astype(BF))
    yield "weight", "ao"
    yield from project_nt(r.e, ready("ao"), r.dc)
    yield "saved", ("a",)
    yield from outer(r.a, r.e, ready("ao"))
    yield "grad", "ao"
    yield "saved", ("join", "ps")
    r.table[...] = jnp.zeros(r.table.shape, F32)
    yield from bwd_self(z, r.join, r.ps, r.dc, r.dq, r.table)
    yield "weight", "qkv"
    yield "saved", ("x", "n1")
    dn1 = dense(mm_nt(r.dq[...], ready("qkv")[...]), sp[...])
    dw, small[G1] = norm_back(r.x[...], vec[G1:G1 + 1], dn1)
    dx = (r.dh[...] + dw).astype(BF)
    stream = r.back_x.shape[1]
    for m in range(z.MB):
        rows = slice(m * z.length, (m + 1) * z.length)
        pick = onehot(r.wanted[rows, :1] == iota((z.length, stream), 1))
        r.back_x[m] = mm_tn(pick, dx[rows]).astype(BF)
    yield "grad", "x"
    yield from outer(r.n1, r.dq, ready("qkv"))
    yield "grad", "qkv"
    pack_smalls(z, small, r)
    yield "grad", "small"


def pack_smalls(z, small, r):
    rows = (GROUPS * 8, z.width)
    vecs = jnp.concatenate([small.get(i, jnp.zeros((1, z.width), F32)) for i in range(8)], 0)
    spot = lambda shape, per, off=0: iota(shape, 0) // 8 == (iota(shape, 1) + off) // per
    ask = lambda cond: jnp.where(cond, 1.0, 0.0)
    per = z.width // GROUPS
    take = ask(iota((GROUPS * 8, 8), 0) % 8 == iota((GROUPS * 8, 8), 1))
    wide = exact(take, vecs, ((1,), (0,)))
    put = ask(iota((z.width, 128), 0) % per == iota((z.width, 128), 1))
    total = exact(jnp.where(spot(rows, per), wide, 0.0), put, ((1,), (0,)))
    per = z.ff // GROUPS
    for i in range(z.ff // tile):
        part = r.upb_sum[:, i * tile:(i + 1) * tile]
        shape = (GROUPS * 8, tile)
        mine = spot(shape, per, i * tile) & (iota(shape, 0) % 8 == UPB)
        put = ask((iota((tile, 128), 0) + i * tile) % per == iota((tile, 128), 1))
        total += exact(jnp.where(mine, jnp.broadcast_to(part, shape), 0.0), put, ((1,), (0,)))
    lanes = table_grad(r.table[...])
    width = z.length // NB
    per = NB // GROUPS
    far = lambda shape, dim: (z.length - 1 - iota(shape, dim)) // width
    shape = (GROUPS * 8, z.length)
    for k in range(per):
        mine = ask((iota(shape, 0) % 8 == REL) & (far(shape, 1) == iota(shape, 0) // 8 * per + k))
        by_head = exact(mine, lanes, ((1,), (1,)))
        put = ask(iota((HEADS, 128), 0) + k * HEADS == iota((HEADS, 128), 1))
        total += exact(by_head, put, ((1,), (0,)))
    r.small_grad[...] = total


class Refs:
    def __init__(self, names, refs):
        for n, ref in zip(names, refs): setattr(self, n, ref)


def weight_shapes(z):
    return {"qkv": (z.wide, 3 * z.att), "ao": (z.att, z.width), "cq": (z.wide, z.att), "kv": (z.wide, 2 * z.att),
            "co": (z.att, z.width), "up": (z.wide, z.ff), "dn": (z.ff, z.width)}


def saved_shapes(z):
    R = z.rows
    S = jax.ShapeDtypeStruct
    pairs = HEADS // 2
    return {"sp": S((z.width, z.wide), BF), "vec": S((SMALLS, z.width), F32), "ep": S((z.MB * z.keys, z.wide), BF),
            "ckv": S((z.MB * z.keys, 2 * z.att), BF), "x": S((R, z.width), F32), "n1": S((R, z.wide), BF),
            "join": S((R, 3 * z.att), BF), "ps": S((z.MB, pairs, 2 * z.length, z.length), F32), "a": S((R, z.att), BF),
            "h1": S((R, z.width), F32), "n2": S((R, z.wide), BF), "cq": S((R, z.att), BF),
            "pc": S((z.MB, pairs, 2 * z.win, z.keys), F32), "c": S((R, z.att), BF), "h2": S((R, z.width), F32),
            "n3": S((R, z.wide), BF), "gl": S((R, z.ff), BF), "slope": S((R, z.ff), F32), "ct": S((R, z.width), BF)}


def forward_plain(z, gathered, wanted, times, pool):
    names = list(gathered)
    saved = saved_shapes(z)
    outs = {**saved, "back_y": jax.ShapeDtypeStruct(gathered["tok"].shape, BF)}
    share = {"up": "qkv", "ct": "tok"}
    room = {k: gathered[k].shape for k in names if k not in share}
    room["qkv"] = gathered["up"].shape
    def kernel(*refs):
        n = len(names)
        held = dict(zip(names, refs[:n]))
        r = Refs(["wanted", "times", "pool"], refs[n:n + 3])
        r.__dict__.update(zip(outs, refs[n + 3:n + 3 + len(outs)]))
        scratch = refs[n + 3 + len(outs):]
        sems, r.bias, r.upb = scratch[:3]
        bufs = dict(zip(room, scratch[3:]))
        def view(k):
            return bufs["qkv"].at[:, :gathered[k].shape[1]] if k in ("qkv", "up") else bufs[share.get(k, k)]
        def copy(k):
            return pltpu.make_async_copy(held[k], view(k), sems.at[names.index(k)])
        for k in room:
            copy(k).start()
        r.save = lambda k: None
        for k in forward_steps(z, view, r):
            if k in ("up0", "ct"):
                copy(k.rstrip("0")).start()
            if k == "up0" or k in names:
                copy(k.rstrip("0")).wait()
    V = pl.BlockSpec(memory_space=pltpu.VMEM)
    A = pl.BlockSpec(memory_space=pl.ANY)
    return dict(zip(outs, pl.pallas_call(kernel, name="layer_forward", out_shape=list(outs.values()),
        in_specs=[A] * len(names) + [V] * 3, out_specs=[V] * len(outs),
        scratch_shapes=[pltpu.SemaphoreType.DMA((len(names),)), pltpu.VMEM((HEADS, z.length, z.length), F32), pltpu.VMEM((1, z.ff), F32)]
            + [pltpu.VMEM(v, BF) for v in room.values()],
        compiler_params=pltpu.CompilerParams(vmem_limit_bytes=63 * MIB))(*gathered.values(), wanted, times, pool)))


def backward_plain(z, weights, saved, wanted, times):
    names = list(WEIGHTS)
    shapes = weight_shapes(z)
    ins = list(saved)
    S = jax.ShapeDtypeStruct
    outs = {"pool_grad": S((z.MB * z.keys, z.width), F32), "back_x": S((z.MB, z.stream, z.width), BF), "small_grad": S((GROUPS * 8, 128), F32)}
    part = z.keys // 2
    local = {"du": ((z.rows, z.ff), BF), "upb_sum": ((1, z.ff), F32), "dh": ((z.rows, z.width), F32), "e": ((z.rows, z.width), BF),
             "dc": ((z.rows, z.att), BF), "dcq": ((z.rows, z.att), BF), "dckv": ((z.MB * z.keys, 2 * z.att), BF),
             "table": ((z.length, HEADS * z.length), F32), "tiles": ((2, z.rows, tile), F32), "pool_tiles": ((2, part, z.width), F32)}
    kept = [k for k in names if k != "qkv"]

    def kernel(*refs):
        refs = list(refs)
        take = lambda k: [refs.pop(0) for _ in range(k)]
        held = dict(zip(names, take(len(names))))
        r = Refs(ins + ["wanted", "times"], take(len(ins) + 2))
        grads = dict(zip(names, take(len(names))))
        r.__dict__.update(zip(outs, take(len(outs))))
        sems, gsem, tsem, psem = take(4)
        bufs = dict(zip(kept, take(len(kept))))
        bufs["qkv"] = bufs["up"].at[:, :shapes["qkv"][1]]
        r.__dict__.update(zip(local, take(len(local))))
        r.dq = r.du.at[:, :3 * z.att]
        load = lambda k: pltpu.make_async_copy(held[k], bufs[k], sems.at[names.index(k)])
        store = lambda k: pltpu.make_async_copy(bufs[k], grads[k], gsem.at[names.index(k)])
        slope = lambda i: pltpu.make_async_copy(r.slope.at[:, i * tile:(i + 1) * tile], r.tiles.at[i % 2], tsem.at[i % 2])
        slope(0).start()
        for k in ("dn", "up", "co", "kv", "cq", "ao"):
            load(k).start()
        def slope_tile(i):
            if i + 1 < z.ff // tile:
                slope(i + 1).start()
            slope(i).wait()
            return r.tiles[i % 2]
        pool_copy = lambda i: pltpu.make_async_copy(r.pool_tiles.at[i % 2], r.pool_grad.at[i * part:(i + 1) * part], psem.at[i % 2])
        def put_pool(i, value):
            if i >= 2:
                pool_copy(i - 2).wait()
            r.pool_tiles[i % 2] = value
            pool_copy(i).start()
        r.slope_tile, r.put_pool = slope_tile, put_pool
        for event in backward_steps(z, lambda k: bufs[k], r):
            kind, k = event or (None, None)
            if kind == "weight":
                load(k).wait()
            if kind == "grad" and k in names:
                store(k).start()
                if k == "co":
                    store("up").wait()
                    load("qkv").start()
        for k in names:
            if k != "up":
                store(k).wait()
        for i in (z.MB * 2 - 2, z.MB * 2 - 1):
            pool_copy(i).wait()
    V = pl.BlockSpec(memory_space=pltpu.VMEM)
    A = pl.BlockSpec(memory_space=pl.ANY)
    D = pltpu.SemaphoreType.DMA
    res = pl.pallas_call(kernel, name="layer_backward", out_shape=[S(shapes[k], BF) for k in names] + list(outs.values()),
        in_specs=[A] * len(names) + [A if k == "slope" else V for k in ins] + [V] * 2, out_specs=[A] * (len(names) + 1) + [V] * 2,
        scratch_shapes=[D((len(names),)), D((len(names),)), D((2,)), D((2,))] + [pltpu.VMEM(shapes[k], BF) for k in kept]
            + [pltpu.VMEM(*v) for v in local.values()],
        compiler_params=pltpu.CompilerParams(vmem_limit_bytes=63 * MIB))(*[weights[k] for k in names], *saved.values(), wanted, times)
    return dict(zip(names, res)), dict(zip(outs, res[len(names):]))


MESH = pl.DeviceIdType.MESH

def when(pred, fn):
    if pred is None: fn()
    else: pl.when(pred)(fn)

def both(a, b):
    if a is None: return b
    if b is None: return a
    return jnp.logical_and(a, b)

class Place:
    def __init__(self, nz):
        dp, fs = lax.axis_index("dp"), lax.axis_index("fsdp")
        self.nz = nz
        self.y, self.x = dp // 2, lax.rem(dp, 2)
        self.z, self.c = fs // 2, lax.rem(fs, 2)
        y, x, z, c = self.y, self.x, self.z, self.c
        self.y1, self.x1 = y + c * (1 - 2 * y), x + (1 - c) * (1 - 2 * x)
        self.y2, self.x2 = y + (1 - c) * (1 - 2 * y), x + c * (1 - 2 * x)
        self.yo, self.xo = 1 - y, 1 - x
        self.first = {"dp": self.y1 * 2 + self.x1, "fsdp": fs}
        self.second = {"dp": self.y2 * 2 + self.x2, "fsdp": fs}
        self.pair = {"dp": dp, "fsdp": z * 2 + 1 - c}
        self.up = {"dp": dp, "fsdp": fs + 2}
        self.down = {"dp": dp, "fsdp": fs - 2}
        self.has_up, self.has_down = z < nz - 1, z > 0

    def barrier(self):
        bar = pltpu.get_barrier_semaphore()
        ways = [(None, self.pair), (None, self.first), (None, self.second), (self.has_up, self.up), (self.has_down, self.down)]
        for pred, dev in ways:
            when(pred, lambda dev=dev: pl.semaphore_signal(bar, inc=1, device_id=dev, device_id_type=MESH))
        pl.semaphore_wait(bar, 3 + jnp.minimum(self.z, 1) + jnp.minimum(self.nz - 1 - self.z, 1))

class Gather:
    def __init__(self, at, block, out, sems, line_only=False):
        self.at, self.block, self.out, self.line_only = at, block, out, line_only
        self.zs, self.zr, self.ps, self.pr, self.own = sems
        self.late = []

    def cell(self, z, c):
        p = self.at
        return self.out.at[:, z, c] if self.line_only else self.out.at[p.y, p.x, z, c]
    def line(self, y, x, c):
        return self.out.at[:, :, c] if self.line_only else self.out.at[y, x, :, c]
    def copy(self, src, dst, s, r, dev):
        return pltpu.make_async_remote_copy(src_ref=src, dst_ref=dst, send_sem=s, recv_sem=r, device_id=dev, device_id_type=MESH)
    def send(self, pred, src, dst, s, r, dev):
        def go():
            self.copy(src, dst, s, r, dev).start()
        when(pred, go)
        def done():
            self.copy(src, dst, s, r, dev).wait_send()
        self.late.append((pred, done))
    def arrived(self, pred, ref, s, r):
        when(pred, lambda: self.copy(ref, ref, s, r, self.at.pair).wait_recv())

    def across(self, pred, ref, block=None):
        p = self.at
        src = ref if block is None else block
        if not self.line_only:
            for k, dev in ((4, p.first), (5, p.second)):
                when(pred, lambda k=k, dev=dev: self.copy(src, ref, self.ps.at[k], self.pr.at[k], dev).start())
    def start(self):
        p = self.at
        mine = self.cell(p.z, p.c)
        self.send(p.has_up, self.block, mine, self.zs.at[0, 0], self.zr.at[0, 0], p.up)
        self.send(p.has_down, self.block, mine, self.zs.at[1, 0], self.zr.at[1, 0], p.down)
        self.across(None, mine, self.block)
        pltpu.make_async_copy(self.block, mine, self.own).start()
    def hop(self, j):
        p = self.at
        for way, pred, more, ref, dev in ((0, p.z >= j, p.has_up, self.cell(p.z - j, p.c), p.up),
                                          (1, p.z < p.nz - j, p.has_down, self.cell(p.z + j, p.c), p.down)):
            self.arrived(pred, ref, self.zs.at[way, j - 1], self.zr.at[way, j - 1])
            if j < p.nz - 1:
                self.send(both(pred, more), ref, ref, self.zs.at[way, j], self.zr.at[way, j], dev)
            self.across(pred, ref)
    def z_done(self):
        p = self.at
        pltpu.make_async_copy(self.block, self.cell(p.z, p.c), self.own).wait()
        mine = self.line(p.y, p.x, p.c)
        self.send(None, mine, mine, self.ps.at[0], self.pr.at[0], p.pair)
        if not self.line_only:
            for k in (4, 5):
                self.late.append((None, lambda k=k: self.copy(mine, mine, self.ps.at[k], self.pr.at[k], p.pair).wait_send()))
    def after_first(self):
        p = self.at
        if self.line_only: return
        got = self.line(p.y1, p.x1, p.c)
        self.arrived(None, got, self.ps.at[4], self.pr.at[4])
        self.send(None, got, got, self.ps.at[6], self.pr.at[6], p.second)
        self.send(None, got, got, self.ps.at[1], self.pr.at[1], p.pair)
    def after_second(self):
        p = self.at
        if self.line_only: return
        for k, (y, x) in enumerate(((p.y2, p.x2), (p.yo, p.xo))):
            got = self.line(y, x, p.c)
            self.arrived(None, got, self.ps.at[5 + k], self.pr.at[5 + k])
            self.send(None, got, got, self.ps.at[2 + k], self.pr.at[2 + k], p.pair)
    def whole(self):
        p = self.at
        lines = [(p.y, p.x)] if self.line_only else [(p.y, p.x), (p.y2, p.x2), (p.y1, p.x1), (p.yo, p.xo)]
        for k, (y, x) in enumerate(lines):
            self.arrived(None, self.line(y, x, 1 - p.c), self.ps.at[k], self.pr.at[k])
    def drain(self):
        for pred, done in self.late:
            when(pred, done)

def sem_shapes(n, nz):
    D = pltpu.SemaphoreType.DMA
    return [D((n, 2, nz)), D((n, 2, nz)), D((n, 8)), D((n, 8)), D((n,))]


class Scatter:
    def __init__(self, at, src, out, bufs, sems, line_only=False):
        self.at, self.src, self.out, self.line_only = at, src, out, line_only
        if line_only: self.acc, self.rc, self.ru, self.rd = bufs
        else: self.acc, self.rc, self.r2, self.r1, self.ru, self.rd = bufs
        self.ps, self.pr, self.us, self.ur, self.ds, self.dr, self.own = sems
        self.late = []
    def copy(self, src, dst, s, r, dev):
        return pltpu.make_async_remote_copy(src_ref=src, dst_ref=dst, send_sem=s, recv_sem=r, device_id=dev, device_id_type=MESH)
    def send(self, pred, src, dst, s, r, dev):
        when(pred, lambda: self.copy(src, dst, s, r, dev).start())
        self.late.append((pred, lambda: self.copy(src, dst, s, r, dev).wait_send()))
    def arrived(self, ref, s, r):
        self.copy(ref, ref, s, r, self.at.pair).wait_recv()
    def add(self, mine, theirs):
        lead = mine.shape[:-2]
        count = 1
        for n in lead: count *= n
        def step(i, carry):
            at, rest = [], i
            for n in reversed(lead):
                at.append(lax.rem(rest, n)); rest = rest // n
            at = tuple(reversed(at))
            mine[at] = (mine[at].astype(F32) + theirs[at].astype(F32)).astype(mine.dtype)
            return carry
        lax.fori_loop(0, count, step, 0)
    def part(self, c):
        return self.src.at[:, :, c] if self.line_only else self.src.at[:, :, :, c]
    def start(self):
        p = self.at
        pltpu.make_async_copy(self.part(p.c), self.acc, self.own).start()
        self.send(None, self.part(1 - p.c), self.rc, self.ps.at[0], self.pr.at[0], p.pair)
    def after_pair(self):
        p = self.at
        pltpu.make_async_copy(self.part(p.c), self.acc, self.own).wait()
        self.arrived(self.rc, self.ps.at[0], self.pr.at[0])
        if self.line_only:
            self.add(self.acc, self.rc)
            return
        for k, (y, x) in enumerate(((p.y2, p.x2), (p.yo, p.xo))):
            self.add(self.acc.at[y, x], self.rc.at[y, x])
            self.send(None, self.acc.at[y, x], self.r2.at[k], self.ps.at[1 + k], self.pr.at[1 + k], p.second)
        for y, x in ((p.y1, p.x1), (p.y, p.x)):
            self.add(self.acc.at[y, x], self.rc.at[y, x])
    def after_second(self):
        p = self.at
        if self.line_only: return
        self.arrived(self.r2.at[1], self.ps.at[2], self.pr.at[2])
        self.add(self.acc.at[p.y1, p.x1], self.r2.at[1])
        self.send(None, self.acc.at[p.y1, p.x1], self.r1, self.ps.at[3], self.pr.at[3], p.first)
        self.arrived(self.r2.at[0], self.ps.at[1], self.pr.at[1])
        self.add(self.acc.at[p.y, p.x], self.r2.at[0])
    def after_first(self):
        p = self.at
        if self.line_only: return
        self.arrived(self.r1, self.ps.at[3], self.pr.at[3])
        self.add(self.acc.at[p.y, p.x], self.r1)
    def cell(self, z):
        return self.acc.at[:, z] if self.line_only else self.acc.at[self.at.y, self.at.x, z]
    def z_step(self, h):
        p, nz = self.at, self.at.nz
        for j in range(nz - h, 0, -1):
            here = p.z == h - 1
            if h > 1:
                def up():
                    self.arrived(self.ru.at[j], self.us.at[j + 1], self.ur.at[j])
                    self.add(self.cell(h - 1 + j), self.ru.at[j])
                when(here, up)
            self.send(here, self.cell(h - 1 + j), self.ru.at[j - 1], self.us.at[j], self.ur.at[j - 1], p.up)
            here = p.z == nz - h
            if h > 1:
                def down():
                    self.arrived(self.rd.at[j], self.ds.at[j + 1], self.dr.at[j])
                    self.add(self.cell(nz - h - j), self.rd.at[j])
                when(here, down)
            self.send(here, self.cell(nz - h - j), self.rd.at[j - 1], self.ds.at[j], self.dr.at[j - 1], p.down)
    def finish(self):
        p = self.at
        mine = self.cell(p.z)
        def up():
            self.arrived(self.ru.at[0], self.us.at[1], self.ur.at[0])
            self.add(mine, self.ru.at[0])
        when(p.has_down, up)
        def down():
            self.arrived(self.rd.at[0], self.ds.at[1], self.dr.at[0])
            self.add(mine, self.rd.at[0])
        when(p.has_up, down)
        if self.line_only: self.out[...] = mine[...].astype(self.out.dtype)
        else: self.out[...] = mine[...][:self.out.shape[0]].astype(self.out.dtype)
    def drain(self):
        for pred, done in self.late: when(pred, done)

def rs_bufs(src, line_only, nz):
    V = pltpu.VMEM
    if line_only:
        m, _, _, r, n = src.shape
        return [V((m, nz, r, n), src.dtype), V((m, nz, r, n), src.dtype), V((nz - 1, m, r, n), src.dtype), V((nz - 1, m, r, n), src.dtype)]
    r, n = src.shape[-2:]
    b = (r, n)
    return [V((2, 2, nz) + b, src.dtype), V((2, 2, nz) + b, src.dtype), V((2, nz) + b, src.dtype), V((nz,) + b, src.dtype), V((nz - 1,) + b, src.dtype), V((nz - 1,) + b, src.dtype)]

def scatter_kernel(n, nz, line_only, ahead, *refs):
    refs = list(refs)
    take = lambda k: [refs.pop(0) for _ in range(k)]
    srcs, outs = take(n), take(n)
    bufs = [take(4 if lo else 6) for lo in line_only]
    sems = take(7)
    at = Place(nz)
    at.barrier()
    ss = [Scatter(at, srcs[i], outs[i], bufs[i], [s.at[i] for s in sems], line_only[i]) for i in range(n)]
    for s in ss[:ahead]: s.start()
    for t in range(n + nz + 2):
        def stage(k): return ss[t - k] if 0 <= t - k < n else None
        if t + ahead < n: ss[t + ahead].start()
        if stage(0): stage(0).after_pair()
        if stage(1): stage(1).after_second()
        if stage(2):
            stage(2).after_first(); stage(2).z_step(1)
        for h in range(2, nz):
            if stage(h + 1): stage(h + 1).z_step(h)
        if stage(nz + 1): stage(nz + 1).finish()
    for s in ss: s.drain()

def scatter_all(srcs, line_only, outs, nz, ahead=2, name="scatter_grads", cid=2):
    n = len(srcs)
    D = pltpu.SemaphoreType.DMA
    scratch = [b for s, lo in zip(srcs, line_only) for b in rs_bufs(s, lo, nz)]
    return pl.pallas_call(partial(scatter_kernel, n, nz, line_only, ahead), name=name, out_shape=outs,
        in_specs=[pl.BlockSpec(memory_space=pl.ANY)] * n, out_specs=[pl.BlockSpec(memory_space=pltpu.VMEM)] * n,
        scratch_shapes=scratch + [D((n, 4)), D((n, 4)), D((n, nz + 1)), D((n, nz + 1)), D((n, nz + 1)), D((n, nz + 1)), D((n,))],
        compiler_params=pltpu.CompilerParams(collective_id=cid, has_side_effects=True, vmem_limit_bytes=63 * MIB))(*srcs)


def pad16(r):
    return (r + 15) // 16 * 16


PIECES = (("small", 0), ("kv", 0), ("tok", 0), ("kv", 1), ("tok", 1), ("qkv", 0), ("qkv", 1), ("qkv", 2), ("ao", 0), ("ct", 0), ("cq", 0),
          ("co", 0), ("ct", 1), ("up", 0), ("up", 1), ("up", 2), ("up", 3), ("dn", 0), ("dn", 1))
lines_only = ("tok", "ct")
hop_lag, first_lag, second_lag, whole_lag, send_ahead, units_per_step = 0, 3, 4, 5, 2, 4


def piece(ref, name, c):
    cut = sum(k == name for k, _ in PIECES)
    if cut == 1:
        return ref
    if name in lines_only:
        return ref.at[c:c + 1]
    lead = (slice(None),) * (len(ref.shape) - 2)
    if name == "dn":
        tiles = ref.shape[-2] // 16
        return ref.at[lead + (slice(tiles * c // cut * 16, tiles * (c + 1) // cut * 16),)]
    cols = ref.shape[-1] // cut
    return ref.at[lead + (slice(None), slice(c * cols, (c + 1) * cols))]


def forward_gather(z, arrays, wanted, times, pool, nz):
    names = list(arrays)
    S = jax.ShapeDtypeStruct
    whole, stages = {}, []
    for k, b in arrays.items():
        if k in lines_only:
            whole[k] = S((b.shape[0], nz, 2) + b.shape[1:], b.dtype)
            stages.append(pltpu.VMEM(b.shape, b.dtype))
        else:
            r = pad16(b.shape[0])
            whole[k] = S((2, 2, nz, 2, r, b.shape[1]), b.dtype)
            stages.append(pltpu.VMEM((r, b.shape[1]), b.dtype))
    saved = {**saved_shapes(z), "back_y": S((z.MB, z.stream, z.width), BF)}
    share = {"up": "qkv", "ct": "tok"}
    room = {k: whole[k] for k in names if k not in share}
    room["qkv"] = whole["up"]
    count = len(PIECES)

    def kernel(*refs):
        refs = list(refs)
        take = lambda k: [refs.pop(0) for _ in range(k)]
        blocks = dict(zip(names, take(len(names))))
        r = Refs(["wanted", "times", "pool"], take(3))
        landed = dict(zip(names, take(len(names))))
        kept = dict(zip(saved, take(len(saved))))
        stage = dict(zip(names, take(len(names))))
        r.__dict__.update(zip(saved, take(len(saved))))
        bufs = dict(zip(room, take(len(room))))
        r.bias, r.upb, loads, saves = take(4)
        sems = take(5)
        at = Place(nz)
        for k in names:
            b, s = blocks[k], stage[k]
            if s.shape == b.shape:
                s[...] = b[...]
            else:
                s[...] = jnp.zeros(s.shape, s.dtype)
                s[:b.shape[0], :] = b[...]
        at.barrier()
        gs = [Gather(at, piece(stage[k], k, c), piece(landed[k], k, c), [s.at[j] for s in sems], k in lines_only)
              for j, (k, c) in enumerate(PIECES)]

        def save(k):
            pltpu.make_async_copy(getattr(r, k), kept[k], saves.at[list(saved).index(k)]).start()
        r.save = save
        def buffer(k):
            if k in ("qkv", "up"):
                return bufs["qkv"].at[:, :, :, :, :, :whole[k].shape[-1]]
            return bufs[share.get(k, k)]
        def load(j):
            k, c = PIECES[j]
            return pltpu.make_async_copy(piece(landed[k], k, c), piece(buffer(k), k, c), loads.at[j])
        def ready(k):
            b = bufs[share.get(k, k)]
            if k in lines_only:
                return b.reshape(z.MB, z.stream, z.width)
            flat = b.reshape(GROUPS * b.shape[-2], b.shape[-1])
            return flat.at[:, :whole[k].shape[-1]] if k in ("qkv", "up") else flat

        there, started, waited = set(), set(), set()
        free = set(room)
        work = forward_steps(z, ready, r)
        state = {"need": next(work), "done": False}
        def start_loads():
            for j in sorted(there - started):
                if PIECES[j][0] in free:
                    load(j).start()
                    started.add(j)
        def advance(units):
            while units and not state["done"]:
                need = state["need"]
                if need:
                    if need == "ao":
                        free.add("up")
                    if need == "qkv":
                        free.add("ct")
                    start_loads()
                    ask = {j for j, (k, c) in enumerate(PIECES) if k == need or k + str(c) == need}
                    if not ask <= started:
                        return
                    for j in sorted(ask - waited):
                        load(j).wait()
                    waited.update(ask)
                try:
                    state["need"] = next(work)
                except StopIteration:
                    state["done"] = True
                units -= 1

        for g in gs[:send_ahead]:
            g.start()
        for t in range(count + whole_lag):
            def stage_of(lag):
                return gs[t - lag] if 0 <= t - lag < count else None
            if t + send_ahead < count:
                gs[t + send_ahead].start()
            for j in range(1, nz):
                if g := stage_of(j - 1):
                    g.hop(j)
            if g := stage_of(nz - 2):
                g.z_done()
            if g := stage_of(first_lag):
                g.after_first()
            if g := stage_of(second_lag):
                g.after_second()
            if g := stage_of(whole_lag):
                g.whole()
                there.add(t - whole_lag)
                start_loads()
            advance(units_per_step if t < count + whole_lag - 1 else 1 << 20)
        for g in gs:
            g.drain()
        for i, k in enumerate(saved):
            pltpu.make_async_copy(getattr(r, k), kept[k], saves.at[i]).wait()

    V = pl.BlockSpec(memory_space=pltpu.VMEM)
    A = pl.BlockSpec(memory_space=pl.ANY)
    D = pltpu.SemaphoreType.DMA
    got = pl.pallas_call(kernel, name="gather_forward", out_shape=list(whole.values()) + list(saved.values()),
        in_specs=[V] * (len(names) + 3), out_specs=[A] * (len(names) + len(saved)),
        scratch_shapes=stages + [pltpu.VMEM(s.shape, s.dtype) for s in saved.values()] + [pltpu.VMEM(s.shape, s.dtype) for s in room.values()]
            + [pltpu.VMEM((HEADS, z.length, z.length), F32), pltpu.VMEM((1, z.ff), F32), D((count,)), D((len(saved),))] + sem_shapes(count, nz),
        compiler_params=pltpu.CompilerParams(collective_id=1, has_side_effects=True, vmem_limit_bytes=63 * MIB))(*arrays.values(), wanted, times, pool)
    flat = lambda k, v: v.reshape(-1, v.shape[-1])
    return {k: flat(k, v) for k, v in zip(names, got) if k in WEIGHTS}, dict(zip(saved, got[len(names):]))

def scatter_named(lines, small, grads, shards, z, nz):
    S = jax.ShapeDtypeStruct
    tok = z.length // 2
    as_line = lambda v: v.reshape(z.MB, nz, 2, tok, z.width)
    as_blocks = lambda v: v.reshape(2, 2, nz, 2, v.shape[0] // GROUPS, v.shape[1])
    order = ["dn", "up", "co", "kv", "cq", "ao", "qkv"]
    srcs = [as_line(lines["y"])] + [as_blocks(grads[k]) for k in order] + [as_blocks(small), as_line(lines["x"])]
    line = [True] + [False] * 8 + [True]
    outs = [S((z.MB, tok, z.width), BF)] + [S(shards[k].shape, F32) for k in order] + [S((8, 128), F32), S((z.MB, tok, z.width), BF)]
    got = scatter_all(srcs, line, outs, nz)
    return got[0], got[-1], got[-2], dict(zip(order, got[1:-2]))


def vectors(norm1_gain, norm2_gain, norm3_gain, attn_out_bias, cca_out_bias, ffw_down_bias, rel_table, ffw_up_bias):
    return [norm1_gain, norm2_gain, norm3_gain, attn_out_bias, cca_out_bias, ffw_down_bias, rel_table, ffw_up_bias]


def to_groups(v):
    small = v.shape[0] // GROUPS
    big = (small + 15) // 16 * 16
    return jnp.pad(v.reshape(GROUPS, small, -1), ((0, 0), (0, big - small), (0, 0))).reshape(GROUPS * big, -1)


def from_groups(v, rows):
    return v.reshape(GROUPS, v.shape[0] // GROUPS, -1)[:, :rows // GROUPS].reshape(rows, -1)


def body(tokens, cotangent, lengths, deal, pool, neighbour_ids, norm1_gain, attn_qkv, attn_out, attn_out_bias, rel_table,
         norm2_gain, cca_query, cca_kv, cca_out, cca_out_bias, norm3_gain, ffw_up, ffw_up_bias, ffw_down, ffw_down_bias):
    members, member = lax.axis_size("fsdp"), lax.axis_index("fsdp")
    devices = members * lax.axis_size("dp")
    MB, tok_rows, width = tokens.shape
    length = 2 * tok_rows
    z = Sizes(MB, length, width, HEADS * HEAD_DIM, ffw_up.shape[1], pool.shape[1])
    z.stream = members * tok_rows
    shards = {"qkv": attn_qkv, "ao": attn_out, "cq": cca_query, "kv": cca_kv, "co": cca_out, "up": ffw_up, "dn": ffw_down}
    vecs = vectors(norm1_gain, norm2_gain, norm3_gain, attn_out_bias, cca_out_bias, ffw_down_bias, rel_table, ffw_up_bias)

    ids = jnp.arange(members, dtype=jnp.int32)
    lens, dealt = lengths[:, 0], deal[:, 0]
    starts = jnp.sum(jnp.where(ids[None, :, None] > ids[None, None, :], lens[:, None, :], 0), 2)
    mine = dealt == member
    own_start = jnp.sum(jnp.where(mine, starts, 0), 1)
    own_len = jnp.sum(jnp.where(mine, lens, 0), 1)
    place = jnp.arange(length, dtype=jnp.int32)
    wanted = jnp.where(place[None] < own_len[:, None], own_start[:, None] + place[None], -1).reshape(-1)
    wanted = jnp.broadcast_to(wanted[:, None], (MB * length, 128))
    spans = length // CH
    ids3 = neighbour_ids.reshape(MB, spans, K_NB)
    held = jnp.sum((ids3[..., None] == jnp.arange(z.pool, dtype=jnp.int32)).astype(F32), 2)
    row = jnp.arange(low_row, length, dtype=jnp.int32)
    in_span = ((row[:, None] - (CH - 1)) // CH == jnp.arange(spans, dtype=jnp.int32)) & (row[:, None] >= CH - 1)
    times = jnp.sum(jnp.where(in_span[None, :, :, None], held[:, None], 0.0), 2)
    times = jnp.broadcast_to(times[..., None], times.shape + (NL,)).reshape(MB, z.win, z.keys)
    neighbours = pool.reshape(MB * z.keys, width)

    direct = lax.axis_size("dp") == 4 and members % 2 == 0 and devices == GROUPS
    nz = members // 2
    if direct:
        packed = jnp.concatenate([jnp.pad(v[None], ((0, 0), (0, 128 - v.shape[0]))) for v in vecs] + [jnp.zeros((SMALLS - 8, 128), BF)], 0)
        weights, saved = forward_gather(z, {"small": packed, "tok": tokens, "ct": cotangent, **shards}, wanted, times, neighbours, nz)
    else:
        whole = lambda v: lax.all_gather(v, ("dp", "fsdp"), axis=0, tiled=True)
        rows = [jnp.pad(w, ((0, 0), (0, 128 - w.shape[1])))[:, None] for w in [whole(v).reshape(GROUPS, -1) for v in vecs]]
        packed = jnp.concatenate(rows + [jnp.zeros((GROUPS, SMALLS - 8, 128), BF)], 1).reshape(GROUPS * SMALLS, 128)
        gathered = {"small": packed, **{k: to_groups(whole(v)) for k, v in shards.items()},
                    "tok": lax.all_gather(tokens, "fsdp", axis=1, tiled=True), "ct": lax.all_gather(cotangent, "fsdp", axis=1, tiled=True)}
        weights = {k: gathered[k] for k in WEIGHTS}
        saved = forward_plain(z, gathered, wanted, times, neighbours)
    back_y = saved.pop("back_y")
    grads, outs = backward_plain(z, weights, saved, wanted, times)
    back_x, small = outs["back_x"], outs["small_grad"]
    if direct:
        lines = {"y": back_y, "x": back_x}
        act, dx, small, mine = scatter_named(lines, small, grads, shards, z, nz)
        parts = [small[i, :v.shape[0]] for i, v in enumerate(vecs)]
    else:
        down = lambda v: lax.psum_scatter(v.astype(F32), ("dp", "fsdp"), scatter_dimension=0, tiled=True)
        line = lambda v: lax.psum_scatter(v, "fsdp", scatter_dimension=1, tiled=True)
        act, dx = line(back_y), line(back_x)
        mine = {k: down(from_groups(grads[k], shards[k].shape[0] * devices)) for k in shards}
        small = small.reshape(GROUPS, 8, 128)
        parts = [down(small[:, i, :v.shape[0] * devices // GROUPS].reshape(-1)) for i, v in enumerate(vecs)]
    g1, g2, g3, ba, bc, bd, rel, upb = parts
    return (act, dx, outs["pool_grad"].reshape(pool.shape), g1, mine["qkv"], mine["ao"], ba, rel, g2, mine["cq"], mine["kv"],
            mine["co"], bc, g3, mine["up"], upb, mine["dn"], bd)


def solution(mesh):
    everywhere = ("dp", "fsdp")
    rows, vec = P(everywhere, None), P(everywhere)
    slots = P(None, everywhere, None)
    return jax.shard_map(
        body,
        mesh=mesh,
        in_specs=(slots, slots, P(None, "dp", None), P(None, "dp", None), P(None, everywhere, None, None), slots,
                  vec, rows, rows, vec, vec, vec, rows, rows, rows, vec, vec, rows, vec, rows, vec),
        out_specs=(slots, slots, P(None, everywhere, None, None), vec, rows, rows, vec, vec, vec, rows, rows, rows, vec, vec,
                   rows, vec, rows, vec),
        check_vma=False,
    )
```

```python
from functools import partial

import jax
import jax.numpy as jnp
from jax import lax
from jax.experimental import pallas as pl
from jax.experimental.pallas import tpu as pltpu
from jax.sharding import PartitionSpec as P

K_0 = "0"
K_A = "a"
K_AO = "ao"
K_BACK_X = "back_x"
K_BACK_Y = "back_y"
K_C = "c"
K_CKV = "ckv"
K_CO = "co"
K_CQ = "cq"
K_CT = "ct"
K_DC = "dc"
K_DH = "dh"
K_DN = "dn"
K_DONE = "done"
K_DP = "dp"
K_DU = "du"
K_E = "e"
K_EP = "ep"
K_FINISH = "finish"
K_FIRST = "first"
K_FSDP = "fsdp"
K_GL = "gl"
K_GRAD = "grad"
K_H1 = "h1"
K_H2 = "h2"
K_JOIN = "join"
K_KV = "kv"
K_N1 = "n1"
K_N2 = "n2"
K_N3 = "n3"
K_NEED = "need"
K_PAIR = "pair"
K_PC = "pc"
K_POOL = "pool"
K_POOL_GRAD = "pool_grad"
K_PS = "ps"
K_QKV = "qkv"
K_SAVED = "saved"
K_SECOND = "second"
K_SLOPE = "slope"
K_SMALL = "small"
K_SMALL_GRAD = "small_grad"
K_SPT = "spt"
K_TABLE = "table"
K_TILE = "tile"
K_TILES = "tiles"
K_TIMES = "times"
K_TOK = "tok"
K_UP = "up"
K_UP0 = "up0"
K_UPB_SUM = "upb_sum"
K_VEC = "vec"
K_WANTED = "wanted"
K_WEIGHT = "weight"
K_X = "x"
K_Y = "y"
MIB = 1 << 20
F32, BF = jnp.float32, jnp.bfloat16
HEADS, HEAD_DIM, CH, NL, K_NB, NB = 16, 64, 64, 128, 2, 64
epsilon = 1e-06
masked_score = -1e30
tile = 512
unroll = 4
low_row = 48
GROUPS = 32
SMALLS = 16
G1, G2, G3, BA, BC, BD, REL, UPB = range(8)


def mm(a, b):
    return jnp.dot(a, b, preferred_element_type=F32)
def mm_tn(a, b):
    return lax.dot_general(a, b, (((0,), (0,)), ((), ())), preferred_element_type=F32)
def mm_nt(a, b):
    return lax.dot_general(a, b, (((1,), (1,)), ((), ())), preferred_element_type=F32)
def iota(shape, dim):
    return lax.broadcasted_iota(jnp.int32, shape, dim)
def onehot(cond):
    return jnp.where(cond, 1.0, 0.0).astype(BF)
def split2(v):
    hi = v.astype(BF)
    return hi, (v - hi.astype(F32)).astype(BF)
def columns(i, size):
    return pl.ds(pl.multiple_of(i * size, size), size)
def loop(count, body):
    def step(i, carry):
        body(i)
        return carry
    lax.fori_loop(0, count, step, 0)


def spread(width):
    small = width // GROUPS
    big = (small + 15) // 16 * 16
    row, col = iota((width, GROUPS * big), 0), iota((width, GROUPS * big), 1)
    return onehot((col // big == row // small) & (col % big == row % small))


def gather_up(width):
    small = width // GROUPS
    big = (small + 15) // 16 * 16
    row, col = iota((GROUPS * big, width), 1), iota((GROUPS * big, width), 0)
    return onehot((col // big == row // small) & (col % big == row % small))


def dense(v, back):
    hi, lo = split2(v)
    return mm(hi, back) + mm(lo, back)


def small_rows(packed, width):
    per = width // GROUPS
    put = onehot(iota((128, width), 0) == iota((128, width), 1) % per)
    placed = mm(packed, put)
    shape = (GROUPS * SMALLS, width)
    placed = jnp.where(iota(shape, 0) // SMALLS == iota(shape, 1) // per, placed, 0.0).astype(BF)
    take = onehot(iota((SMALLS, GROUPS * SMALLS), 1) % SMALLS == iota((SMALLS, GROUPS * SMALLS), 0))
    return mm(take, placed)


def table_rows(packed, length):
    per = NB * HEADS // GROUPS // HEADS
    width = length // NB
    take = onehot(iota((GROUPS, GROUPS * SMALLS), 1) == iota((GROUPS, GROUPS * SMALLS), 0) * SMALLS + REL)
    held = mm(take, packed).astype(BF)
    far = (length - iota((GROUPS, length), 1)) % length // width
    at = mm_tn(held, onehot(far // per == iota((GROUPS, length), 0)))
    which = (length - iota((HEADS, length), 1)) % length // width % per
    out = jnp.zeros((HEADS, length), F32)
    for k in range(per):
        out = jnp.where(which == k, at[k * HEADS:(k + 1) * HEADS], out)
    return out


def biases(rows, bias):
    length = bias.shape[1]
    below = iota((length, length), 0) >= iota((length, length), 1)
    for h in range(HEADS):
        wide = jnp.broadcast_to(rows[h:h + 1], (length, length))
        bias[h] = jnp.where(below, pltpu.roll(wide, 0, 1, stride=1, stride_axis=0), masked_score)


def rms(v):
    return lax.rsqrt(jnp.mean(v * v, -1, keepdims=True) + epsilon)


def norm(v, gain):
    return (v * rms(v) * gain).astype(BF)


def norm_back(v, gain, dn):
    r = rms(v)
    unit = v * r
    gained = dn * gain
    return r * (gained - unit * jnp.mean(gained * unit, -1, keepdims=True)), jnp.sum(dn * unit, 0, keepdims=True)


def halves(v):
    first = iota(v.shape, 1) < HEAD_DIM
    zero = jnp.zeros(v.shape, v.dtype)
    return jnp.concatenate([jnp.where(first, v, zero), jnp.where(first, zero, v)], 0)


def joined(v):
    n = v.shape[0] // 2
    return jnp.where(iota((n, v.shape[1]), 1) < HEAD_DIM, v[:n], v[n:])


def head_parts(count, parts, body):
    pairs = HEADS // 2
    total = count * pairs
    def step(i, carry):
        m, p = i // pairs, i % pairs
        body(m, p, p * 2 * HEAD_DIM)
        return carry
    for k in range(parts):
        lax.fori_loop(total * k // parts, total * (k + 1) // parts, step, 0, unroll=unroll)
        yield


class Sizes:
    def __init__(self, MB, length, width, att, ff, pool):
        self.MB, self.length, self.width, self.att, self.ff, self.pool = MB, length, width, att, ff, pool
        self.rows = MB * length
        self.win = length - low_row
        self.wide = GROUPS * ((width // GROUPS + 15) // 16 * 16)
        self.keys = pool * NL


def fwd_self(z, join, bias, ps, att):
    factor = HEAD_DIM ** -0.5
    def body(m, p, c):
        rows = pl.ds(pl.multiple_of(m * z.length, 128), z.length)
        at = lambda part: pl.ds(pl.multiple_of(part * z.att + c, 128), 128)
        q, k, v = join[rows, at(0)], join[rows, at(1)], join[rows, at(2)]
        s = mm_nt(halves(q), k) * factor + jnp.concatenate([bias[2 * p], bias[2 * p + 1]], 0)
        e = jnp.exp(s - jnp.max(s, -1, keepdims=True))
        soft = e * (1.0 / jnp.sum(e, -1, keepdims=True))
        ps[m, p] = soft
        att[rows, at(0)] = joined(mm(soft.astype(BF), v)).astype(BF)
    yield from head_parts(z.MB, 4, body)


def fwd_cross(z, cq, ckv, times, pc, c_out):
    factor = HEAD_DIM ** -0.5
    for m in range(z.MB):
        c_out[m * z.length:m * z.length + low_row] = jnp.zeros((low_row, z.att), BF)
    def body(m, p, c):
        rows = pl.ds(pl.multiple_of(m * z.length + low_row, 16), z.win)
        keys = pl.ds(pl.multiple_of(m * z.keys, 128), z.keys)
        at = lambda part: pl.ds(pl.multiple_of(part * z.att + c, 128), 128)
        q, k, v = cq[rows, at(0)], ckv[keys, at(0)], ckv[keys, at(1)]
        cnt = times[m]
        cnt = jnp.concatenate([cnt, cnt], 0)
        s = jnp.where(cnt > 0, mm_nt(halves(q), k) * factor, masked_score)
        e = jnp.exp(s - jnp.max(s, -1, keepdims=True))
        total = jnp.sum(e * cnt, -1, keepdims=True)
        soft = e * (1.0 / jnp.where(total > 0, total, 1.0))
        for k in range(z.keys // NL):
            pc[m, p, k] = soft[:, k * NL:(k + 1) * NL]
        c_out[rows, at(0)] = joined(mm((soft.astype(BF).astype(F32) * cnt).astype(BF), v)).astype(BF)
    yield from head_parts(z.MB, 4, body)


def gelu_parts(u):
    k = 0.7978845608028654
    t = jnp.tanh(k * (u + 0.044715 * u * u * u))
    half = 0.5 * (1.0 + t)
    return u * half, half + 0.5 * u * (1.0 - t * t) * k * (1.0 + 3 * 0.044715 * u * u)


def fwd_up(z, n3, up, upb, gl, slope, at):
    u = mm(n3[...], up[:, at]) + upb[:, at]
    value, d = gelu_parts(u)
    gl[:, at] = value.astype(BF)
    slope[:, at] = d


def project(left, weight, out, size=tile):
    for i in range(out.shape[1] // size):
        at = slice(i * size, (i + 1) * size)
        out[:, at] = mm(left[...], weight[:, at]).astype(out.dtype)
        yield


def project_nt(left, weight, out, size=tile):
    for i in range(out.shape[1] // size):
        at = slice(i * size, (i + 1) * size)
        out[:, at] = mm_nt(left[...], weight[at, :]).astype(out.dtype)
        yield


def outer(left, right, out, lo, hi, size=256):
    for i in range(out.shape[0] // size):
        at = slice(i * size, (i + 1) * size)
        out[at, lo:hi] = mm_tn(left[:, at], right[:, lo:hi]).astype(out.dtype)
        yield


def bwd_self(z, join, ps, da, dq, table_sum):
    factor = HEAD_DIM ** -0.5
    def body(m, p, c):
        rows = pl.ds(pl.multiple_of(m * z.length, 128), z.length)
        at = lambda part: pl.ds(pl.multiple_of(part * z.att + c, 128), 128)
        q, k, v = join[rows, at(0)], join[rows, at(1)], join[rows, at(2)]
        d = halves(da[rows, at(0)])
        soft = ps[m, p]
        dp = mm_nt(d, v)
        ds = (soft * (dp - jnp.sum(dp * soft, -1, keepdims=True))).astype(BF)
        dq[rows, at(0)] = (joined(mm(ds, k)) * factor).astype(BF)
        dq[rows, at(1)] = (mm_tn(ds, halves(q)) * factor).astype(BF)
        dq[rows, at(2)] = mm_tn(soft.astype(BF), d).astype(BF)
        wide = ds.astype(F32)
        for k in range(2):
            heads = pl.ds(pl.multiple_of((2 * p + k) * z.length, 128), z.length)
            table_sum[:, heads] += wide[k * z.length:(k + 1) * z.length]
    yield from head_parts(z.MB, 4, body)


def bwd_cross(z, cq, ckv, times, pc, dc, dcq, dckv):
    factor = HEAD_DIM ** -0.5
    for m in range(z.MB):
        dcq[m * z.length:m * z.length + low_row] = jnp.zeros((low_row, z.att), BF)
    def body(m, p, c):
        rows = pl.ds(pl.multiple_of(m * z.length + low_row, 16), z.win)
        keys = pl.ds(pl.multiple_of(m * z.keys, 128), z.keys)
        at = lambda part: pl.ds(pl.multiple_of(part * z.att + c, 128), 128)
        q, k, v = cq[rows, at(0)], ckv[keys, at(0)], ckv[keys, at(1)]
        d = halves(dc[rows, at(0)])
        cnt = times[m]
        cnt = jnp.concatenate([cnt, cnt], 0)
        soft = jnp.concatenate([pc[m, p, k] for k in range(z.keys // NL)], 1)
        dp = mm_nt(d, v)
        ds = (soft * (dp - jnp.sum(dp * soft * cnt, -1, keepdims=True))).astype(BF)
        ds = (ds.astype(F32) * cnt).astype(BF)
        pb = (soft.astype(BF).astype(F32) * cnt).astype(BF)
        dcq[rows, at(0)] = (joined(mm(ds, k)) * factor).astype(BF)
        dckv[keys, at(0)] = (mm_tn(ds, halves(q)) * factor).astype(BF)
        dckv[keys, at(1)] = mm_tn(pb, d).astype(BF)
    yield from head_parts(z.MB, 4, body)


def exact(a, b, dims):
    return lax.dot_general(a, b, (dims, ((), ())), precision=lax.Precision.HIGHEST, preferred_element_type=F32)


def table_grad(table_sum):
    length = table_sum.shape[0]
    flip = onehot(iota((length, length), 0) + iota((length, length), 1) == length - 1)
    hi, lo = split2(table_sum)
    flipped = mm(flip, hi) + mm(flip, lo)
    rows = []
    for h in range(HEADS):
        turned = pltpu.roll(flipped[:, h * length:(h + 1) * length], 0, 1, stride=1, stride_axis=0)
        rows.append(jnp.sum(turned, 0, keepdims=True))
    return jnp.concatenate(rows, 0)


WEIGHTS = (K_QKV, K_AO, K_CQ, K_KV, K_CO, K_UP, K_DN)


def forward_steps(z, ready, r):
    yield K_SMALL
    r.sp[...] = spread(z.width)
    r.spt[...] = gather_up(z.width)
    r.save(K_SPT)
    packed = ready(K_SMALL)[...]
    r.vec[...] = small_rows(packed, z.width)
    r.save(K_VEC)
    yield
    def upb(i):
        at = columns(i, tile)
        per = z.ff // GROUPS
        put = onehot(iota((128, tile), 0) == (iota((128, tile), 1) + i * tile) % per)
        placed = mm(packed, put)
        shape = (GROUPS * SMALLS, tile)
        mine = (iota(shape, 0) // SMALLS == (iota(shape, 1) + i * tile) // per) & (iota(shape, 0) % SMALLS == UPB)
        r.upb[:, at] = jnp.sum(jnp.where(mine, placed, 0.0), 0, keepdims=True)
    loop(z.ff // tile, upb)
    biases(table_rows(packed, z.length), r.bias)
    half = z.keys // 2
    for i in range(z.MB * 2):
        rows = slice(i * half, (i + 1) * half)
        r.ep[rows, :] = mm(r.pool[rows, :], r.sp[...]).astype(BF)
        yield
    r.save(K_EP)
    yield K_KV
    kv = ready(K_KV)
    yield from project(r.ep, kv, r.ckv, 256)
    r.save(K_CKV)
    yield K_TOK
    tok = ready(K_TOK)
    stream = tok.shape[1]
    for m in range(z.MB):
        rows = slice(m * z.length, (m + 1) * z.length)
        pick = onehot(r.wanted[rows, :1] == iota((z.length, stream), 1))
        r.x[rows] = mm(pick, tok[m])
    r.save(K_X)
    yield
    r.n1[...] = mm(norm(r.x[...], r.vec[G1:G1 + 1]), r.sp[...]).astype(BF)
    r.save(K_N1)
    yield K_QKV
    yield from project(r.n1, ready(K_QKV), r.join)
    r.save(K_JOIN)
    yield from fwd_self(z, r.join, r.bias, r.ps, r.a)
    r.save(K_PS)
    r.save(K_A)
    yield K_AO
    h1 = r.x[...] + (mm(r.a[...], ready(K_AO)[...]) + r.vec[BA:BA + 1])
    r.h1[...] = h1
    r.save(K_H1)
    r.n2[...] = mm(norm(h1, r.vec[G2:G2 + 1]), r.sp[...]).astype(BF)
    r.save(K_N2)
    yield K_CQ
    yield from project(r.n2, ready(K_CQ), r.cq)
    r.save(K_CQ)
    yield from fwd_cross(z, r.cq, r.ckv, r.times, r.pc, r.c)
    r.save(K_PC)
    r.save(K_C)
    yield K_CO
    h2 = r.h1[...] + (mm(r.c[...], ready(K_CO)[...]) + r.vec[BC:BC + 1])
    r.h2[...] = h2
    r.save(K_H2)
    r.n3[...] = mm(norm(h2, r.vec[G3:G3 + 1]), r.sp[...]).astype(BF)
    r.save(K_N3)
    yield K_CT
    ct = ready(K_CT)
    for m in range(z.MB):
        rows = slice(m * z.length, (m + 1) * z.length)
        pick = onehot(r.wanted[rows, :1] == iota((z.length, stream), 1))
        r.ct[rows] = mm(pick, ct[m]).astype(BF)
    r.save(K_CT)
    step = z.ff // 4
    for i in range(4):
        yield K_UP + str(i)
        cut = (step // 2 + 127) // 128 * 128
        for lo, hi in ((0, cut), (cut, step)):
            fwd_up(z, r.n3, ready(K_UP), r.upb, r.gl, r.slope, slice(i * step + lo, i * step + hi))
            yield
    r.save(K_GL)
    r.save(K_SLOPE)
    yield K_DN
    dn = ready(K_DN)
    out = mm(r.gl[...], dn[...])
    y = (r.h2[...] + (out + r.vec[BD:BD + 1])).astype(BF)
    for m in range(z.MB):
        rows = slice(m * z.length, (m + 1) * z.length)
        pick = onehot(r.wanted[rows, :1] == iota((z.length, stream), 1))
        r.back_y[m] = mm_tn(pick, y[rows]).astype(BF)
    r.save(K_BACK_Y)


def backward_steps(z, ready, r):
    vec, back = r.vec, r.spt
    small = {}
    ones = lambda v: jnp.sum(v.astype(F32), 0, keepdims=True)
    def pieces(name, left, right):
        out, count = ready(name), r.cuts[name]
        size = out.shape[1] // count
        for c in range(count):
            yield from outer(left, right, out, c * size, (c + 1) * size)
            yield K_GRAD, name, c
    yield K_SAVED, (K_CT,)
    dn = ready(K_DN)
    small[BD] = ones(r.ct[...])
    step = z.ff // 4
    for i in range(4):
        at = slice(i * step, (i + 1) * step)
        yield K_TILE, i
        du = (mm_nt(r.ct[...], dn[at, :]) * r.slope_tile(i)).astype(BF)
        r.du[:, at] = du
        r.upb_sum[:, at] = ones(du)
    yield K_SAVED, (K_GL,)
    yield from outer(r.gl, r.ct, ready(K_DN), 0, z.width)
    yield K_GRAD, K_DN, 0
    yield K_GRAD, K_DN, 1
    yield K_SAVED, (K_SPT, K_VEC, K_H2, K_N3)
    yield K_WEIGHT, K_UP
    dn3 = dense(mm_nt(r.du[...], ready(K_UP)[...]), back[...])
    dw, small[G3] = norm_back(r.h2[...], vec[G3:G3 + 1], dn3)
    dh = r.ct[...].astype(F32) + dw
    r.dh[...] = dh
    r.e[...] = dh.astype(BF)
    small[BC] = ones(dh.astype(BF))
    yield
    yield from pieces(K_UP, r.n3, r.du)
    yield K_WEIGHT, K_CO
    yield from project_nt(r.e, ready(K_CO), r.dc)
    yield K_SAVED, (K_C,)
    yield from pieces(K_CO, r.c, r.e)
    yield K_SAVED, (K_CQ, K_CKV, K_PC)
    yield from bwd_cross(z, r.cq, r.ckv, r.times, r.pc, r.dc, r.dcq, r.dckv)
    yield K_SAVED, (K_EP,)
    yield from pieces(K_KV, r.ep, r.dckv)
    yield K_WEIGHT, K_CQ
    yield K_SAVED, (K_H1, K_N2)
    dn2 = dense(mm_nt(r.dcq[...], ready(K_CQ)[...]), back[...])
    dw, small[G2] = norm_back(r.h1[...], vec[G2:G2 + 1], dn2)
    dh = r.dh[...] + dw
    r.dh[...] = dh
    r.e[...] = dh.astype(BF)
    small[BA] = ones(dh.astype(BF))
    yield
    yield from pieces(K_CQ, r.n2, r.dcq)
    yield K_WEIGHT, K_AO
    yield from project_nt(r.e, ready(K_AO), r.dc)
    yield K_SAVED, (K_A,)
    yield from pieces(K_AO, r.a, r.e)
    yield K_SAVED, (K_JOIN, K_PS)
    r.table[...] = jnp.zeros(r.table.shape, F32)
    yield from bwd_self(z, r.join, r.ps, r.dc, r.dq, r.table)
    yield K_WEIGHT, K_QKV
    yield K_SAVED, (K_X, K_N1)
    dn1 = dense(mm_nt(r.dq[...], ready(K_QKV)[...]), back[...])
    dw, small[G1] = norm_back(r.x[...], vec[G1:G1 + 1], dn1)
    dx = (r.dh[...] + dw).astype(BF)
    stream = r.back_x.shape[1]
    for m in range(z.MB):
        rows = slice(m * z.length, (m + 1) * z.length)
        pick = onehot(r.wanted[rows, :1] == iota((z.length, stream), 1))
        r.back_x[m] = mm_tn(pick, dx[rows]).astype(BF)
    yield K_GRAD, K_X, 0
    pack_smalls(z, small, r)
    yield K_GRAD, K_SMALL, 0
    yield from pieces(K_QKV, r.n1, r.dq)


def pool_steps(z, ready, r):
    yield K_WEIGHT, K_KV
    kv = ready(K_KV)
    size = z.wide // 4
    for i in range(4):
        at = slice(i * size, (i + 1) * size)
        r.pool_hi[:, at], r.pool_lo[:, at] = split2(mm_nt(r.dckv[...], kv[at, :]))
        yield
    part = z.keys // 2
    for i in range(z.MB * 2):
        rows = slice(i * part, (i + 1) * part)
        r.put_pool(i, mm(r.pool_hi[rows, :], r.spt[...]) + mm(r.pool_lo[rows, :], r.spt[...]))
        yield


def pack_smalls(z, small, r):
    vecs = jnp.concatenate([small.get(i, jnp.zeros((1, z.width), F32)) for i in range(8)], 0)
    per = z.width // GROUPS
    shape = (GROUPS * 8, z.width)
    mine = iota(shape, 0) // 8 == iota(shape, 1) // per
    take = onehot(iota((GROUPS * 8, 8), 0) % 8 == iota((GROUPS * 8, 8), 1))
    put = onehot(iota((z.width, 128), 0) % per == iota((z.width, 128), 1))
    total = jnp.zeros((GROUPS * 8, 128), F32)
    for v in split2(vecs):
        total += mm(jnp.where(mine, mm(take, v), 0.0).astype(BF), put)
    per = z.ff // GROUPS
    bias = jnp.zeros((GROUPS, 128), F32)
    for i in range(z.ff // tile):
        shape = (GROUPS, tile)
        mine = iota(shape, 0) == (iota(shape, 1) + i * tile) // per
        put = onehot((iota((tile, 128), 0) + i * tile) % per == iota((tile, 128), 1))
        for v in split2(r.upb_sum[:, i * tile:(i + 1) * tile]):
            bias += mm(jnp.where(mine, jnp.broadcast_to(v.astype(F32), shape), 0.0).astype(BF), put)
    width = z.length // NB
    per = NB // GROUPS
    shape = (GROUPS, z.length)
    table = jnp.zeros((GROUPS, 128), F32)
    for v in split2(table_grad(r.table[...])):
        for k in range(per):
            mine = onehot((z.length - 1 - iota(shape, 1)) // width == iota(shape, 0) * per + k)
            put = onehot(iota((HEADS, 128), 0) + k * HEADS == iota((HEADS, 128), 1))
            table += mm(mm_nt(mine, v).astype(BF), put)
    for which, v in ((UPB, bias), (REL, table)):
        take = onehot(iota((GROUPS * 8, GROUPS), 0) == iota((GROUPS * 8, GROUPS), 1) * 8 + which)
        for part in split2(v):
            total += mm(take, part)
    r.small_grad[...] = total


class Refs:
    def __init__(self, names, refs):
        for n, ref in zip(names, refs): setattr(self, n, ref)


def weight_shapes(z):
    return {K_QKV: (z.wide, 3 * z.att), K_AO: (z.att, z.width), K_CQ: (z.wide, z.att), K_KV: (z.wide, 2 * z.att),
            K_CO: (z.att, z.width), K_UP: (z.wide, z.ff), K_DN: (z.ff, z.width)}


def saved_shapes(z):
    R = z.rows
    S = jax.ShapeDtypeStruct
    pairs = HEADS // 2
    return {K_SPT: S((z.wide, z.width), BF), K_VEC: S((SMALLS, z.width), F32), K_EP: S((z.MB * z.keys, z.wide), BF),
            K_CKV: S((z.MB * z.keys, 2 * z.att), BF), K_X: S((R, z.width), F32), K_N1: S((R, z.wide), BF),
            K_JOIN: S((R, 3 * z.att), BF), K_PS: S((z.MB, pairs, 2 * z.length, z.length), F32), K_A: S((R, z.att), BF),
            K_H1: S((R, z.width), F32), K_N2: S((R, z.wide), BF), K_CQ: S((R, z.att), BF),
            K_PC: S((z.MB, pairs, z.keys // NL, 2 * z.win, NL), F32), K_C: S((R, z.att), BF), K_H2: S((R, z.width), F32),
            K_N3: S((R, z.wide), BF), K_GL: S((R, z.ff), BF), K_SLOPE: S((R, z.ff), F32), K_CT: S((R, z.width), BF)}


def forward_plain(z, gathered, wanted, times, pool):
    names = list(gathered)
    saved = saved_shapes(z)
    outs = {**saved, K_BACK_Y: jax.ShapeDtypeStruct(gathered[K_TOK].shape, BF)}
    share = {K_UP: K_QKV, K_CT: K_TOK}
    room = {k: gathered[k].shape for k in names if k not in share}
    room[K_QKV] = gathered[K_UP].shape
    def kernel(*refs):
        n = len(names)
        held = dict(zip(names, refs[:n]))
        r = Refs([K_WANTED, K_TIMES, K_POOL], refs[n:n + 3])
        r.__dict__.update(zip(outs, refs[n + 3:n + 3 + len(outs)]))
        scratch = refs[n + 3 + len(outs):]
        sems, r.bias, r.upb, r.sp = scratch[:4]
        bufs = dict(zip(room, scratch[4:]))
        def view(k):
            return bufs[K_QKV].at[:, :gathered[k].shape[1]] if k in (K_QKV, K_UP) else bufs[share.get(k, k)]
        def copy(k):
            return pltpu.make_async_copy(held[k], view(k), sems.at[names.index(k)])
        for k in room:
            copy(k).start()
        r.save = lambda k: None
        for k in forward_steps(z, view, r):
            if k in (K_UP0, K_CT):
                copy(k.rstrip(K_0)).start()
            if k == K_UP0 or k in names:
                copy(k.rstrip(K_0)).wait()
    V = pl.BlockSpec(memory_space=pltpu.VMEM)
    A = pl.BlockSpec(memory_space=pl.ANY)
    return dict(zip(outs, pl.pallas_call(kernel, name="layer_forward", out_shape=list(outs.values()),
        in_specs=[A] * len(names) + [V] * 3, out_specs=[V] * len(outs),
        scratch_shapes=[pltpu.SemaphoreType.DMA((len(names),)), pltpu.VMEM((HEADS, z.length, z.length), F32), pltpu.VMEM((1, z.ff), F32), pltpu.VMEM((z.width, z.wide), BF)]
            + [pltpu.VMEM(v, BF) for v in room.values()],
        compiler_params=pltpu.CompilerParams(vmem_limit_bytes=63 * MIB))(*gathered.values(), wanted, times, pool)))


def backward_plain(z, weights, saved, wanted, times):
    names = list(WEIGHTS)
    shapes = weight_shapes(z)
    ins = list(saved)
    S = jax.ShapeDtypeStruct
    outs = {K_POOL_GRAD: S((z.MB * z.keys, z.width), F32), K_BACK_X: S((z.MB, z.stream, z.width), BF), K_SMALL_GRAD: S((GROUPS * 8, 128), F32)}
    part = z.keys // 2
    local = {K_DU: ((z.rows, z.ff), BF), K_UPB_SUM: ((1, z.ff), F32), K_DH: ((z.rows, z.width), F32), K_E: ((z.rows, z.width), BF),
             K_DC: ((z.rows, z.att), BF), "dcq": ((z.rows, z.att), BF), "dckv": ((z.MB * z.keys, 2 * z.att), BF),
             K_TABLE: ((z.length, HEADS * z.length), F32), K_TILES: ((2, max(z.rows, part), z.ff // 4), F32)}
    kept = [k for k in names if k != K_QKV]

    def kernel(*refs):
        refs = list(refs)
        take = lambda k: [refs.pop(0) for _ in range(k)]
        held = dict(zip(names, take(len(names))))
        r = Refs(ins + [K_WANTED, K_TIMES], take(len(ins) + 2))
        grads = dict(zip(names, take(len(names))))
        r.__dict__.update(zip(outs, take(len(outs))))
        sems, gsem, tsem, psem = take(4)
        bufs = dict(zip(kept, take(len(kept))))
        bufs[K_QKV] = bufs[K_UP].at[:, :shapes[K_QKV][1]]
        r.__dict__.update(zip(local, take(len(local))))
        r.dq = r.du.at[:, :3 * z.att]
        load = lambda k: pltpu.make_async_copy(held[k], bufs[k], sems.at[names.index(k)])
        store = lambda k: pltpu.make_async_copy(bufs[k], grads[k], gsem.at[names.index(k)])
        step = z.ff // 4
        r.slope_tiles, r.pool_tiles = r.tiles.at[:, :z.rows], r.tiles.at[:, :part, :z.width]
        r.pool_hi, r.pool_lo = r.ep, bufs[K_UP].at[:z.MB * z.keys, :z.wide]
        slope = lambda i: pltpu.make_async_copy(r.slope.at[:, i * step:(i + 1) * step], r.slope_tiles.at[i % 2], tsem.at[i % 2])
        slope(0).start()
        for k in (K_DN, K_UP, K_CO, K_CQ, K_AO):
            load(k).start()
        def slope_tile(i):
            if i + 1 < 4:
                slope(i + 1).start()
            slope(i).wait()
            return r.slope_tiles[i % 2]
        pool_copy = lambda i: pltpu.make_async_copy(r.pool_tiles.at[i % 2], r.pool_grad.at[i * part:(i + 1) * part], psem.at[i % 2])
        def put_pool(i, value):
            if i >= 2:
                pool_copy(i - 2).wait()
            r.pool_tiles[i % 2] = value
            pool_copy(i).start()
        r.slope_tile, r.put_pool = slope_tile, put_pool
        r.cuts = dict.fromkeys(names, 1)
        load(K_DN).wait()
        for event in backward_steps(z, lambda k: bufs[k], r):
            kind, k = (event or (None, None))[:2]
            if kind == K_WEIGHT:
                load(k).wait()
            if kind == K_GRAD and k in names and event[2] == int(k == K_DN):
                store(k).start()
                if k == K_CO:
                    store(K_UP).wait()
                    load(K_QKV).start()
        store(K_KV).wait()
        store(K_QKV).wait()
        load(K_KV).start()
        for event in pool_steps(z, lambda k: bufs[k], r):
            if event:
                load(K_KV).wait()
        for k in names:
            if k not in (K_UP, K_KV, K_QKV):
                store(k).wait()
        for i in (z.MB * 2 - 2, z.MB * 2 - 1):
            pool_copy(i).wait()
    V = pl.BlockSpec(memory_space=pltpu.VMEM)
    A = pl.BlockSpec(memory_space=pl.ANY)
    D = pltpu.SemaphoreType.DMA
    res = pl.pallas_call(kernel, name="layer_backward", out_shape=[S(shapes[k], BF) for k in names] + list(outs.values()),
        in_specs=[A] * len(names) + [A if k == K_SLOPE else V for k in ins] + [V] * 2, out_specs=[A] * (len(names) + 1) + [V] * 2,
        scratch_shapes=[D((len(names),)), D((len(names),)), D((2,)), D((2,))] + [pltpu.VMEM(shapes[k], BF) for k in kept]
            + [pltpu.VMEM(*v) for v in local.values()],
        compiler_params=pltpu.CompilerParams(vmem_limit_bytes=63 * MIB))(*[weights[k] for k in names], *saved.values(), wanted, times)
    return dict(zip(names, res)), dict(zip(outs, res[len(names):]))


MESH = pl.DeviceIdType.MESH

def when(pred, fn):
    if pred is None: fn()
    else: pl.when(pred)(fn)

def both(a, b):
    if a is None: return b
    if b is None: return a
    return jnp.logical_and(a, b)

class Place:
    def __init__(self, nz):
        dp, fs = lax.axis_index(K_DP), lax.axis_index(K_FSDP)
        self.nz = nz
        self.y, self.x = dp // 2, lax.rem(dp, 2)
        self.z, self.c = fs // 2, lax.rem(fs, 2)
        y, x, z, c = self.y, self.x, self.z, self.c
        self.y1, self.x1 = y + c * (1 - 2 * y), x + (1 - c) * (1 - 2 * x)
        self.y2, self.x2 = y + (1 - c) * (1 - 2 * y), x + c * (1 - 2 * x)
        self.yo, self.xo = 1 - y, 1 - x
        self.first = {K_DP: self.y1 * 2 + self.x1, K_FSDP: fs}
        self.second = {K_DP: self.y2 * 2 + self.x2, K_FSDP: fs}
        self.pair = {K_DP: dp, K_FSDP: z * 2 + 1 - c}
        self.up = {K_DP: dp, K_FSDP: fs + 2}
        self.down = {K_DP: dp, K_FSDP: fs - 2}
        self.has_up, self.has_down = z < nz - 1, z > 0

    def barrier(self):
        bar = pltpu.get_barrier_semaphore()
        ways = [(None, self.pair), (None, self.first), (None, self.second), (self.has_up, self.up), (self.has_down, self.down)]
        for pred, dev in ways:
            when(pred, lambda dev=dev: pl.semaphore_signal(bar, inc=1, device_id=dev, device_id_type=MESH))
        pl.semaphore_wait(bar, 3 + jnp.minimum(self.z, 1) + jnp.minimum(self.nz - 1 - self.z, 1))

class Gather:
    def __init__(self, at, block, out, sems, line_only=False):
        self.at, self.block, self.out, self.line_only = at, block, out, line_only
        self.zs, self.zr, self.ps, self.pr, self.own = sems
        self.late = []

    def cell(self, z, c):
        p = self.at
        return self.out.at[:, z, c] if self.line_only else self.out.at[p.y, p.x, z, c]
    def line(self, y, x, c):
        return self.out.at[:, :, c] if self.line_only else self.out.at[y, x, :, c]
    def copy(self, src, dst, s, r, dev):
        return pltpu.make_async_remote_copy(src_ref=src, dst_ref=dst, send_sem=s, recv_sem=r, device_id=dev, device_id_type=MESH)
    def send(self, pred, src, dst, s, r, dev):
        def go():
            self.copy(src, dst, s, r, dev).start()
        when(pred, go)
        def done():
            self.copy(src, dst, s, r, dev).wait_send()
        self.late.append((pred, done))
    def arrived(self, pred, ref, s, r):
        when(pred, lambda: self.copy(ref, ref, s, r, self.at.pair).wait_recv())

    def across(self, pred, ref, block=None):
        p = self.at
        src = ref if block is None else block
        if not self.line_only:
            for k, dev in ((4, p.first), (5, p.second)):
                when(pred, lambda k=k, dev=dev: self.copy(src, ref, self.ps.at[k], self.pr.at[k], dev).start())
    def start(self):
        p = self.at
        mine = self.cell(p.z, p.c)
        self.send(p.has_up, self.block, mine, self.zs.at[0, 0], self.zr.at[0, 0], p.up)
        self.send(p.has_down, self.block, mine, self.zs.at[1, 0], self.zr.at[1, 0], p.down)
        self.across(None, mine, self.block)
        pltpu.make_async_copy(self.block, mine, self.own).start()
    def hop(self, j):
        p = self.at
        for way, pred, more, ref, dev in ((0, p.z >= j, p.has_up, self.cell(p.z - j, p.c), p.up),
                                          (1, p.z < p.nz - j, p.has_down, self.cell(p.z + j, p.c), p.down)):
            self.arrived(pred, ref, self.zs.at[way, j - 1], self.zr.at[way, j - 1])
            if j < p.nz - 1:
                self.send(both(pred, more), ref, ref, self.zs.at[way, j], self.zr.at[way, j], dev)
            self.across(pred, ref)
    def z_done(self):
        p = self.at
        pltpu.make_async_copy(self.block, self.cell(p.z, p.c), self.own).wait()
        mine = self.line(p.y, p.x, p.c)
        self.send(None, mine, mine, self.ps.at[0], self.pr.at[0], p.pair)
        if not self.line_only:
            for k in (4, 5):
                self.late.append((None, lambda k=k: self.copy(mine, mine, self.ps.at[k], self.pr.at[k], p.pair).wait_send()))
    def after_first(self):
        p = self.at
        if self.line_only: return
        got = self.line(p.y1, p.x1, p.c)
        self.arrived(None, got, self.ps.at[4], self.pr.at[4])
        self.send(None, got, got, self.ps.at[6], self.pr.at[6], p.second)
        self.send(None, got, got, self.ps.at[1], self.pr.at[1], p.pair)
    def after_second(self):
        p = self.at
        if self.line_only: return
        for k, (y, x) in enumerate(((p.y2, p.x2), (p.yo, p.xo))):
            got = self.line(y, x, p.c)
            self.arrived(None, got, self.ps.at[5 + k], self.pr.at[5 + k])
            self.send(None, got, got, self.ps.at[2 + k], self.pr.at[2 + k], p.pair)
    def whole(self):
        p = self.at
        lines = [(p.y, p.x)] if self.line_only else [(p.y, p.x), (p.y2, p.x2), (p.y1, p.x1), (p.yo, p.xo)]
        for k, (y, x) in enumerate(lines):
            self.arrived(None, self.line(y, x, 1 - p.c), self.ps.at[k], self.pr.at[k])
    def drain(self):
        for pred, done in self.late:
            when(pred, done)

def sem_shapes(n, nz):
    D = pltpu.SemaphoreType.DMA
    return [D((n, 2, nz)), D((n, 2, nz)), D((n, 8)), D((n, 8)), D((n,))]


def pad16(r):
    return (r + 15) // 16 * 16


PIECES = ((K_SMALL, 0), (K_KV, 0), (K_TOK, 0), (K_KV, 1), (K_TOK, 1), (K_QKV, 0), (K_QKV, 1), (K_QKV, 2), (K_AO, 0), (K_CT, 0), (K_CQ, 0),
          (K_CO, 0), (K_CT, 1), (K_UP, 0), (K_UP, 1), (K_UP, 2), (K_UP, 3), (K_DN, 0), (K_DN, 1))
lines_only = (K_TOK, K_CT)
hop_lag, first_lag, second_lag, whole_lag, send_ahead, units_per_step = 0, 3, 4, 5, 2, 4


def piece(ref, name, c):
    cut = sum(k == name for k, _ in PIECES)
    if cut == 1:
        return ref
    if name in lines_only:
        return ref.at[c:c + 1]
    lead = (slice(None),) * (len(ref.shape) - 2)
    if name == K_DN:
        tiles = ref.shape[-2] // 16
        return ref.at[lead + (slice(tiles * c // cut * 16, tiles * (c + 1) // cut * 16),)]
    cols = ref.shape[-1] // cut
    return ref.at[lead + (slice(None), slice(c * cols, (c + 1) * cols))]


def forward_gather(z, arrays, wanted, times, pool, nz):
    names = list(arrays)
    S = jax.ShapeDtypeStruct
    whole, stages = {}, []
    for k, b in arrays.items():
        if k in lines_only:
            whole[k] = S((b.shape[0], nz, 2) + b.shape[1:], b.dtype)
            stages.append(pltpu.VMEM(b.shape, b.dtype))
        else:
            r = pad16(b.shape[0])
            whole[k] = S((2, 2, nz, 2, r, b.shape[1]), b.dtype)
            stages.append(pltpu.VMEM((r, b.shape[1]), b.dtype))
    saved = {**saved_shapes(z), K_BACK_Y: S((z.MB, z.stream, z.width), BF)}
    share = {K_UP: K_QKV, K_CT: K_TOK}
    room = {k: whole[k] for k in names if k not in share}
    room[K_QKV] = whole[K_UP]
    count = len(PIECES)

    def kernel(*refs):
        refs = list(refs)
        take = lambda k: [refs.pop(0) for _ in range(k)]
        blocks = dict(zip(names, take(len(names))))
        r = Refs([K_WANTED, K_TIMES, K_POOL], take(3))
        landed = dict(zip(names, take(len(names))))
        kept = dict(zip(saved, take(len(saved))))
        stage = dict(zip(names, take(len(names))))
        r.__dict__.update(zip(saved, take(len(saved))))
        bufs = dict(zip(room, take(len(room))))
        r.bias, r.upb, r.sp, loads, saves = take(5)
        sems = take(5)
        at = Place(nz)
        for k in names:
            b, s = blocks[k], stage[k]
            if s.shape == b.shape:
                s[...] = b[...]
            else:
                s[...] = jnp.zeros(s.shape, s.dtype)
                s[:b.shape[0], :] = b[...]
        at.barrier()
        gs = [Gather(at, piece(stage[k], k, c), piece(landed[k], k, c), [s.at[j] for s in sems], k in lines_only)
              for j, (k, c) in enumerate(PIECES)]

        def save(k):
            pltpu.make_async_copy(getattr(r, k), kept[k], saves.at[list(saved).index(k)]).start()
        r.save = save
        def buffer(k):
            if k in (K_QKV, K_UP):
                return bufs[K_QKV].at[:, :, :, :, :, :whole[k].shape[-1]]
            return bufs[share.get(k, k)]
        def load(j):
            k, c = PIECES[j]
            return pltpu.make_async_copy(piece(landed[k], k, c), piece(buffer(k), k, c), loads.at[j])
        def ready(k):
            b = bufs[share.get(k, k)]
            if k in lines_only:
                return b.reshape(z.MB, z.stream, z.width)
            flat = b.reshape(GROUPS * b.shape[-2], b.shape[-1])
            return flat.at[:, :whole[k].shape[-1]] if k in (K_QKV, K_UP) else flat

        there, started, waited = set(), set(), set()
        free = set(room)
        work = forward_steps(z, ready, r)
        state = {K_NEED: next(work), K_DONE: False}
        def start_loads():
            for j in sorted(there - started):
                if PIECES[j][0] in free:
                    load(j).start()
                    started.add(j)
        def advance(units):
            while units and not state[K_DONE]:
                need = state[K_NEED]
                if need:
                    if need == K_AO:
                        free.add(K_UP)
                    if need == K_QKV:
                        free.add(K_CT)
                    start_loads()
                    ask = {j for j, (k, c) in enumerate(PIECES) if k == need or k + str(c) == need}
                    if not ask <= started:
                        return
                    for j in sorted(ask - waited):
                        load(j).wait()
                    waited.update(ask)
                try:
                    state[K_NEED] = next(work)
                except StopIteration:
                    state[K_DONE] = True
                units -= 1

        for g in gs[:send_ahead]:
            g.start()
        for t in range(count + whole_lag):
            def stage_of(lag):
                return gs[t - lag] if 0 <= t - lag < count else None
            if t + send_ahead < count:
                gs[t + send_ahead].start()
            for j in range(1, nz):
                if g := stage_of(j - 1):
                    g.hop(j)
            if g := stage_of(nz - 2):
                g.z_done()
            if g := stage_of(first_lag):
                g.after_first()
            if g := stage_of(second_lag):
                g.after_second()
            if g := stage_of(whole_lag):
                g.whole()
                there.add(t - whole_lag)
                start_loads()
            advance(units_per_step if t < count + whole_lag - 1 else 1 << 20)
        for g in gs:
            g.drain()
        for i, k in enumerate(saved):
            pltpu.make_async_copy(getattr(r, k), kept[k], saves.at[i]).wait()

    V = pl.BlockSpec(memory_space=pltpu.VMEM)
    A = pl.BlockSpec(memory_space=pl.ANY)
    D = pltpu.SemaphoreType.DMA
    got = pl.pallas_call(kernel, name="gather_forward", out_shape=list(whole.values()) + list(saved.values()),
        in_specs=[V] * (len(names) + 3), out_specs=[A] * (len(names) + len(saved)),
        scratch_shapes=stages + [pltpu.VMEM(s.shape, s.dtype) for s in saved.values()] + [pltpu.VMEM(s.shape, s.dtype) for s in room.values()]
            + [pltpu.VMEM((HEADS, z.length, z.length), F32), pltpu.VMEM((1, z.ff), F32), pltpu.VMEM((z.width, z.wide), BF), D((count,)), D((len(saved),))] + sem_shapes(count, nz),
        compiler_params=pltpu.CompilerParams(collective_id=1, has_side_effects=True, vmem_limit_bytes=63 * MIB))(*arrays.values(), wanted, times, pool)
    flat = lambda k, v: v.reshape(-1, v.shape[-1])
    return {k: flat(k, v) for k, v in zip(names, got) if k in WEIGHTS}, dict(zip(saved, got[len(names):]))


CUTS = {K_DN: 2, K_UP: 4, K_CO: 1, K_KV: 2, K_CQ: 1, K_AO: 1, K_QKV: 6}
SUMS = tuple((k, c) for k in (K_Y, K_DN, K_UP, K_CO, K_KV, K_CQ, K_AO, K_X, K_SMALL, K_QKV) for c in range(CUTS.get(k, 1)))
early_lags, late_lags, late_pieces = (1, 3, 5, 7), (1, 2, 3, 4), 4


def lags_of(i, nz):
    pair, second, first, along = early_lags if i < len(SUMS) - late_pieces else late_lags
    return {K_PAIR: pair, K_SECOND: second, K_FIRST: first, **{h: along + h - 1 for h in range(1, nz)}, K_FINISH: along + nz - 1}


class Sum:
    def __init__(self, at, held, landing, out, sems, line_only, stages):
        self.at, self.held, self.out, self.line_only, self.stages = at, held, out, line_only, stages
        if line_only:
            self.rc, self.ru, self.rd = landing
        else:
            self.rc, self.r2, self.r1, self.ru, self.rd = landing
        self.ps, self.pr, self.us, self.ur, self.ds, self.dr = sems
        self.late = []
    def copy(self, src, dst, s, r, dev):
        return pltpu.make_async_remote_copy(src_ref=src, dst_ref=dst, send_sem=s, recv_sem=r, device_id=dev, device_id_type=MESH)
    def send(self, pred, src, dst, s, r, dev):
        when(pred, lambda: self.copy(src, dst, s, r, dev).start())
        self.late.append((pred, lambda: self.copy(src, dst, s, r, dev).wait_send()))
    def fetch(self, pred, ref, s, r):
        stage, sem = self.stages.room(ref)
        def go():
            self.copy(ref, ref, s, r, self.at.pair).wait_recv()
            pltpu.make_async_copy(ref, stage, sem).start()
        when(pred, go)
        def add(mine):
            def body():
                pltpu.make_async_copy(ref, stage, sem).wait()
                mine[...] = mine[...] + stage[...]
            when(pred, body)
        return add
    def line(self, y, x):
        return self.held.at[y, x, :, self.at.c]
    def cell(self, z):
        return self.held.at[:, z, self.at.c] if self.line_only else self.held.at[self.at.y, self.at.x, z, self.at.c]
    def start(self):
        p = self.at
        other = self.held.at[:, :, 1 - p.c] if self.line_only else self.held.at[:, :, :, 1 - p.c]
        self.send(None, other, self.rc, self.ps.at[0], self.pr.at[0], p.pair)
    def after_pair(self):
        p = self.at
        if self.line_only:
            add = self.fetch(None, self.rc, self.ps.at[0], self.pr.at[0])
            return [lambda: add(self.held.at[:, :, p.c])]
        stage, sem = self.stages.room(self.rc)
        self.copy(self.rc, self.rc, self.ps.at[0], self.pr.at[0], p.pair).wait_recv()
        fetch = pltpu.make_async_copy(self.rc, stage, sem)
        fetch.start()
        def adds():
            fetch.wait()
            def plus(y, x):
                mine = self.line(y, x)
                mine[...] = mine[...] + stage[y, x]
            for k, (y, x) in enumerate(((p.y2, p.x2), (p.yo, p.xo))):
                plus(y, x)
                self.send(None, self.line(y, x), self.r2.at[k], self.ps.at[1 + k], self.pr.at[1 + k], p.second)
            plus(p.y1, p.x1)
            plus(p.y, p.x)
        return [adds]
    def after_second(self):
        p = self.at
        if self.line_only:
            return []
        far = self.fetch(None, self.r2.at[1], self.ps.at[2], self.pr.at[2])
        near = self.fetch(None, self.r2.at[0], self.ps.at[1], self.pr.at[1])
        def adds():
            far(self.line(p.y1, p.x1))
            self.send(None, self.line(p.y1, p.x1), self.r1, self.ps.at[3], self.pr.at[3], p.first)
            near(self.line(p.y, p.x))
        return [adds]
    def after_first(self):
        if self.line_only:
            return []
        add = self.fetch(None, self.r1, self.ps.at[3], self.pr.at[3])
        return [lambda: add(self.line(self.at.y, self.at.x))]
    def z_step(self, h):
        p, nz = self.at, self.at.nz
        todo = []
        for j in range(nz - h, 0, -1):
            for here, goal, land, s, r, dev in ((p.z == h - 1, h - 1 + j, self.ru, self.us, self.ur, p.up),
                                                (p.z == nz - h, nz - h - j, self.rd, self.ds, self.dr, p.down)):
                add = self.fetch(here, land.at[j], s.at[j + 1], r.at[j]) if h > 1 else None
                def go(add=add, here=here, goal=goal, land=land, s=s, r=r, dev=dev, j=j):
                    if add:
                        add(self.cell(goal))
                    self.send(here, self.cell(goal), land.at[j - 1], s.at[j], r.at[j - 1], dev)
                todo.append(go)
        return todo
    def finish(self):
        p = self.at
        up = self.fetch(p.has_down, self.ru.at[0], self.us.at[1], self.ur.at[0])
        down = self.fetch(p.has_up, self.rd.at[0], self.ds.at[1], self.dr.at[0])
        def go():
            mine = self.cell(p.z)
            up(mine)
            down(mine)
            if self.line_only:
                self.out[...] = mine[...]
            else:
                self.out[...] = mine[...][:self.out.shape[0]].astype(self.out.dtype)
        return [go]
    def drain(self):
        for pred, done in self.late:
            when(pred, done)


class Stages:
    def __init__(self, pools, sems):
        self.pools, self.sems = pools, sems
        self.reset()
    def reset(self):
        self.used, self.count = {}, 0
    def room(self, ref):
        lead = ref.shape[:-1]
        n = 1
        for k in lead:
            n *= k
        key = (ref.shape[-1], jnp.dtype(ref.dtype).name)
        off = self.used.get(key, 0)
        self.used[key] = off + n
        sem = self.sems.at[self.count]
        self.count += 1
        return self.pools[key].at[off:off + n].reshape(ref.shape), sem


def landing_shapes(shape, line_only, nz):
    if line_only:
        m, _, _, r, n = shape
        return [(m, nz, r, n), (nz - 1, m, r, n), (nz - 1, m, r, n)]
    r, n = shape[-2:]
    return [(2, 2, nz, r, n), (2, nz, r, n), (nz, r, n), (nz - 1, r, n), (nz - 1, r, n)]


def sum_piece_shape(whole, name, c):
    cut = sum(k == name for k, _ in SUMS)
    r, n = whole[-2:]
    rows, cols = slice(0, r), slice(0, n)
    if name == K_DN:
        rows = slice(r // 16 * c // cut * 16, r // 16 * (c + 1) // cut * 16)
    elif cut > 1:
        cols = slice(n // cut * c, n // cut * (c + 1))
    return whole[:-2] + (rows.stop - rows.start, cols.stop - cols.start), rows, cols


def backward_scatter(z, weights, saved, back_y, wanted, times, shards, nz):
    names = list(WEIGHTS)
    shapes = weight_shapes(z)
    S = jax.ShapeDtypeStruct
    tok = z.length // 2
    blocked = {k: (2, 2, nz, 2, shapes[k][0] // GROUPS, shapes[k][1]) for k in names}
    blocked[K_SMALL] = (2, 2, nz, 2, 8, 128)
    blocked[K_Y] = blocked[K_X] = (z.MB, nz, 2, tok, z.width)
    kinds = {k: F32 if k == K_SMALL else BF for k in blocked}
    lines = (K_Y, K_X)
    placed = [sum_piece_shape(blocked[k], k, c) for k, c in SUMS]
    landings = [S(s, kinds[k]) for (k, c), (shape, _, _) in zip(SUMS, placed) for s in landing_shapes(shape, k in lines, nz)]
    outs = {K_POOL_GRAD: S((z.MB * z.keys, z.width), F32)}
    for k in names:
        outs[k] = S(shards[k].shape, F32)
    outs.update(small=S((8, 128), F32), y=S((z.MB, tok, z.width), BF), x=S((z.MB, tok, z.width), BF))
    part = z.keys // 2
    share = {K_H1: K_H2, K_X: K_H2, K_N2: K_N3, K_N1: K_N3, K_A: K_C, K_JOIN: K_GL, K_PS: K_PC}
    after = {(K_TILE, 0): (K_GL,), (K_TILE, 1): ("w up",), (K_TILE, 2): (K_SPT, K_VEC, K_H2, K_N3), (K_TILE, 3): (K_C, "w co"),
             (K_GRAD, K_DN, CUTS[K_DN] - 1): (K_JOIN, K_CQ, K_CKV), (K_GRAD, K_UP, 0): (K_PC, K_EP),
             (K_GRAD, K_UP, CUTS[K_UP] - 1): (K_H1, K_N2, "w cq"), (K_GRAD, K_CO, 0): (K_A, "w ao", "w qkv"),
             (K_GRAD, K_KV, 0): (K_PS,), (K_GRAD, K_CQ, 0): (K_X, K_N1)}
    room = {k: saved[k] for k in saved if k not in share and k != K_SLOPE}
    local = {K_DU: ((z.rows, z.ff), BF), K_UPB_SUM: ((1, z.ff), F32), K_DH: ((z.rows, z.width), F32), K_E: ((z.rows, z.width), BF),
             K_DC: ((z.rows, z.att), BF), K_TABLE: ((z.length, HEADS * z.length), F32),
             K_TILES: ((2, max(z.rows, part), max(z.ff // 4, z.width)), F32), K_SMALL_GRAD: ((2, 2, nz, 2, 8, 128), F32), "line": ((z.MB, nz, 2, tok, z.width), BF)}
    steps = max(i + max(lags_of(i, nz).values()) for i in range(len(SUMS))) + 1
    plan = {}
    most = [0]

    def schedule(t):
        return [(i, name) for i in range(len(SUMS)) for name, lag in lags_of(i, nz).items() if i + lag == t]
    def asks(i, name):
        (k, c), (shape, _, _) = SUMS[i], placed[i]
        got = landing_shapes(shape, k in lines, nz)
        if name == K_PAIR:
            return [got[0]]
        if name in (K_SECOND, K_FIRST):
            return [] if k in lines else [got[1][1:]] * 2 if name == K_SECOND else [got[2]]
        z_block = got[-1][1:]
        return [z_block] * 2 if name == K_FINISH else [z_block] * (2 * (nz - name) if name > 1 else 0)
    for t in range(steps):
        need, count = {}, 0
        for i, name in schedule(t):
            for s in asks(i, name):
                n = 1
                for d in s[:-1]:
                    n *= d
                key = (s[-1], jnp.dtype(kinds[SUMS[i][0]]).name)
                need[key] = need.get(key, 0) + n
                count += 1
        for key, n in need.items():
            plan[key] = max(plan.get(key, 0), n)
        most[0] = max(most[0], count)

    def kernel(*refs):
        refs = list(refs)
        take = lambda k: [refs.pop(0) for _ in range(k)]
        stored = dict(zip(names, take(len(names))))
        kept = dict(zip(saved, take(len(saved))))
        y_in = take(1)[0]
        r = Refs([K_WANTED, K_TIMES], take(2))
        result = dict(zip(outs, take(len(outs))))
        land = take(len(landings))
        bufs = dict(zip(names, take(len(names))))
        slots = dict(zip(room, take(len(room))))
        r.__dict__.update(zip(local, take(len(local))))
        pools = dict(zip(plan, take(len(plan))))
        wsem, ssem, tsem, psem, ysem, dsem, stage_sem = take(7)
        sems = take(6)
        at = Place(nz)
        def slot(k):
            ref = slots[share.get(k, k)]
            if k == K_JOIN:
                return ref.at[:, :3 * z.att]
            if k == K_PS:
                return ref.reshape(z.MB, HEADS // 2, 2 * z.win * z.pool, NL).at[:, :, :2 * z.length]
            return ref
        for k in saved:
            if k != K_SLOPE:
                setattr(r, k, slot(k))
        small_held = r.small_grad
        r.small_grad = small_held.reshape(GROUPS * 8, 128)
        r.dq, r.dcq, r.dckv = r.join, r.cq, r.ckv
        r.back_x = r.line.reshape(z.MB, z.stream, z.width)
        step = z.ff // 4
        slope_tiles, r.pool_tiles = r.tiles.at[:, :z.rows, :step], r.tiles.at[:, :part, :z.width]
        r.pool_hi, r.pool_lo = r.ep, bufs[K_UP].reshape(shapes[K_UP]).at[:z.MB * z.keys, 2 * z.att:2 * z.att + z.wide]
        held = {**bufs, K_SMALL: small_held, K_Y: r.line, K_X: r.line}
        load = lambda k: pltpu.make_async_copy(stored[k], bufs[k], wsem.at[names.index(k)])
        get = lambda k: pltpu.make_async_copy(kept[k], slot(k), ssem.at[list(saved).index(k)])
        slope = lambda i: pltpu.make_async_copy(kept[K_SLOPE].at[:, i * step:(i + 1) * step], slope_tiles.at[i % 2], tsem.at[i % 2])
        y_load = pltpu.make_async_copy(y_in, r.line, ysem)
        dn_load = lambda i: pltpu.make_async_copy(stored[K_DN].at[i // 2, i % 2], bufs[K_DN].at[i // 2, i % 2], dsem.at[i])
        get(K_CT).start()
        for i in range(4):
            dn_load(i).start()
            if i < 2:
                slope(i).start()
        y_load.start()
        begin = lambda k: load(k[2:]).start() if k[:2] == "w " else get(k).start()
        at.barrier()
        def slope_tile(i):
            slope(i).wait()
            return slope_tiles[i % 2]
        pool_copy = lambda i: pltpu.make_async_copy(r.pool_tiles.at[i % 2], result[K_POOL_GRAD].at[i * part:(i + 1) * part], psem.at[i % 2])
        def put_pool(i, value):
            if i >= 2:
                pool_copy(i - 2).wait()
            r.pool_tiles[i % 2] = value
            pool_copy(i).start()
        r.slope_tile, r.put_pool, r.cuts = slope_tile, put_pool, CUTS
        ready = lambda k: bufs[k].reshape(shapes[k])

        stages = Stages(pools, stage_sem)
        sums, spot = [], 0
        for i, ((k, c), (shape, rows, cols)) in enumerate(zip(SUMS, placed)):
            n = len(landing_shapes(shape, k in lines, nz))
            out = result[k]
            if k in names:
                lead = (slice(None),) * 4
                part_of = held[k].at[lead + (rows, cols)]
                last = min(rows.stop, out.shape[0])
                out = out.at[rows.start:last, cols]
            else:
                part_of = held[k]
            sums.append(Sum(at, part_of, land[spot:spot + n], out, [s.at[i] for s in sems], k in lines, stages))
            spot += n

        work = backward_steps(z, ready, r)
        made = set()
        def until(piece):
            if piece == (K_Y, 0):
                y_load.wait()
                return
            if piece == (K_X, 0):
                sums[0].drain()
                sums[0].late = []
            while piece not in made:
                event = next(work)
                kind = event and event[0]
                if kind == K_WEIGHT:
                    load(event[1]).wait()
                if kind == K_SAVED:
                    for k in event[1]:
                        get(k).wait()
                if kind == K_GRAD:
                    made.add(event[1:])
                if kind == K_TILE:
                    i = event[1]
                    dn_load(i).wait()
                    if 1 <= i <= 2:
                        slope(i + 1).start()
                for k in after.get(event, ()):
                    begin(k)

        spare = bufs[K_UP].at[:, :, :, :, :, :shapes[K_KV][1]]
        again = pltpu.make_async_copy(stored[K_KV], spare, wsem.at[names.index(K_KV)])
        pool_work = pool_steps(z, lambda k: bufs[K_UP].reshape(shapes[K_UP]).at[:, :shapes[K_KV][1]], r)
        def idle():
            event = next(pool_work, K_DONE)
            if event and event != K_DONE:
                again.wait()
                event = next(pool_work)
            return event != K_DONE

        for t in range(steps):
            if t < len(SUMS):
                until(SUMS[t])
                sums[t].start()
                if t + 1 == len(SUMS):
                    for i, (k, _) in enumerate(SUMS):
                        if k == K_UP:
                            sums[i].drain()
                            sums[i].late = []
                    again.start()
            for part_of_step in ((K_PAIR, K_SECOND, K_FIRST), None):
                todo = []
                stages.reset()
                for i, name in schedule(t):
                    s = sums[i]
                    if (part_of_step is None) == (name in (K_PAIR, K_SECOND, K_FIRST)):
                        continue
                    if name == K_FINISH:
                        todo += s.finish()
                    elif name == K_PAIR:
                        todo += s.after_pair()
                    elif name == K_SECOND:
                        todo += s.after_second()
                    elif name == K_FIRST:
                        todo += s.after_first()
                    else:
                        todo += s.z_step(name)
                if t >= len(SUMS):
                    idle()
                for go in todo:
                    go()
        while idle():
            pass
        for s in sums:
            s.drain()
        for i in (z.MB * 2 - 2, z.MB * 2 - 1):
            pool_copy(i).wait()

    V = pl.BlockSpec(memory_space=pltpu.VMEM)
    A = pl.BlockSpec(memory_space=pl.ANY)
    D = pltpu.SemaphoreType.DMA
    n = len(SUMS)
    got = pl.pallas_call(kernel, name="backward_scatter", out_shape=list(outs.values()) + landings,
        in_specs=[A] * (len(names) + len(saved) + 1) + [V] * 2,
        out_specs=[A] + [V] * (len(outs) - 1) + [A] * len(landings),
        scratch_shapes=[pltpu.VMEM(blocked[k], BF) for k in names] + [pltpu.VMEM(v.shape, v.dtype) for v in room.values()]
            + [pltpu.VMEM(*v) for v in local.values()] + [pltpu.VMEM((rows, key[0]), jnp.dtype(key[1])) for key, rows in plan.items()]
            + [D((len(names),)), D((len(saved),)), D((2,)), D((2,)), D, D((4,)), D((most[0],))]
            + [D((n, 4)), D((n, 4)), D((n, nz + 1)), D((n, nz + 1)), D((n, nz + 1)), D((n, nz + 1))],
        compiler_params=pltpu.CompilerParams(collective_id=2, has_side_effects=True, vmem_limit_bytes=63 * MIB),
    )(*[weights[k].reshape(blocked[k]) for k in names], *saved.values(), back_y.reshape(blocked[K_Y]), wanted, times)
    return dict(zip(outs, got))


def vectors(norm1_gain, norm2_gain, norm3_gain, attn_out_bias, cca_out_bias, ffw_down_bias, rel_table, ffw_up_bias):
    return [norm1_gain, norm2_gain, norm3_gain, attn_out_bias, cca_out_bias, ffw_down_bias, rel_table, ffw_up_bias]


def to_groups(v):
    small = v.shape[0] // GROUPS
    big = (small + 15) // 16 * 16
    return jnp.pad(v.reshape(GROUPS, small, -1), ((0, 0), (0, big - small), (0, 0))).reshape(GROUPS * big, -1)


def from_groups(v, rows):
    return v.reshape(GROUPS, v.shape[0] // GROUPS, -1)[:, :rows // GROUPS].reshape(rows, -1)


def body(tokens, cotangent, lengths, deal, pool, neighbour_ids, norm1_gain, attn_qkv, attn_out, attn_out_bias, rel_table,
         norm2_gain, cca_query, cca_kv, cca_out, cca_out_bias, norm3_gain, ffw_up, ffw_up_bias, ffw_down, ffw_down_bias):
    members, member = lax.axis_size(K_FSDP), lax.axis_index(K_FSDP)
    devices = members * lax.axis_size(K_DP)
    MB, tok_rows, width = tokens.shape
    length = 2 * tok_rows
    z = Sizes(MB, length, width, HEADS * HEAD_DIM, ffw_up.shape[1], pool.shape[1])
    z.stream = members * tok_rows
    shards = {K_QKV: attn_qkv, K_AO: attn_out, K_CQ: cca_query, K_KV: cca_kv, K_CO: cca_out, K_UP: ffw_up, K_DN: ffw_down}
    vecs = vectors(norm1_gain, norm2_gain, norm3_gain, attn_out_bias, cca_out_bias, ffw_down_bias, rel_table, ffw_up_bias)

    ids = jnp.arange(members, dtype=jnp.int32)
    lens, dealt = lengths[:, 0], deal[:, 0]
    starts = jnp.sum(jnp.where(ids[None, :, None] > ids[None, None, :], lens[:, None, :], 0), 2)
    mine = dealt == member
    own_start = jnp.sum(jnp.where(mine, starts, 0), 1)
    own_len = jnp.sum(jnp.where(mine, lens, 0), 1)
    place = jnp.arange(length, dtype=jnp.int32)
    wanted = jnp.where(place[None] < own_len[:, None], own_start[:, None] + place[None], -1).reshape(-1)
    wanted = jnp.broadcast_to(wanted[:, None], (MB * length, 128))
    spans = length // CH
    ids3 = neighbour_ids.reshape(MB, spans, K_NB)
    held = jnp.sum((ids3[..., None] == jnp.arange(z.pool, dtype=jnp.int32)).astype(F32), 2)
    row = jnp.arange(low_row, length, dtype=jnp.int32)
    in_span = ((row[:, None] - (CH - 1)) // CH == jnp.arange(spans, dtype=jnp.int32)) & (row[:, None] >= CH - 1)
    times = jnp.sum(jnp.where(in_span[None, :, :, None], held[:, None], 0.0), 2)
    times = jnp.broadcast_to(times[..., None], times.shape + (NL,)).reshape(MB, z.win, z.keys)
    neighbours = pool.reshape(MB * z.keys, width)

    direct = lax.axis_size(K_DP) == 4 and members % 2 == 0 and devices == GROUPS
    nz = members // 2
    if direct:
        packed = jnp.concatenate([jnp.pad(v[None], ((0, 0), (0, 128 - v.shape[0]))) for v in vecs] + [jnp.zeros((SMALLS - 8, 128), BF)], 0)
        weights, saved = forward_gather(z, {K_SMALL: packed, K_TOK: tokens, K_CT: cotangent, **shards}, wanted, times, neighbours, nz)
        back_y = saved.pop(K_BACK_Y)
        outs = backward_scatter(z, weights, saved, back_y, wanted, times, shards, nz)
        act, dx, small, mine = outs[K_Y], outs[K_X], outs[K_SMALL], outs
        parts = [small[i, :v.shape[0]] for i, v in enumerate(vecs)]
    else:
        whole = lambda v: lax.all_gather(v, (K_DP, K_FSDP), axis=0, tiled=True)
        rows = [jnp.pad(w, ((0, 0), (0, 128 - w.shape[1])))[:, None] for w in [whole(v).reshape(GROUPS, -1) for v in vecs]]
        packed = jnp.concatenate(rows + [jnp.zeros((GROUPS, SMALLS - 8, 128), BF)], 1).reshape(GROUPS * SMALLS, 128)
        gathered = {K_SMALL: packed, **{k: to_groups(whole(v)) for k, v in shards.items()},
                    K_TOK: lax.all_gather(tokens, K_FSDP, axis=1, tiled=True), K_CT: lax.all_gather(cotangent, K_FSDP, axis=1, tiled=True)}
        weights = {k: gathered[k] for k in WEIGHTS}
        saved = forward_plain(z, gathered, wanted, times, neighbours)
        back_y = saved.pop(K_BACK_Y)
        grads, outs = backward_plain(z, weights, saved, wanted, times)
        back_x, small = outs[K_BACK_X], outs[K_SMALL_GRAD]
        down = lambda v: lax.psum_scatter(v.astype(F32), (K_DP, K_FSDP), scatter_dimension=0, tiled=True)
        line = lambda v: lax.psum_scatter(v, K_FSDP, scatter_dimension=1, tiled=True)
        act, dx = line(back_y), line(back_x)
        mine = {k: down(from_groups(grads[k], shards[k].shape[0] * devices)) for k in shards}
        small = small.reshape(GROUPS, 8, 128)
        parts = [down(small[:, i, :v.shape[0] * devices // GROUPS].reshape(-1)) for i, v in enumerate(vecs)]
    g1, g2, g3, ba, bc, bd, rel, upb = parts
    return (act, dx, outs[K_POOL_GRAD].reshape(pool.shape), g1, mine[K_QKV], mine[K_AO], ba, rel, g2, mine[K_CQ], mine[K_KV],
            mine[K_CO], bc, g3, mine[K_UP], upb, mine[K_DN], bd)


def solution(mesh):
    everywhere = (K_DP, K_FSDP)
    rows, vec = P(everywhere, None), P(everywhere)
    slots = P(None, everywhere, None)
    return jax.shard_map(
        body,
        mesh=mesh,
        in_specs=(slots, slots, P(None, K_DP, None), P(None, K_DP, None), P(None, everywhere, None, None), slots,
                  vec, rows, rows, vec, vec, vec, rows, rows, rows, vec, vec, rows, vec, rows, vec),
        out_specs=(slots, slots, P(None, everywhere, None, None), vec, rows, rows, vec, vec, vec, rows, rows, rows, vec, vec,
                   rows, vec, rows, vec),
        check_vma=False,
    )
```

```python
from functools import partial

import jax
import jax.numpy as jnp
from jax import lax
from jax.experimental import pallas as pl
from jax.experimental.pallas import tpu as pltpu
from jax.sharding import PartitionSpec as P

K_0 = "0"
K_A = "a"
K_AO = "ao"
K_BACK_X = "back_x"
K_BACK_Y = "back_y"
K_C = "c"
K_CKV = "ckv"
K_CO = "co"
K_CQ = "cq"
K_CT = "ct"
K_DC = "dc"
K_DH = "dh"
K_DN = "dn"
K_DONE = "done"
K_DP = "dp"
K_DU = "du"
K_E = "e"
K_EP = "ep"
K_FINISH = "finish"
K_FIRST = "first"
K_FSDP = "fsdp"
K_GL = "gl"
K_GRAD = "grad"
K_H1 = "h1"
K_H2 = "h2"
K_JOIN = "join"
K_KV = "kv"
K_N1 = "n1"
K_N2 = "n2"
K_N3 = "n3"
K_NEED = "need"
K_PAIR = "pair"
K_PC = "pc"
K_POOL = "pool"
K_POOL_GRAD = "pool_grad"
K_PS = "ps"
K_QKV = "qkv"
K_SAVED = "saved"
K_SECOND = "second"
K_SLOPE = "slope"
K_SMALL = "small"
K_SMALL_GRAD = "small_grad"
K_SPT = "spt"
K_TABLE = "table"
K_TILE = "tile"
K_TILES = "tiles"
K_TIMES = "times"
K_TOK = "tok"
K_UP = "up"
K_UP0 = "up0"
K_UPB_SUM = "upb_sum"
K_VEC = "vec"
K_WANTED = "wanted"
K_WEIGHT = "weight"
K_X = "x"
K_Y = "y"
MIB = 1 << 20
F32, BF = jnp.float32, jnp.bfloat16
HEADS, HEAD_DIM, CH, NL, K_NB, NB = 16, 64, 64, 128, 2, 64
epsilon = 1e-06
masked_score = -1e30
tile = 512
unroll = 4
low_row = 48
GROUPS = 32
SMALLS = 16
G1, G2, G3, BA, BC, BD, REL, UPB = range(8)


def mm(a, b):
    return jnp.dot(a, b, preferred_element_type=F32)
def mm_tn(a, b):
    return lax.dot_general(a, b, (((0,), (0,)), ((), ())), preferred_element_type=F32)
def mm_nt(a, b):
    return lax.dot_general(a, b, (((1,), (1,)), ((), ())), preferred_element_type=F32)
def iota(shape, dim):
    return lax.broadcasted_iota(jnp.int32, shape, dim)
def onehot(cond):
    return jnp.where(cond, 1.0, 0.0).astype(BF)
def split2(v):
    hi = v.astype(BF)
    return hi, (v - hi.astype(F32)).astype(BF)
def columns(i, size):
    return pl.ds(pl.multiple_of(i * size, size), size)
def loop(count, body):
    def step(i, carry):
        body(i)
        return carry
    lax.fori_loop(0, count, step, 0)


def spread(width):
    small = width // GROUPS
    big = (small + 15) // 16 * 16
    row, col = iota((width, GROUPS * big), 0), iota((width, GROUPS * big), 1)
    return onehot((col // big == row // small) & (col % big == row % small))


def gather_up(width):
    small = width // GROUPS
    big = (small + 15) // 16 * 16
    row, col = iota((GROUPS * big, width), 1), iota((GROUPS * big, width), 0)
    return onehot((col // big == row // small) & (col % big == row % small))


def dense(v, back):
    hi, lo = split2(v)
    return mm(hi, back) + mm(lo, back)


def small_rows(packed, width):
    per = width // GROUPS
    put = onehot(iota((128, width), 0) == iota((128, width), 1) % per)
    placed = mm(packed, put)
    shape = (GROUPS * SMALLS, width)
    placed = jnp.where(iota(shape, 0) // SMALLS == iota(shape, 1) // per, placed, 0.0).astype(BF)
    take = onehot(iota((SMALLS, GROUPS * SMALLS), 1) % SMALLS == iota((SMALLS, GROUPS * SMALLS), 0))
    return mm(take, placed)


def table_rows(packed, length):
    per = NB * HEADS // GROUPS // HEADS
    width = length // NB
    take = onehot(iota((GROUPS, GROUPS * SMALLS), 1) == iota((GROUPS, GROUPS * SMALLS), 0) * SMALLS + REL)
    held = mm(take, packed).astype(BF)
    far = (length - iota((GROUPS, length), 1)) % length // width
    at = mm_tn(held, onehot(far // per == iota((GROUPS, length), 0)))
    which = (length - iota((HEADS, length), 1)) % length // width % per
    out = jnp.zeros((HEADS, length), F32)
    for k in range(per):
        out = jnp.where(which == k, at[k * HEADS:(k + 1) * HEADS], out)
    return out


def biases(rows, bias):
    length = bias.shape[1]
    below = iota((length, length), 0) >= iota((length, length), 1)
    for h in range(HEADS):
        wide = jnp.broadcast_to(rows[h:h + 1], (length, length))
        bias[h] = jnp.where(below, pltpu.roll(wide, 0, 1, stride=1, stride_axis=0), masked_score)


def rms(v):
    return lax.rsqrt(jnp.mean(v * v, -1, keepdims=True) + epsilon)


def norm(v, gain):
    return (v * rms(v) * gain).astype(BF)


def norm_back(v, gain, dn):
    r = rms(v)
    unit = v * r
    gained = dn * gain
    return r * (gained - unit * jnp.mean(gained * unit, -1, keepdims=True)), jnp.sum(dn * unit, 0, keepdims=True)


def halves(v):
    first = iota(v.shape, 1) < HEAD_DIM
    zero = jnp.zeros(v.shape, v.dtype)
    return jnp.concatenate([jnp.where(first, v, zero), jnp.where(first, zero, v)], 0)


def joined(v):
    n = v.shape[0] // 2
    return jnp.where(iota((n, v.shape[1]), 1) < HEAD_DIM, v[:n], v[n:])


def head_parts(count, parts, body):
    pairs = HEADS // 2
    total = count * pairs
    def step(i, carry):
        m, p = i // pairs, i % pairs
        body(m, p, p * 2 * HEAD_DIM)
        return carry
    for k in range(parts):
        lax.fori_loop(total * k // parts, total * (k + 1) // parts, step, 0, unroll=unroll)
        yield


class Sizes:
    def __init__(self, MB, length, width, att, ff, pool):
        self.MB, self.length, self.width, self.att, self.ff, self.pool = MB, length, width, att, ff, pool
        self.rows = MB * length
        self.win = length - low_row
        self.wide = GROUPS * ((width // GROUPS + 15) // 16 * 16)
        self.keys = pool * NL


def fwd_self(z, join, bias, ps, att):
    factor = HEAD_DIM ** -0.5
    def body(m, p, c):
        rows = pl.ds(pl.multiple_of(m * z.length, 128), z.length)
        at = lambda part: pl.ds(pl.multiple_of(part * z.att + c, 128), 128)
        q, k, v = join[rows, at(0)], join[rows, at(1)], join[rows, at(2)]
        s = mm_nt(halves(q), k) * factor + jnp.concatenate([bias[2 * p], bias[2 * p + 1]], 0)
        e = jnp.exp(s - jnp.max(s, -1, keepdims=True))
        soft = e * (1.0 / jnp.sum(e, -1, keepdims=True))
        ps[m, p] = soft
        att[rows, at(0)] = joined(mm(soft.astype(BF), v)).astype(BF)
    yield from head_parts(z.MB, 4, body)


def fwd_cross(z, cq, ckv, times, pc, c_out):
    factor = HEAD_DIM ** -0.5
    for m in range(z.MB):
        c_out[m * z.length:m * z.length + low_row] = jnp.zeros((low_row, z.att), BF)
    def body(m, p, c):
        rows = pl.ds(pl.multiple_of(m * z.length + low_row, 16), z.win)
        keys = pl.ds(pl.multiple_of(m * z.keys, 128), z.keys)
        at = lambda part: pl.ds(pl.multiple_of(part * z.att + c, 128), 128)
        q, k, v = cq[rows, at(0)], ckv[keys, at(0)], ckv[keys, at(1)]
        cnt = times[m]
        cnt = jnp.concatenate([cnt, cnt], 0)
        s = jnp.where(cnt > 0, mm_nt(halves(q), k) * factor, masked_score)
        e = jnp.exp(s - jnp.max(s, -1, keepdims=True))
        total = jnp.sum(e * cnt, -1, keepdims=True)
        soft = e * (1.0 / jnp.where(total > 0, total, 1.0))
        for k in range(z.keys // NL):
            pc[m, p, k] = soft[:, k * NL:(k + 1) * NL]
        c_out[rows, at(0)] = joined(mm((soft.astype(BF).astype(F32) * cnt).astype(BF), v)).astype(BF)
    yield from head_parts(z.MB, 4, body)


def gelu_parts(u):
    k = 0.7978845608028654
    t = jnp.tanh(k * (u + 0.044715 * u * u * u))
    half = 0.5 * (1.0 + t)
    return u * half, half + 0.5 * u * (1.0 - t * t) * k * (1.0 + 3 * 0.044715 * u * u)


def fwd_up(z, n3, up, upb, gl, slope, at):
    u = mm(n3[...], up[:, at]) + upb[:, at]
    value, d = gelu_parts(u)
    gl[:, at] = value.astype(BF)
    slope[:, at] = d


def project(left, weight, out, size=tile):
    for i in range(out.shape[1] // size):
        at = slice(i * size, (i + 1) * size)
        out[:, at] = mm(left[...], weight[:, at]).astype(out.dtype)
        yield


def project_nt(left, weight, out, size=tile):
    for i in range(out.shape[1] // size):
        at = slice(i * size, (i + 1) * size)
        out[:, at] = mm_nt(left[...], weight[at, :]).astype(out.dtype)
        yield


def outer(left, right, out, lo, hi, size=256):
    for i in range(out.shape[0] // size):
        at = slice(i * size, (i + 1) * size)
        out[at, lo:hi] = mm_tn(left[:, at], right[:, lo:hi]).astype(out.dtype)
        yield


def bwd_self(z, join, ps, da, dq, table_sum):
    factor = HEAD_DIM ** -0.5
    def body(m, p, c):
        rows = pl.ds(pl.multiple_of(m * z.length, 128), z.length)
        at = lambda part: pl.ds(pl.multiple_of(part * z.att + c, 128), 128)
        q, k, v = join[rows, at(0)], join[rows, at(1)], join[rows, at(2)]
        d = halves(da[rows, at(0)])
        soft = ps[m, p]
        dp = mm_nt(d, v)
        ds = (soft * (dp - jnp.sum(dp * soft, -1, keepdims=True))).astype(BF)
        dq[rows, at(0)] = (joined(mm(ds, k)) * factor).astype(BF)
        dq[rows, at(1)] = (mm_tn(ds, halves(q)) * factor).astype(BF)
        dq[rows, at(2)] = mm_tn(soft.astype(BF), d).astype(BF)
        wide = ds.astype(F32)
        for k in range(2):
            heads = pl.ds(pl.multiple_of((2 * p + k) * z.length, 128), z.length)
            table_sum[:, heads] += wide[k * z.length:(k + 1) * z.length]
    yield from head_parts(z.MB, 4, body)


def bwd_cross(z, cq, ckv, times, pc, dc, dcq, dckv):
    factor = HEAD_DIM ** -0.5
    for m in range(z.MB):
        dcq[m * z.length:m * z.length + low_row] = jnp.zeros((low_row, z.att), BF)
    def body(m, p, c):
        rows = pl.ds(pl.multiple_of(m * z.length + low_row, 16), z.win)
        keys = pl.ds(pl.multiple_of(m * z.keys, 128), z.keys)
        at = lambda part: pl.ds(pl.multiple_of(part * z.att + c, 128), 128)
        q, k, v = cq[rows, at(0)], ckv[keys, at(0)], ckv[keys, at(1)]
        d = halves(dc[rows, at(0)])
        cnt = times[m]
        cnt = jnp.concatenate([cnt, cnt], 0)
        soft = jnp.concatenate([pc[m, p, k] for k in range(z.keys // NL)], 1)
        dp = mm_nt(d, v)
        ds = (soft * (dp - jnp.sum(dp * soft * cnt, -1, keepdims=True))).astype(BF)
        ds = (ds.astype(F32) * cnt).astype(BF)
        pb = (soft.astype(BF).astype(F32) * cnt).astype(BF)
        dcq[rows, at(0)] = (joined(mm(ds, k)) * factor).astype(BF)
        dckv[keys, at(0)] = (mm_tn(ds, halves(q)) * factor).astype(BF)
        dckv[keys, at(1)] = mm_tn(pb, d).astype(BF)
    yield from head_parts(z.MB, 4, body)


def exact(a, b, dims):
    return lax.dot_general(a, b, (dims, ((), ())), precision=lax.Precision.HIGHEST, preferred_element_type=F32)


def table_grad(table_sum):
    length = table_sum.shape[0]
    flip = onehot(iota((length, length), 0) + iota((length, length), 1) == length - 1)
    hi, lo = split2(table_sum)
    flipped = mm(flip, hi) + mm(flip, lo)
    rows = []
    for h in range(HEADS):
        turned = pltpu.roll(flipped[:, h * length:(h + 1) * length], 0, 1, stride=1, stride_axis=0)
        rows.append(jnp.sum(turned, 0, keepdims=True))
    return jnp.concatenate(rows, 0)


WEIGHTS = (K_QKV, K_AO, K_CQ, K_KV, K_CO, K_UP, K_DN)


def forward_steps(z, ready, r):
    yield K_SMALL
    r.sp[...] = spread(z.width)
    r.spt[...] = gather_up(z.width)
    r.save(K_SPT)
    packed = ready(K_SMALL)[...]
    r.vec[...] = small_rows(packed, z.width)
    r.save(K_VEC)
    yield
    def upb(i):
        at = columns(i, tile)
        per = z.ff // GROUPS
        put = onehot(iota((128, tile), 0) == (iota((128, tile), 1) + i * tile) % per)
        placed = mm(packed, put)
        shape = (GROUPS * SMALLS, tile)
        mine = (iota(shape, 0) // SMALLS == (iota(shape, 1) + i * tile) // per) & (iota(shape, 0) % SMALLS == UPB)
        r.upb[:, at] = jnp.sum(jnp.where(mine, placed, 0.0), 0, keepdims=True)
    loop(z.ff // tile, upb)
    biases(table_rows(packed, z.length), r.bias)
    half = z.keys // 2
    for i in range(z.MB * 2):
        rows = slice(i * half, (i + 1) * half)
        r.ep[rows, :] = mm(r.pool[rows, :], r.sp[...]).astype(BF)
        yield
    r.save(K_EP)
    yield K_KV
    kv = ready(K_KV)
    yield from project(r.ep, kv, r.ckv, 256)
    r.save(K_CKV)
    yield K_TOK
    tok = ready(K_TOK)
    stream = tok.shape[1]
    for m in range(z.MB):
        rows = slice(m * z.length, (m + 1) * z.length)
        pick = onehot(r.wanted[rows, :1] == iota((z.length, stream), 1))
        r.x[rows] = mm(pick, tok[m])
    r.save(K_X)
    yield
    r.n1[...] = mm(norm(r.x[...], r.vec[G1:G1 + 1]), r.sp[...]).astype(BF)
    r.save(K_N1)
    yield K_QKV
    yield from project(r.n1, ready(K_QKV), r.join)
    r.save(K_JOIN)
    yield from fwd_self(z, r.join, r.bias, r.ps, r.a)
    r.save(K_PS)
    r.save(K_A)
    yield K_AO
    h1 = r.x[...] + (mm(r.a[...], ready(K_AO)[...]) + r.vec[BA:BA + 1])
    r.h1[...] = h1
    r.save(K_H1)
    r.n2[...] = mm(norm(h1, r.vec[G2:G2 + 1]), r.sp[...]).astype(BF)
    r.save(K_N2)
    yield K_CQ
    yield from project(r.n2, ready(K_CQ), r.cq)
    r.save(K_CQ)
    yield from fwd_cross(z, r.cq, r.ckv, r.times, r.pc, r.c)
    r.save(K_PC)
    r.save(K_C)
    yield K_CO
    h2 = r.h1[...] + (mm(r.c[...], ready(K_CO)[...]) + r.vec[BC:BC + 1])
    r.h2[...] = h2
    r.save(K_H2)
    r.n3[...] = mm(norm(h2, r.vec[G3:G3 + 1]), r.sp[...]).astype(BF)
    r.save(K_N3)
    yield K_CT
    ct = ready(K_CT)
    for m in range(z.MB):
        rows = slice(m * z.length, (m + 1) * z.length)
        pick = onehot(r.wanted[rows, :1] == iota((z.length, stream), 1))
        r.ct[rows] = mm(pick, ct[m]).astype(BF)
    r.save(K_CT)
    step = z.ff // 4
    for i in range(4):
        yield K_UP + str(i)
        cut = (step // 2 + 127) // 128 * 128
        for lo, hi in ((0, cut), (cut, step)):
            fwd_up(z, r.n3, ready(K_UP), r.upb, r.gl, r.slope, slice(i * step + lo, i * step + hi))
            yield
    r.save(K_GL)
    r.save(K_SLOPE)
    yield K_DN
    dn = ready(K_DN)
    out = mm(r.gl[...], dn[...])
    y = (r.h2[...] + (out + r.vec[BD:BD + 1])).astype(BF)
    for m in range(z.MB):
        rows = slice(m * z.length, (m + 1) * z.length)
        pick = onehot(r.wanted[rows, :1] == iota((z.length, stream), 1))
        r.back_y[m] = mm_tn(pick, y[rows]).astype(BF)
    r.save(K_BACK_Y)


def backward_steps(z, ready, r):
    vec, back = r.vec, r.spt
    small = {}
    ones = lambda v: jnp.sum(v.astype(F32), 0, keepdims=True)
    def pieces(name, left, right):
        out, count = ready(name), r.cuts[name]
        size = out.shape[1] // count
        for c in range(count):
            yield from outer(left, right, out, c * size, (c + 1) * size)
            yield K_GRAD, name, c
    yield K_SAVED, (K_CT,)
    dn = ready(K_DN)
    small[BD] = ones(r.ct[...])
    step = z.ff // 4
    for i in range(4):
        at = slice(i * step, (i + 1) * step)
        yield K_TILE, i
        du = (mm_nt(r.ct[...], dn[at, :]) * r.slope_tile(i)).astype(BF)
        r.du[:, at] = du
        r.upb_sum[:, at] = ones(du)
    yield K_SAVED, (K_GL,)
    yield from outer(r.gl, r.ct, ready(K_DN), 0, z.width)
    yield K_GRAD, K_DN, 0
    yield K_GRAD, K_DN, 1
    yield K_SAVED, (K_SPT, K_VEC, K_H2, K_N3)
    yield K_WEIGHT, K_UP
    dn3 = dense(mm_nt(r.du[...], ready(K_UP)[...]), back[...])
    dw, small[G3] = norm_back(r.h2[...], vec[G3:G3 + 1], dn3)
    dh = r.ct[...].astype(F32) + dw
    r.dh[...] = dh
    r.e[...] = dh.astype(BF)
    small[BC] = ones(dh.astype(BF))
    yield
    yield from pieces(K_UP, r.n3, r.du)
    yield K_WEIGHT, K_CO
    yield from project_nt(r.e, ready(K_CO), r.dc)
    yield K_SAVED, (K_C,)
    yield from pieces(K_CO, r.c, r.e)
    yield K_SAVED, (K_CQ, K_CKV, K_PC)
    yield from bwd_cross(z, r.cq, r.ckv, r.times, r.pc, r.dc, r.dcq, r.dckv)
    yield K_SAVED, (K_EP,)
    yield from pieces(K_KV, r.ep, r.dckv)
    yield K_WEIGHT, K_CQ
    yield K_SAVED, (K_H1, K_N2)
    dn2 = dense(mm_nt(r.dcq[...], ready(K_CQ)[...]), back[...])
    dw, small[G2] = norm_back(r.h1[...], vec[G2:G2 + 1], dn2)
    dh = r.dh[...] + dw
    r.dh[...] = dh
    r.e[...] = dh.astype(BF)
    small[BA] = ones(dh.astype(BF))
    yield
    yield from pieces(K_CQ, r.n2, r.dcq)
    yield K_WEIGHT, K_AO
    yield from project_nt(r.e, ready(K_AO), r.dc)
    yield K_SAVED, (K_A,)
    yield from pieces(K_AO, r.a, r.e)
    yield K_SAVED, (K_JOIN, K_PS)
    r.table[...] = jnp.zeros(r.table.shape, F32)
    yield from bwd_self(z, r.join, r.ps, r.dc, r.dq, r.table)
    yield K_WEIGHT, K_QKV
    yield K_SAVED, (K_X, K_N1)
    dn1 = dense(mm_nt(r.dq[...], ready(K_QKV)[...]), back[...])
    dw, small[G1] = norm_back(r.x[...], vec[G1:G1 + 1], dn1)
    dx = (r.dh[...] + dw).astype(BF)
    stream = r.back_x.shape[1]
    for m in range(z.MB):
        rows = slice(m * z.length, (m + 1) * z.length)
        pick = onehot(r.wanted[rows, :1] == iota((z.length, stream), 1))
        r.back_x[m] = mm_tn(pick, dx[rows]).astype(BF)
    yield K_GRAD, K_X, 0
    pack_smalls(z, small, r)
    yield K_GRAD, K_SMALL, 0
    yield from pieces(K_QKV, r.n1, r.dq)


def pool_steps(z, ready, r):
    yield K_WEIGHT, K_KV
    kv = ready(K_KV)
    size = z.wide // 4
    for i in range(4):
        at = slice(i * size, (i + 1) * size)
        r.pool_hi[:, at], r.pool_lo[:, at] = split2(mm_nt(r.dckv[...], kv[at, :]))
        yield
    part = z.keys // 2
    for i in range(z.MB * 2):
        rows = slice(i * part, (i + 1) * part)
        r.put_pool(i, mm(r.pool_hi[rows, :], r.spt[...]) + mm(r.pool_lo[rows, :], r.spt[...]))
        yield


def pack_smalls(z, small, r):
    vecs = jnp.concatenate([small.get(i, jnp.zeros((1, z.width), F32)) for i in range(8)], 0)
    per = z.width // GROUPS
    shape = (GROUPS * 8, z.width)
    mine = iota(shape, 0) // 8 == iota(shape, 1) // per
    take = onehot(iota((GROUPS * 8, 8), 0) % 8 == iota((GROUPS * 8, 8), 1))
    put = onehot(iota((z.width, 128), 0) % per == iota((z.width, 128), 1))
    total = jnp.zeros((GROUPS * 8, 128), F32)
    for v in split2(vecs):
        total += mm(jnp.where(mine, mm(take, v), 0.0).astype(BF), put)
    per = z.ff // GROUPS
    bias = jnp.zeros((GROUPS, 128), F32)
    for i in range(z.ff // tile):
        shape = (GROUPS, tile)
        mine = iota(shape, 0) == (iota(shape, 1) + i * tile) // per
        put = onehot((iota((tile, 128), 0) + i * tile) % per == iota((tile, 128), 1))
        for v in split2(r.upb_sum[:, i * tile:(i + 1) * tile]):
            bias += mm(jnp.where(mine, jnp.broadcast_to(v.astype(F32), shape), 0.0).astype(BF), put)
    width = z.length // NB
    per = NB // GROUPS
    shape = (GROUPS, z.length)
    table = jnp.zeros((GROUPS, 128), F32)
    for v in split2(table_grad(r.table[...])):
        for k in range(per):
            mine = onehot((z.length - 1 - iota(shape, 1)) // width == iota(shape, 0) * per + k)
            put = onehot(iota((HEADS, 128), 0) + k * HEADS == iota((HEADS, 128), 1))
            table += mm(mm_nt(mine, v).astype(BF), put)
    for which, v in ((UPB, bias), (REL, table)):
        take = onehot(iota((GROUPS * 8, GROUPS), 0) == iota((GROUPS * 8, GROUPS), 1) * 8 + which)
        for part in split2(v):
            total += mm(take, part)
    r.small_grad[...] = total


class Refs:
    def __init__(self, names, refs):
        for n, ref in zip(names, refs): setattr(self, n, ref)


def weight_shapes(z):
    return {K_QKV: (z.wide, 3 * z.att), K_AO: (z.att, z.width), K_CQ: (z.wide, z.att), K_KV: (z.wide, 2 * z.att),
            K_CO: (z.att, z.width), K_UP: (z.wide, z.ff), K_DN: (z.ff, z.width)}


def saved_shapes(z):
    R = z.rows
    S = jax.ShapeDtypeStruct
    pairs = HEADS // 2
    return {K_SPT: S((z.wide, z.width), BF), K_VEC: S((SMALLS, z.width), F32), K_EP: S((z.MB * z.keys, z.wide), BF),
            K_CKV: S((z.MB * z.keys, 2 * z.att), BF), K_X: S((R, z.width), F32), K_N1: S((R, z.wide), BF),
            K_JOIN: S((R, 3 * z.att), BF), K_PS: S((z.MB, pairs, 2 * z.length, z.length), F32), K_A: S((R, z.att), BF),
            K_H1: S((R, z.width), F32), K_N2: S((R, z.wide), BF), K_CQ: S((R, z.att), BF),
            K_PC: S((z.MB, pairs, z.keys // NL, 2 * z.win, NL), F32), K_C: S((R, z.att), BF), K_H2: S((R, z.width), F32),
            K_N3: S((R, z.wide), BF), K_GL: S((R, z.ff), BF), K_SLOPE: S((R, z.ff), F32), K_CT: S((R, z.width), BF)}


def forward_plain(z, gathered, wanted, times, pool):
    names = list(gathered)
    saved = saved_shapes(z)
    outs = {**saved, K_BACK_Y: jax.ShapeDtypeStruct(gathered[K_TOK].shape, BF)}
    share = {K_UP: K_QKV, K_CT: K_TOK}
    room = {k: gathered[k].shape for k in names if k not in share}
    room[K_QKV] = gathered[K_UP].shape
    def kernel(*refs):
        n = len(names)
        held = dict(zip(names, refs[:n]))
        r = Refs([K_WANTED, K_TIMES, K_POOL], refs[n:n + 3])
        r.__dict__.update(zip(outs, refs[n + 3:n + 3 + len(outs)]))
        scratch = refs[n + 3 + len(outs):]
        sems, r.bias, r.upb, r.sp = scratch[:4]
        bufs = dict(zip(room, scratch[4:]))
        def view(k):
            return bufs[K_QKV].at[:, :gathered[k].shape[1]] if k in (K_QKV, K_UP) else bufs[share.get(k, k)]
        def copy(k):
            return pltpu.make_async_copy(held[k], view(k), sems.at[names.index(k)])
        for k in room:
            copy(k).start()
        r.save = lambda k: None
        for k in forward_steps(z, view, r):
            if k in (K_UP0, K_CT):
                copy(k.rstrip(K_0)).start()
            if k == K_UP0 or k in names:
                copy(k.rstrip(K_0)).wait()
    V = pl.BlockSpec(memory_space=pltpu.VMEM)
    A = pl.BlockSpec(memory_space=pl.ANY)
    return dict(zip(outs, pl.pallas_call(kernel, name="layer_forward", out_shape=list(outs.values()),
        in_specs=[A] * len(names) + [V] * 3, out_specs=[V] * len(outs),
        scratch_shapes=[pltpu.SemaphoreType.DMA((len(names),)), pltpu.VMEM((HEADS, z.length, z.length), F32), pltpu.VMEM((1, z.ff), F32), pltpu.VMEM((z.width, z.wide), BF)]
            + [pltpu.VMEM(v, BF) for v in room.values()],
        compiler_params=pltpu.CompilerParams(vmem_limit_bytes=63 * MIB))(*gathered.values(), wanted, times, pool)))


def backward_plain(z, weights, saved, wanted, times):
    names = list(WEIGHTS)
    shapes = weight_shapes(z)
    ins = list(saved)
    S = jax.ShapeDtypeStruct
    outs = {K_POOL_GRAD: S((z.MB * z.keys, z.width), F32), K_BACK_X: S((z.MB, z.stream, z.width), BF), K_SMALL_GRAD: S((GROUPS * 8, 128), F32)}
    part = z.keys // 2
    local = {K_DU: ((z.rows, z.ff), BF), K_UPB_SUM: ((1, z.ff), F32), K_DH: ((z.rows, z.width), F32), K_E: ((z.rows, z.width), BF),
             K_DC: ((z.rows, z.att), BF), "dcq": ((z.rows, z.att), BF), "dckv": ((z.MB * z.keys, 2 * z.att), BF),
             K_TABLE: ((z.length, HEADS * z.length), F32), K_TILES: ((2, max(z.rows, part), z.ff // 4), F32)}
    kept = [k for k in names if k != K_QKV]

    def kernel(*refs):
        refs = list(refs)
        take = lambda k: [refs.pop(0) for _ in range(k)]
        held = dict(zip(names, take(len(names))))
        r = Refs(ins + [K_WANTED, K_TIMES], take(len(ins) + 2))
        grads = dict(zip(names, take(len(names))))
        r.__dict__.update(zip(outs, take(len(outs))))
        sems, gsem, tsem, psem = take(4)
        bufs = dict(zip(kept, take(len(kept))))
        bufs[K_QKV] = bufs[K_UP].at[:, :shapes[K_QKV][1]]
        r.__dict__.update(zip(local, take(len(local))))
        r.dq = r.du.at[:, :3 * z.att]
        load = lambda k: pltpu.make_async_copy(held[k], bufs[k], sems.at[names.index(k)])
        store = lambda k: pltpu.make_async_copy(bufs[k], grads[k], gsem.at[names.index(k)])
        step = z.ff // 4
        r.slope_tiles, r.pool_tiles = r.tiles.at[:, :z.rows], r.tiles.at[:, :part, :z.width]
        r.pool_hi, r.pool_lo = r.ep, bufs[K_UP].at[:z.MB * z.keys, :z.wide]
        slope = lambda i: pltpu.make_async_copy(r.slope.at[:, i * step:(i + 1) * step], r.slope_tiles.at[i % 2], tsem.at[i % 2])
        slope(0).start()
        for k in (K_DN, K_UP, K_CO, K_CQ, K_AO):
            load(k).start()
        def slope_tile(i):
            if i + 1 < 4:
                slope(i + 1).start()
            slope(i).wait()
            return r.slope_tiles[i % 2]
        pool_copy = lambda i: pltpu.make_async_copy(r.pool_tiles.at[i % 2], r.pool_grad.at[i * part:(i + 1) * part], psem.at[i % 2])
        def put_pool(i, value):
            if i >= 2:
                pool_copy(i - 2).wait()
            r.pool_tiles[i % 2] = value
            pool_copy(i).start()
        r.slope_tile, r.put_pool = slope_tile, put_pool
        r.cuts = dict.fromkeys(names, 1)
        load(K_DN).wait()
        for event in backward_steps(z, lambda k: bufs[k], r):
            kind, k = (event or (None, None))[:2]
            if kind == K_WEIGHT:
                load(k).wait()
            if kind == K_GRAD and k in names and event[2] == int(k == K_DN):
                store(k).start()
                if k == K_CO:
                    store(K_UP).wait()
                    load(K_QKV).start()
        store(K_KV).wait()
        store(K_QKV).wait()
        load(K_KV).start()
        for event in pool_steps(z, lambda k: bufs[k], r):
            if event:
                load(K_KV).wait()
        for k in names:
            if k not in (K_UP, K_KV, K_QKV):
                store(k).wait()
        for i in (z.MB * 2 - 2, z.MB * 2 - 1):
            pool_copy(i).wait()
    V = pl.BlockSpec(memory_space=pltpu.VMEM)
    A = pl.BlockSpec(memory_space=pl.ANY)
    D = pltpu.SemaphoreType.DMA
    res = pl.pallas_call(kernel, name="layer_backward", out_shape=[S(shapes[k], BF) for k in names] + list(outs.values()),
        in_specs=[A] * len(names) + [A if k == K_SLOPE else V for k in ins] + [V] * 2, out_specs=[A] * (len(names) + 1) + [V] * 2,
        scratch_shapes=[D((len(names),)), D((len(names),)), D((2,)), D((2,))] + [pltpu.VMEM(shapes[k], BF) for k in kept]
            + [pltpu.VMEM(*v) for v in local.values()],
        compiler_params=pltpu.CompilerParams(vmem_limit_bytes=63 * MIB))(*[weights[k] for k in names], *saved.values(), wanted, times)
    return dict(zip(names, res)), dict(zip(outs, res[len(names):]))


MESH = pl.DeviceIdType.MESH

def when(pred, fn):
    if pred is None: fn()
    else: pl.when(pred)(fn)

def both(a, b):
    if a is None: return b
    if b is None: return a
    return jnp.logical_and(a, b)

class Place:
    def __init__(self, nz):
        dp, fs = lax.axis_index(K_DP), lax.axis_index(K_FSDP)
        self.nz = nz
        self.y, self.x = dp // 2, lax.rem(dp, 2)
        self.z, self.c = fs // 2, lax.rem(fs, 2)
        y, x, z, c = self.y, self.x, self.z, self.c
        self.y1, self.x1 = y + c * (1 - 2 * y), x + (1 - c) * (1 - 2 * x)
        self.y2, self.x2 = y + (1 - c) * (1 - 2 * y), x + c * (1 - 2 * x)
        self.yo, self.xo = 1 - y, 1 - x
        self.first = {K_DP: self.y1 * 2 + self.x1, K_FSDP: fs}
        self.second = {K_DP: self.y2 * 2 + self.x2, K_FSDP: fs}
        self.pair = {K_DP: dp, K_FSDP: z * 2 + 1 - c}
        self.up = {K_DP: dp, K_FSDP: fs + 2}
        self.down = {K_DP: dp, K_FSDP: fs - 2}
        self.has_up, self.has_down = z < nz - 1, z > 0

    def barrier(self):
        bar = pltpu.get_barrier_semaphore()
        ways = [(None, self.pair), (None, self.first), (None, self.second), (self.has_up, self.up), (self.has_down, self.down)]
        for pred, dev in ways:
            when(pred, lambda dev=dev: pl.semaphore_signal(bar, inc=1, device_id=dev, device_id_type=MESH))
        pl.semaphore_wait(bar, 3 + jnp.minimum(self.z, 1) + jnp.minimum(self.nz - 1 - self.z, 1))

class Gather:
    def __init__(self, at, block, out, sems, line_only=False):
        self.at, self.block, self.out, self.line_only = at, block, out, line_only
        self.zs, self.zr, self.ps, self.pr, self.own = sems
        self.late = []

    def cell(self, z, c):
        p = self.at
        return self.out.at[:, z, c] if self.line_only else self.out.at[p.y, p.x, z, c]
    def line(self, y, x, c):
        return self.out.at[:, :, c] if self.line_only else self.out.at[y, x, :, c]
    def copy(self, src, dst, s, r, dev):
        return pltpu.make_async_remote_copy(src_ref=src, dst_ref=dst, send_sem=s, recv_sem=r, device_id=dev, device_id_type=MESH)
    def send(self, pred, src, dst, s, r, dev):
        def go():
            self.copy(src, dst, s, r, dev).start()
        when(pred, go)
        def done():
            self.copy(src, dst, s, r, dev).wait_send()
        self.late.append((pred, done))
    def arrived(self, pred, ref, s, r):
        when(pred, lambda: self.copy(ref, ref, s, r, self.at.pair).wait_recv())

    def across(self, pred, ref, block=None):
        p = self.at
        src = ref if block is None else block
        if not self.line_only:
            for k, dev in ((4, p.first), (5, p.second)):
                when(pred, lambda k=k, dev=dev: self.copy(src, ref, self.ps.at[k], self.pr.at[k], dev).start())
    def start(self):
        p = self.at
        mine = self.cell(p.z, p.c)
        self.send(p.has_up, self.block, mine, self.zs.at[0, 0], self.zr.at[0, 0], p.up)
        self.send(p.has_down, self.block, mine, self.zs.at[1, 0], self.zr.at[1, 0], p.down)
        self.across(None, mine, self.block)
        pltpu.make_async_copy(self.block, mine, self.own).start()
    def hop(self, j):
        p = self.at
        for way, pred, more, ref, dev in ((0, p.z >= j, p.has_up, self.cell(p.z - j, p.c), p.up),
                                          (1, p.z < p.nz - j, p.has_down, self.cell(p.z + j, p.c), p.down)):
            self.arrived(pred, ref, self.zs.at[way, j - 1], self.zr.at[way, j - 1])
            if j < p.nz - 1:
                self.send(both(pred, more), ref, ref, self.zs.at[way, j], self.zr.at[way, j], dev)
            self.across(pred, ref)
    def z_done(self):
        p = self.at
        pltpu.make_async_copy(self.block, self.cell(p.z, p.c), self.own).wait()
        mine = self.line(p.y, p.x, p.c)
        self.send(None, mine, mine, self.ps.at[0], self.pr.at[0], p.pair)
        if not self.line_only:
            for k in (4, 5):
                self.late.append((None, lambda k=k: self.copy(mine, mine, self.ps.at[k], self.pr.at[k], p.pair).wait_send()))
    def after_first(self):
        p = self.at
        if self.line_only: return
        got = self.line(p.y1, p.x1, p.c)
        self.arrived(None, got, self.ps.at[4], self.pr.at[4])
        self.send(None, got, got, self.ps.at[6], self.pr.at[6], p.second)
        self.send(None, got, got, self.ps.at[1], self.pr.at[1], p.pair)
    def after_second(self):
        p = self.at
        if self.line_only: return
        for k, (y, x) in enumerate(((p.y2, p.x2), (p.yo, p.xo))):
            got = self.line(y, x, p.c)
            self.arrived(None, got, self.ps.at[5 + k], self.pr.at[5 + k])
            self.send(None, got, got, self.ps.at[2 + k], self.pr.at[2 + k], p.pair)
    def whole(self):
        p = self.at
        lines = [(p.y, p.x)] if self.line_only else [(p.y, p.x), (p.y2, p.x2), (p.y1, p.x1), (p.yo, p.xo)]
        for k, (y, x) in enumerate(lines):
            self.arrived(None, self.line(y, x, 1 - p.c), self.ps.at[k], self.pr.at[k])
    def drain(self):
        for pred, done in self.late:
            when(pred, done)

def sem_shapes(n, nz):
    D = pltpu.SemaphoreType.DMA
    return [D((n, 2, nz)), D((n, 2, nz)), D((n, 8)), D((n, 8)), D((n,))]


def pad16(r):
    return (r + 15) // 16 * 16


PIECES = ((K_SMALL, 0), (K_KV, 0), (K_TOK, 0), (K_KV, 1), (K_TOK, 1), (K_QKV, 0), (K_QKV, 1), (K_QKV, 2), (K_AO, 0), (K_CT, 0), (K_CQ, 0),
          (K_CO, 0), (K_CT, 1), (K_UP, 0), (K_UP, 1), (K_UP, 2), (K_UP, 3), (K_DN, 0), (K_DN, 1))
lines_only = (K_TOK, K_CT)
first_lag, second_lag, whole_lag, send_ahead, units_per_step = 3, 5, 6, 2, 4


def piece(ref, name, c):
    cut = sum(k == name for k, _ in PIECES)
    if cut == 1:
        return ref
    if name in lines_only:
        return ref.at[c:c + 1]
    lead = (slice(None),) * (len(ref.shape) - 2)
    if name == K_DN:
        tiles = ref.shape[-2] // 16
        return ref.at[lead + (slice(tiles * c // cut * 16, tiles * (c + 1) // cut * 16),)]
    cols = ref.shape[-1] // cut
    return ref.at[lead + (slice(None), slice(c * cols, (c + 1) * cols))]


def forward_gather(z, arrays, wanted, times, pool, nz):
    names = list(arrays)
    S = jax.ShapeDtypeStruct
    whole, stages = {}, []
    for k, b in arrays.items():
        if k in lines_only:
            whole[k] = S((b.shape[0], nz, 2) + b.shape[1:], b.dtype)
            stages.append(pltpu.VMEM(b.shape, b.dtype))
        else:
            r = pad16(b.shape[0])
            whole[k] = S((2, 2, nz, 2, r, b.shape[1]), b.dtype)
            stages.append(pltpu.VMEM((r, b.shape[1]), b.dtype))
    saved = {**saved_shapes(z), K_BACK_Y: S((z.MB, z.stream, z.width), BF)}
    share = {K_UP: K_QKV, K_CT: K_TOK}
    room = {k: whole[k] for k in names if k not in share}
    room[K_QKV] = whole[K_UP]
    count = len(PIECES)

    def kernel(*refs):
        refs = list(refs)
        take = lambda k: [refs.pop(0) for _ in range(k)]
        blocks = dict(zip(names, take(len(names))))
        r = Refs([K_WANTED, K_TIMES, K_POOL], take(3))
        landed = dict(zip(names, take(len(names))))
        kept = dict(zip(saved, take(len(saved))))
        stage = dict(zip(names, take(len(names))))
        r.__dict__.update(zip(saved, take(len(saved))))
        bufs = dict(zip(room, take(len(room))))
        r.bias, r.upb, r.sp, loads, saves = take(5)
        sems = take(5)
        at = Place(nz)
        for k in names:
            b, s = blocks[k], stage[k]
            if s.shape == b.shape:
                s[...] = b[...]
            else:
                s[...] = jnp.zeros(s.shape, s.dtype)
                s[:b.shape[0], :] = b[...]
        at.barrier()
        gs = [Gather(at, piece(stage[k], k, c), piece(landed[k], k, c), [s.at[j] for s in sems], k in lines_only)
              for j, (k, c) in enumerate(PIECES)]

        def save(k):
            pltpu.make_async_copy(getattr(r, k), kept[k], saves.at[list(saved).index(k)]).start()
        r.save = save
        def buffer(k):
            if k in (K_QKV, K_UP):
                return bufs[K_QKV].at[:, :, :, :, :, :whole[k].shape[-1]]
            return bufs[share.get(k, k)]
        def load(j):
            k, c = PIECES[j]
            return pltpu.make_async_copy(piece(landed[k], k, c), piece(buffer(k), k, c), loads.at[j])
        def ready(k):
            b = bufs[share.get(k, k)]
            if k in lines_only:
                return b.reshape(z.MB, z.stream, z.width)
            flat = b.reshape(GROUPS * b.shape[-2], b.shape[-1])
            return flat.at[:, :whole[k].shape[-1]] if k in (K_QKV, K_UP) else flat

        there, started, waited = set(), set(), set()
        free = set(room)
        work = forward_steps(z, ready, r)
        state = {K_NEED: next(work), K_DONE: False}
        def start_loads():
            for j in sorted(there - started):
                if PIECES[j][0] in free:
                    load(j).start()
                    started.add(j)
        def advance(units):
            while units and not state[K_DONE]:
                need = state[K_NEED]
                if need:
                    if need == K_AO:
                        free.add(K_UP)
                    if need == K_QKV:
                        free.add(K_CT)
                    start_loads()
                    ask = {j for j, (k, c) in enumerate(PIECES) if k == need or k + str(c) == need}
                    if not ask <= started:
                        return
                    for j in sorted(ask - waited):
                        load(j).wait()
                    waited.update(ask)
                try:
                    state[K_NEED] = next(work)
                except StopIteration:
                    state[K_DONE] = True
                units -= 1

        for g in gs[:send_ahead]:
            g.start()
        for t in range(count + whole_lag):
            def stage_of(lag):
                return gs[t - lag] if 0 <= t - lag < count else None
            if t + send_ahead < count:
                gs[t + send_ahead].start()
            for j in range(1, nz):
                if g := stage_of(j - 1):
                    g.hop(j)
            if g := stage_of(nz - 2):
                g.z_done()
            if g := stage_of(first_lag):
                g.after_first()
            if g := stage_of(second_lag):
                g.after_second()
            if g := stage_of(whole_lag):
                g.whole()
                there.add(t - whole_lag)
                start_loads()
            advance(units_per_step if t < count + whole_lag - 1 else 1 << 20)
        for g in gs:
            g.drain()
        for i, k in enumerate(saved):
            pltpu.make_async_copy(getattr(r, k), kept[k], saves.at[i]).wait()

    V = pl.BlockSpec(memory_space=pltpu.VMEM)
    A = pl.BlockSpec(memory_space=pl.ANY)
    D = pltpu.SemaphoreType.DMA
    got = pl.pallas_call(kernel, name="gather_forward", out_shape=list(whole.values()) + list(saved.values()),
        in_specs=[V] * (len(names) + 3), out_specs=[A] * (len(names) + len(saved)),
        scratch_shapes=stages + [pltpu.VMEM(s.shape, s.dtype) for s in saved.values()] + [pltpu.VMEM(s.shape, s.dtype) for s in room.values()]
            + [pltpu.VMEM((HEADS, z.length, z.length), F32), pltpu.VMEM((1, z.ff), F32), pltpu.VMEM((z.width, z.wide), BF), D((count,)), D((len(saved),))] + sem_shapes(count, nz),
        compiler_params=pltpu.CompilerParams(collective_id=1, has_side_effects=True, vmem_limit_bytes=63 * MIB))(*arrays.values(), wanted, times, pool)
    flat = lambda k, v: v.reshape(-1, v.shape[-1])
    return {k: flat(k, v) for k, v in zip(names, got) if k in WEIGHTS}, dict(zip(saved, got[len(names):]))


CUTS = {K_DN: 2, K_UP: 4, K_CO: 1, K_KV: 2, K_CQ: 1, K_AO: 1, K_QKV: 6}
SUMS = tuple((k, c) for k in (K_Y, K_DN, K_UP, K_CO, K_KV, K_CQ, K_AO, K_X, K_SMALL, K_QKV) for c in range(CUTS.get(k, 1)))
early_lags, late_lags, late_pieces = (1, 3, 5, 7), (1, 2, 3, 4), 4


def lags_of(i, nz):
    pair, second, first, along = early_lags if i < len(SUMS) - late_pieces else late_lags
    return {K_PAIR: pair, K_SECOND: second, K_FIRST: first, **{h: along + h - 1 for h in range(1, nz)}, K_FINISH: along + nz - 1}


class Sum:
    def __init__(self, at, held, landing, out, sems, line_only, stages):
        self.at, self.held, self.out, self.line_only, self.stages = at, held, out, line_only, stages
        if line_only:
            self.rc, self.ru, self.rd = landing
        else:
            self.rc, self.r2, self.r1, self.ru, self.rd = landing
        self.ps, self.pr, self.us, self.ur, self.ds, self.dr = sems
        self.late = []
    def copy(self, src, dst, s, r, dev):
        return pltpu.make_async_remote_copy(src_ref=src, dst_ref=dst, send_sem=s, recv_sem=r, device_id=dev, device_id_type=MESH)
    def send(self, pred, src, dst, s, r, dev):
        when(pred, lambda: self.copy(src, dst, s, r, dev).start())
        self.late.append((pred, lambda: self.copy(src, dst, s, r, dev).wait_send()))
    def fetch(self, pred, ref, s, r):
        stage, sem = self.stages.room(ref)
        def go():
            self.copy(ref, ref, s, r, self.at.pair).wait_recv()
            pltpu.make_async_copy(ref, stage, sem).start()
        when(pred, go)
        def add(mine):
            def body():
                pltpu.make_async_copy(ref, stage, sem).wait()
                mine[...] = mine[...] + stage[...]
            when(pred, body)
        return add
    def line(self, y, x):
        return self.held.at[y, x, :, self.at.c]
    def cell(self, z):
        return self.held.at[:, z, self.at.c] if self.line_only else self.held.at[self.at.y, self.at.x, z, self.at.c]
    def start(self):
        p = self.at
        other = self.held.at[:, :, 1 - p.c] if self.line_only else self.held.at[:, :, :, 1 - p.c]
        self.send(None, other, self.rc, self.ps.at[0], self.pr.at[0], p.pair)
    def after_pair(self):
        p = self.at
        if self.line_only:
            add = self.fetch(None, self.rc, self.ps.at[0], self.pr.at[0])
            return [lambda: add(self.held.at[:, :, p.c])]
        stage, sem = self.stages.room(self.rc)
        self.copy(self.rc, self.rc, self.ps.at[0], self.pr.at[0], p.pair).wait_recv()
        fetch = pltpu.make_async_copy(self.rc, stage, sem)
        fetch.start()
        def adds():
            fetch.wait()
            def plus(y, x):
                mine = self.line(y, x)
                mine[...] = mine[...] + stage[y, x]
            for k, (y, x) in enumerate(((p.y2, p.x2), (p.yo, p.xo))):
                plus(y, x)
                self.send(None, self.line(y, x), self.r2.at[k], self.ps.at[1 + k], self.pr.at[1 + k], p.second)
            plus(p.y1, p.x1)
            plus(p.y, p.x)
        return [adds]
    def after_second(self):
        p = self.at
        if self.line_only:
            return []
        far = self.fetch(None, self.r2.at[1], self.ps.at[2], self.pr.at[2])
        near = self.fetch(None, self.r2.at[0], self.ps.at[1], self.pr.at[1])
        def adds():
            far(self.line(p.y1, p.x1))
            self.send(None, self.line(p.y1, p.x1), self.r1, self.ps.at[3], self.pr.at[3], p.first)
            near(self.line(p.y, p.x))
        return [adds]
    def after_first(self):
        if self.line_only:
            return []
        add = self.fetch(None, self.r1, self.ps.at[3], self.pr.at[3])
        return [lambda: add(self.line(self.at.y, self.at.x))]
    def z_step(self, h):
        p, nz = self.at, self.at.nz
        todo = []
        for j in range(nz - h, 0, -1):
            for here, goal, land, s, r, dev in ((p.z == h - 1, h - 1 + j, self.ru, self.us, self.ur, p.up),
                                                (p.z == nz - h, nz - h - j, self.rd, self.ds, self.dr, p.down)):
                add = self.fetch(here, land.at[j], s.at[j + 1], r.at[j]) if h > 1 else None
                def go(add=add, here=here, goal=goal, land=land, s=s, r=r, dev=dev, j=j):
                    if add:
                        add(self.cell(goal))
                    self.send(here, self.cell(goal), land.at[j - 1], s.at[j], r.at[j - 1], dev)
                todo.append(go)
        return todo
    def finish(self):
        p = self.at
        up = self.fetch(p.has_down, self.ru.at[0], self.us.at[1], self.ur.at[0])
        down = self.fetch(p.has_up, self.rd.at[0], self.ds.at[1], self.dr.at[0])
        def go():
            mine = self.cell(p.z)
            up(mine)
            down(mine)
            if self.line_only:
                self.out[...] = mine[...]
            else:
                self.out[...] = mine[...][:self.out.shape[0]].astype(self.out.dtype)
        return [go]
    def drain(self):
        for pred, done in self.late:
            when(pred, done)


class Stages:
    def __init__(self, pools, sems):
        self.pools, self.sems = pools, sems
        self.reset()
    def reset(self):
        self.used, self.count = {}, 0
    def room(self, ref):
        lead = ref.shape[:-1]
        n = 1
        for k in lead:
            n *= k
        key = (ref.shape[-1], jnp.dtype(ref.dtype).name)
        off = self.used.get(key, 0)
        self.used[key] = off + n
        sem = self.sems.at[self.count]
        self.count += 1
        return self.pools[key].at[off:off + n].reshape(ref.shape), sem


def landing_shapes(shape, line_only, nz):
    if line_only:
        m, _, _, r, n = shape
        return [(m, nz, r, n), (nz - 1, m, r, n), (nz - 1, m, r, n)]
    r, n = shape[-2:]
    return [(2, 2, nz, r, n), (2, nz, r, n), (nz, r, n), (nz - 1, r, n), (nz - 1, r, n)]


def sum_piece_shape(whole, name, c):
    cut = sum(k == name for k, _ in SUMS)
    r, n = whole[-2:]
    rows, cols = slice(0, r), slice(0, n)
    if name == K_DN:
        rows = slice(r // 16 * c // cut * 16, r // 16 * (c + 1) // cut * 16)
    elif cut > 1:
        cols = slice(n // cut * c, n // cut * (c + 1))
    return whole[:-2] + (rows.stop - rows.start, cols.stop - cols.start), rows, cols


def backward_scatter(z, weights, saved, back_y, wanted, times, shards, nz):
    names = list(WEIGHTS)
    shapes = weight_shapes(z)
    S = jax.ShapeDtypeStruct
    tok = z.length // 2
    blocked = {k: (2, 2, nz, 2, shapes[k][0] // GROUPS, shapes[k][1]) for k in names}
    blocked[K_SMALL] = (2, 2, nz, 2, 8, 128)
    blocked[K_Y] = blocked[K_X] = (z.MB, nz, 2, tok, z.width)
    kinds = {k: F32 if k == K_SMALL else BF for k in blocked}
    lines = (K_Y, K_X)
    placed = [sum_piece_shape(blocked[k], k, c) for k, c in SUMS]
    landings = [S(s, kinds[k]) for (k, c), (shape, _, _) in zip(SUMS, placed) for s in landing_shapes(shape, k in lines, nz)]
    outs = {K_POOL_GRAD: S((z.MB * z.keys, z.width), F32)}
    for k in names:
        outs[k] = S(shards[k].shape, F32)
    outs.update(small=S((8, 128), F32), y=S((z.MB, tok, z.width), BF), x=S((z.MB, tok, z.width), BF))
    part = z.keys // 2
    share = {K_H1: K_H2, K_X: K_H2, K_N2: K_N3, K_N1: K_N3, K_A: K_C, K_JOIN: K_GL, K_PS: K_PC}
    after = {(K_TILE, 0): (K_GL,), (K_TILE, 1): ("w up",), (K_TILE, 2): (K_SPT, K_VEC, K_H2, K_N3), (K_TILE, 3): (K_C, "w co"),
             (K_GRAD, K_DN, CUTS[K_DN] - 1): (K_JOIN, K_CQ, K_CKV), (K_GRAD, K_UP, 0): (K_PC, K_EP),
             (K_GRAD, K_UP, CUTS[K_UP] - 1): (K_H1, K_N2, "w cq"), (K_GRAD, K_CO, 0): (K_A, "w ao", "w qkv"),
             (K_GRAD, K_KV, 0): (K_PS,), (K_GRAD, K_CQ, 0): (K_X, K_N1)}
    room = {k: saved[k] for k in saved if k not in share and k != K_SLOPE}
    local = {K_DU: ((z.rows, z.ff), BF), K_UPB_SUM: ((1, z.ff), F32), K_DH: ((z.rows, z.width), F32), K_E: ((z.rows, z.width), BF),
             K_DC: ((z.rows, z.att), BF), K_TABLE: ((z.length, HEADS * z.length), F32),
             K_TILES: ((2, max(z.rows, part), max(z.ff // 4, z.width)), F32), K_SMALL_GRAD: ((2, 2, nz, 2, 8, 128), F32), "line": ((z.MB, nz, 2, tok, z.width), BF)}
    steps = max(i + max(lags_of(i, nz).values()) for i in range(len(SUMS))) + 1
    plan = {}
    most = [0]

    def schedule(t):
        return [(i, name) for i in range(len(SUMS)) for name, lag in lags_of(i, nz).items() if i + lag == t]
    def asks(i, name):
        (k, c), (shape, _, _) = SUMS[i], placed[i]
        got = landing_shapes(shape, k in lines, nz)
        if name == K_PAIR:
            return [got[0]]
        if name in (K_SECOND, K_FIRST):
            return [] if k in lines else [got[1][1:]] * 2 if name == K_SECOND else [got[2]]
        z_block = got[-1][1:]
        return [z_block] * 2 if name == K_FINISH else [z_block] * (2 * (nz - name) if name > 1 else 0)
    for t in range(steps):
        need, count = {}, 0
        for i, name in schedule(t):
            for s in asks(i, name):
                n = 1
                for d in s[:-1]:
                    n *= d
                key = (s[-1], jnp.dtype(kinds[SUMS[i][0]]).name)
                need[key] = need.get(key, 0) + n
                count += 1
        for key, n in need.items():
            plan[key] = max(plan.get(key, 0), n)
        most[0] = max(most[0], count)

    def kernel(*refs):
        refs = list(refs)
        take = lambda k: [refs.pop(0) for _ in range(k)]
        stored = dict(zip(names, take(len(names))))
        kept = dict(zip(saved, take(len(saved))))
        y_in = take(1)[0]
        r = Refs([K_WANTED, K_TIMES], take(2))
        result = dict(zip(outs, take(len(outs))))
        land = take(len(landings))
        bufs = dict(zip(names, take(len(names))))
        slots = dict(zip(room, take(len(room))))
        r.__dict__.update(zip(local, take(len(local))))
        pools = dict(zip(plan, take(len(plan))))
        wsem, ssem, tsem, psem, ysem, dsem, stage_sem = take(7)
        sems = take(6)
        at = Place(nz)
        def slot(k):
            ref = slots[share.get(k, k)]
            if k == K_JOIN:
                return ref.at[:, :3 * z.att]
            if k == K_PS:
                return ref.reshape(z.MB, HEADS // 2, 2 * z.win * z.pool, NL).at[:, :, :2 * z.length]
            return ref
        for k in saved:
            if k != K_SLOPE:
                setattr(r, k, slot(k))
        small_held = r.small_grad
        r.small_grad = small_held.reshape(GROUPS * 8, 128)
        r.dq, r.dcq, r.dckv = r.join, r.cq, r.ckv
        r.back_x = r.line.reshape(z.MB, z.stream, z.width)
        step = z.ff // 4
        slope_tiles, r.pool_tiles = r.tiles.at[:, :z.rows, :step], r.tiles.at[:, :part, :z.width]
        r.pool_hi, r.pool_lo = r.ep, bufs[K_UP].reshape(shapes[K_UP]).at[:z.MB * z.keys, 2 * z.att:2 * z.att + z.wide]
        held = {**bufs, K_SMALL: small_held, K_Y: r.line, K_X: r.line}
        load = lambda k: pltpu.make_async_copy(stored[k], bufs[k], wsem.at[names.index(k)])
        get = lambda k: pltpu.make_async_copy(kept[k], slot(k), ssem.at[list(saved).index(k)])
        slope = lambda i: pltpu.make_async_copy(kept[K_SLOPE].at[:, i * step:(i + 1) * step], slope_tiles.at[i % 2], tsem.at[i % 2])
        y_load = pltpu.make_async_copy(y_in, r.line, ysem)
        dn_load = lambda i: pltpu.make_async_copy(stored[K_DN].at[i // 2, i % 2], bufs[K_DN].at[i // 2, i % 2], dsem.at[i])
        get(K_CT).start()
        for i in range(4):
            dn_load(i).start()
            if i < 2:
                slope(i).start()
        y_load.start()
        begin = lambda k: load(k[2:]).start() if k[:2] == "w " else get(k).start()
        at.barrier()
        def slope_tile(i):
            slope(i).wait()
            return slope_tiles[i % 2]
        pool_copy = lambda i: pltpu.make_async_copy(r.pool_tiles.at[i % 2], result[K_POOL_GRAD].at[i * part:(i + 1) * part], psem.at[i % 2])
        def put_pool(i, value):
            if i >= 2:
                pool_copy(i - 2).wait()
            r.pool_tiles[i % 2] = value
            pool_copy(i).start()
        r.slope_tile, r.put_pool, r.cuts = slope_tile, put_pool, CUTS
        ready = lambda k: bufs[k].reshape(shapes[k])

        stages = Stages(pools, stage_sem)
        sums, spot = [], 0
        for i, ((k, c), (shape, rows, cols)) in enumerate(zip(SUMS, placed)):
            n = len(landing_shapes(shape, k in lines, nz))
            out = result[k]
            if k in names:
                lead = (slice(None),) * 4
                part_of = held[k].at[lead + (rows, cols)]
                last = min(rows.stop, out.shape[0])
                out = out.at[rows.start:last, cols]
            else:
                part_of = held[k]
            sums.append(Sum(at, part_of, land[spot:spot + n], out, [s.at[i] for s in sems], k in lines, stages))
            spot += n

        work = backward_steps(z, ready, r)
        made = set()
        def until(piece):
            if piece == (K_Y, 0):
                y_load.wait()
                return
            if piece == (K_X, 0):
                sums[0].drain()
                sums[0].late = []
            while piece not in made:
                event = next(work)
                kind = event and event[0]
                if kind == K_WEIGHT:
                    load(event[1]).wait()
                if kind == K_SAVED:
                    for k in event[1]:
                        get(k).wait()
                if kind == K_GRAD:
                    made.add(event[1:])
                if kind == K_TILE:
                    i = event[1]
                    dn_load(i).wait()
                    if 1 <= i <= 2:
                        slope(i + 1).start()
                for k in after.get(event, ()):
                    begin(k)

        spare = bufs[K_UP].at[:, :, :, :, :, :shapes[K_KV][1]]
        again = pltpu.make_async_copy(stored[K_KV], spare, wsem.at[names.index(K_KV)])
        pool_work = pool_steps(z, lambda k: bufs[K_UP].reshape(shapes[K_UP]).at[:, :shapes[K_KV][1]], r)
        def idle():
            event = next(pool_work, K_DONE)
            if event and event != K_DONE:
                again.wait()
                event = next(pool_work)
            return event != K_DONE

        for t in range(steps):
            if t < len(SUMS):
                until(SUMS[t])
                sums[t].start()
                if t + 1 == len(SUMS):
                    for i, (k, _) in enumerate(SUMS):
                        if k == K_UP:
                            sums[i].drain()
                            sums[i].late = []
                    again.start()
            for part_of_step in ((K_PAIR, K_SECOND, K_FIRST), None):
                todo = []
                stages.reset()
                for i, name in schedule(t):
                    s = sums[i]
                    if (part_of_step is None) == (name in (K_PAIR, K_SECOND, K_FIRST)):
                        continue
                    if name == K_FINISH:
                        todo += s.finish()
                    elif name == K_PAIR:
                        todo += s.after_pair()
                    elif name == K_SECOND:
                        todo += s.after_second()
                    elif name == K_FIRST:
                        todo += s.after_first()
                    else:
                        todo += s.z_step(name)
                if t >= len(SUMS):
                    idle()
                for go in todo:
                    go()
        while idle():
            pass
        for s in sums:
            s.drain()
        for i in (z.MB * 2 - 2, z.MB * 2 - 1):
            pool_copy(i).wait()

    V = pl.BlockSpec(memory_space=pltpu.VMEM)
    A = pl.BlockSpec(memory_space=pl.ANY)
    D = pltpu.SemaphoreType.DMA
    n = len(SUMS)
    got = pl.pallas_call(kernel, name="backward_scatter", out_shape=list(outs.values()) + landings,
        in_specs=[A] * (len(names) + len(saved) + 1) + [V] * 2,
        out_specs=[A] + [V] * (len(outs) - 1) + [A] * len(landings),
        scratch_shapes=[pltpu.VMEM(blocked[k], BF) for k in names] + [pltpu.VMEM(v.shape, v.dtype) for v in room.values()]
            + [pltpu.VMEM(*v) for v in local.values()] + [pltpu.VMEM((rows, key[0]), jnp.dtype(key[1])) for key, rows in plan.items()]
            + [D((len(names),)), D((len(saved),)), D((2,)), D((2,)), D, D((4,)), D((most[0],))]
            + [D((n, 4)), D((n, 4)), D((n, nz + 1)), D((n, nz + 1)), D((n, nz + 1)), D((n, nz + 1))],
        compiler_params=pltpu.CompilerParams(collective_id=2, has_side_effects=True, vmem_limit_bytes=63 * MIB),
    )(*[weights[k].reshape(blocked[k]) for k in names], *saved.values(), back_y.reshape(blocked[K_Y]), wanted, times)
    return dict(zip(outs, got))


def vectors(norm1_gain, norm2_gain, norm3_gain, attn_out_bias, cca_out_bias, ffw_down_bias, rel_table, ffw_up_bias):
    return [norm1_gain, norm2_gain, norm3_gain, attn_out_bias, cca_out_bias, ffw_down_bias, rel_table, ffw_up_bias]


def to_groups(v):
    small = v.shape[0] // GROUPS
    big = (small + 15) // 16 * 16
    return jnp.pad(v.reshape(GROUPS, small, -1), ((0, 0), (0, big - small), (0, 0))).reshape(GROUPS * big, -1)


def from_groups(v, rows):
    return v.reshape(GROUPS, v.shape[0] // GROUPS, -1)[:, :rows // GROUPS].reshape(rows, -1)


def copied(arrays):
    n = len(arrays)
    def kernel(*refs):
        copies = [pltpu.make_async_copy(refs[i], refs[n + i], refs[2 * n].at[i]) for i in range(n)]
        for c in copies:
            c.start()
        for c in copies:
            c.wait()
    A = pl.BlockSpec(memory_space=pl.ANY)
    return pl.pallas_call(kernel, name="copy_out", out_shape=[jax.ShapeDtypeStruct(v.shape, v.dtype) for v in arrays],
                          in_specs=[A] * n, out_specs=[A] * n, scratch_shapes=[pltpu.SemaphoreType.DMA((n,))])(*arrays)


def body(tokens, cotangent, lengths, deal, pool, neighbour_ids, norm1_gain, attn_qkv, attn_out, attn_out_bias, rel_table,
         norm2_gain, cca_query, cca_kv, cca_out, cca_out_bias, norm3_gain, ffw_up, ffw_up_bias, ffw_down, ffw_down_bias):
    members, member = lax.axis_size(K_FSDP), lax.axis_index(K_FSDP)
    devices = members * lax.axis_size(K_DP)
    MB, tok_rows, width = tokens.shape
    length = 2 * tok_rows
    z = Sizes(MB, length, width, HEADS * HEAD_DIM, ffw_up.shape[1], pool.shape[1])
    z.stream = members * tok_rows
    shards = {K_QKV: attn_qkv, K_AO: attn_out, K_CQ: cca_query, K_KV: cca_kv, K_CO: cca_out, K_UP: ffw_up, K_DN: ffw_down}
    vecs = vectors(norm1_gain, norm2_gain, norm3_gain, attn_out_bias, cca_out_bias, ffw_down_bias, rel_table, ffw_up_bias)

    ids = jnp.arange(members, dtype=jnp.int32)
    lens, dealt = lengths[:, 0], deal[:, 0]
    starts = jnp.sum(jnp.where(ids[None, :, None] > ids[None, None, :], lens[:, None, :], 0), 2)
    mine = dealt == member
    own_start = jnp.sum(jnp.where(mine, starts, 0), 1)
    own_len = jnp.sum(jnp.where(mine, lens, 0), 1)
    place = jnp.arange(length, dtype=jnp.int32)
    wanted = jnp.where(place[None] < own_len[:, None], own_start[:, None] + place[None], -1).reshape(-1)
    wanted = jnp.broadcast_to(wanted[:, None], (MB * length, 128))
    spans = length // CH
    ids3 = neighbour_ids.reshape(MB, spans, K_NB)
    held = jnp.sum((ids3[..., None] == jnp.arange(z.pool, dtype=jnp.int32)).astype(F32), 2)
    row = jnp.arange(low_row, length, dtype=jnp.int32)
    in_span = ((row[:, None] - (CH - 1)) // CH == jnp.arange(spans, dtype=jnp.int32)) & (row[:, None] >= CH - 1)
    times = jnp.sum(jnp.where(in_span[None, :, :, None], held[:, None], 0.0), 2)
    times = jnp.broadcast_to(times[..., None], times.shape + (NL,)).reshape(MB, z.win, z.keys)
    neighbours = pool.reshape(MB * z.keys, width)

    direct = lax.axis_size(K_DP) == 4 and members % 2 == 0 and devices == GROUPS
    nz = members // 2
    if direct:
        packed = jnp.concatenate([w for v in vecs for w in (v, jnp.zeros((128 - v.shape[0],), BF))] + [jnp.zeros(((SMALLS - 8) * 128,), BF)])
        packed = packed.reshape(SMALLS, 128)
        weights, saved = forward_gather(z, {K_SMALL: packed, K_TOK: tokens, K_CT: cotangent, **shards}, wanted, times, neighbours, nz)
        back_y = saved.pop(K_BACK_Y)
        outs = backward_scatter(z, weights, saved, back_y, wanted, times, shards, nz)
        small = outs.pop(K_SMALL)
        mine = dict(zip(outs, copied(list(outs.values()))))
        act, dx, outs = mine[K_Y], mine[K_X], mine
        parts = [small[i, :v.shape[0]] for i, v in enumerate(vecs)]
    else:
        whole = lambda v: lax.all_gather(v, (K_DP, K_FSDP), axis=0, tiled=True)
        rows = [jnp.pad(w, ((0, 0), (0, 128 - w.shape[1])))[:, None] for w in [whole(v).reshape(GROUPS, -1) for v in vecs]]
        packed = jnp.concatenate(rows + [jnp.zeros((GROUPS, SMALLS - 8, 128), BF)], 1).reshape(GROUPS * SMALLS, 128)
        gathered = {K_SMALL: packed, **{k: to_groups(whole(v)) for k, v in shards.items()},
                    K_TOK: lax.all_gather(tokens, K_FSDP, axis=1, tiled=True), K_CT: lax.all_gather(cotangent, K_FSDP, axis=1, tiled=True)}
        weights = {k: gathered[k] for k in WEIGHTS}
        saved = forward_plain(z, gathered, wanted, times, neighbours)
        back_y = saved.pop(K_BACK_Y)
        grads, outs = backward_plain(z, weights, saved, wanted, times)
        back_x, small = outs[K_BACK_X], outs[K_SMALL_GRAD]
        down = lambda v: lax.psum_scatter(v.astype(F32), (K_DP, K_FSDP), scatter_dimension=0, tiled=True)
        line = lambda v: lax.psum_scatter(v, K_FSDP, scatter_dimension=1, tiled=True)
        act, dx = line(back_y), line(back_x)
        mine = {k: down(from_groups(grads[k], shards[k].shape[0] * devices)) for k in shards}
        small = small.reshape(GROUPS, 8, 128)
        parts = [down(small[:, i, :v.shape[0] * devices // GROUPS].reshape(-1)) for i, v in enumerate(vecs)]
    g1, g2, g3, ba, bc, bd, rel, upb = parts
    return (act, dx, outs[K_POOL_GRAD].reshape(pool.shape), g1, mine[K_QKV], mine[K_AO], ba, rel, g2, mine[K_CQ], mine[K_KV],
            mine[K_CO], bc, g3, mine[K_UP], upb, mine[K_DN], bd)


def solution(mesh):
    everywhere = (K_DP, K_FSDP)
    rows, vec = P(everywhere, None), P(everywhere)
    slots = P(None, everywhere, None)
    return jax.shard_map(
        body,
        mesh=mesh,
        in_specs=(slots, slots, P(None, K_DP, None), P(None, K_DP, None), P(None, everywhere, None, None), slots,
                  vec, rows, rows, vec, vec, vec, rows, rows, rows, vec, vec, rows, vec, rows, vec),
        out_specs=(slots, slots, P(None, everywhere, None, None), vec, rows, rows, vec, vec, vec, rows, rows, rows, vec, vec,
                   rows, vec, rows, vec),
        check_vma=False,
    )
```

```python
from functools import partial

import jax
import jax.numpy as jnp
from jax import lax
from jax.experimental import pallas as pl
from jax.experimental.pallas import tpu as pltpu
from jax.sharding import PartitionSpec as P

K_0 = "0"
K_A = "a"
K_AO = "ao"
K_BACK_X = "back_x"
K_BACK_Y = "back_y"
K_C = "c"
K_CKV = "ckv"
K_CO = "co"
K_CQ = "cq"
K_CT = "ct"
K_DC = "dc"
K_DH = "dh"
K_DN = "dn"
K_DONE = "done"
K_DP = "dp"
K_DU = "du"
K_E = "e"
K_EP = "ep"
K_FINISH = "finish"
K_FIRST = "first"
K_FSDP = "fsdp"
K_GL = "gl"
K_GRAD = "grad"
K_H1 = "h1"
K_H2 = "h2"
K_JOIN = "join"
K_KV = "kv"
K_N1 = "n1"
K_N2 = "n2"
K_N3 = "n3"
K_NEED = "need"
K_PAIR = "pair"
K_PC = "pc"
K_POOL = "pool"
K_POOL_GRAD = "pool_grad"
K_PS = "ps"
K_QKV = "qkv"
K_SAVED = "saved"
K_SECOND = "second"
K_SLOPE = "slope"
K_SMALL = "small"
K_SMALL_GRAD = "small_grad"
K_SPT = "spt"
K_TABLE = "table"
K_TILE = "tile"
K_TILES = "tiles"
K_TIMES = "times"
K_TOK = "tok"
K_UP = "up"
K_UP0 = "up0"
K_UPB_SUM = "upb_sum"
K_VEC = "vec"
K_WANTED = "wanted"
K_WEIGHT = "weight"
K_X = "x"
K_Y = "y"
MIB = 1 << 20
F32, BF = jnp.float32, jnp.bfloat16
HEADS, HEAD_DIM, CH, NL, K_NB, NB = 16, 64, 64, 128, 2, 64
epsilon = 1e-06
masked_score = -1e30
tile = 512
unroll = 4
low_row = 48
GROUPS = 32
SMALLS = 16
G1, G2, G3, BA, BC, BD, REL, UPB = range(8)


def mm(a, b):
    return jnp.dot(a, b, preferred_element_type=F32)
def mm_tn(a, b):
    return lax.dot_general(a, b, (((0,), (0,)), ((), ())), preferred_element_type=F32)
def mm_nt(a, b):
    return lax.dot_general(a, b, (((1,), (1,)), ((), ())), preferred_element_type=F32)
def iota(shape, dim):
    return lax.broadcasted_iota(jnp.int32, shape, dim)
def onehot(cond):
    return jnp.where(cond, 1.0, 0.0).astype(BF)
def split2(v):
    hi = v.astype(BF)
    return hi, (v - hi.astype(F32)).astype(BF)
def columns(i, size):
    return pl.ds(pl.multiple_of(i * size, size), size)
def loop(count, body):
    def step(i, carry):
        body(i)
        return carry
    lax.fori_loop(0, count, step, 0)


def spread(width):
    small = width // GROUPS
    big = (small + 15) // 16 * 16
    row, col = iota((width, GROUPS * big), 0), iota((width, GROUPS * big), 1)
    return onehot((col // big == row // small) & (col % big == row % small))


def gather_up(width):
    small = width // GROUPS
    big = (small + 15) // 16 * 16
    row, col = iota((GROUPS * big, width), 1), iota((GROUPS * big, width), 0)
    return onehot((col // big == row // small) & (col % big == row % small))


def dense(v, back):
    hi, lo = split2(v)
    return mm(hi, back) + mm(lo, back)


def small_rows(packed, width):
    per = width // GROUPS
    put = onehot(iota((128, width), 0) == iota((128, width), 1) % per)
    placed = mm(packed, put)
    shape = (GROUPS * SMALLS, width)
    placed = jnp.where(iota(shape, 0) // SMALLS == iota(shape, 1) // per, placed, 0.0).astype(BF)
    take = onehot(iota((SMALLS, GROUPS * SMALLS), 1) % SMALLS == iota((SMALLS, GROUPS * SMALLS), 0))
    return mm(take, placed)


def table_rows(packed, length):
    per = NB * HEADS // GROUPS // HEADS
    width = length // NB
    take = onehot(iota((GROUPS, GROUPS * SMALLS), 1) == iota((GROUPS, GROUPS * SMALLS), 0) * SMALLS + REL)
    held = mm(take, packed).astype(BF)
    far = (length - iota((GROUPS, length), 1)) % length // width
    at = mm_tn(held, onehot(far // per == iota((GROUPS, length), 0)))
    which = (length - iota((HEADS, length), 1)) % length // width % per
    out = jnp.zeros((HEADS, length), F32)
    for k in range(per):
        out = jnp.where(which == k, at[k * HEADS:(k + 1) * HEADS], out)
    return out


def biases(rows, bias):
    length = bias.shape[1]
    below = iota((length, length), 0) >= iota((length, length), 1)
    for h in range(HEADS):
        wide = jnp.broadcast_to(rows[h:h + 1], (length, length))
        bias[h] = jnp.where(below, pltpu.roll(wide, 0, 1, stride=1, stride_axis=0), masked_score)


def rms(v):
    return lax.rsqrt(jnp.mean(v * v, -1, keepdims=True) + epsilon)


def norm(v, gain):
    return (v * rms(v) * gain).astype(BF)


def norm_back(v, gain, dn):
    r = rms(v)
    unit = v * r
    gained = dn * gain
    return r * (gained - unit * jnp.mean(gained * unit, -1, keepdims=True)), jnp.sum(dn * unit, 0, keepdims=True)


def halves(v):
    first = iota(v.shape, 1) < HEAD_DIM
    zero = jnp.zeros(v.shape, v.dtype)
    return jnp.concatenate([jnp.where(first, v, zero), jnp.where(first, zero, v)], 0)


def joined(v):
    n = v.shape[0] // 2
    return jnp.where(iota((n, v.shape[1]), 1) < HEAD_DIM, v[:n], v[n:])


def head_parts(count, parts, body):
    pairs = HEADS // 2
    total = count * pairs
    def step(i, carry):
        m, p = i // pairs, i % pairs
        body(m, p, p * 2 * HEAD_DIM)
        return carry
    for k in range(parts):
        lax.fori_loop(total * k // parts, total * (k + 1) // parts, step, 0, unroll=unroll)
        yield


class Sizes:
    def __init__(self, MB, length, width, att, ff, pool):
        self.MB, self.length, self.width, self.att, self.ff, self.pool = MB, length, width, att, ff, pool
        self.rows = MB * length
        self.win = length - low_row
        self.wide = GROUPS * ((width // GROUPS + 15) // 16 * 16)
        self.keys = pool * NL


def fwd_self(z, join, bias, ps, att):
    factor = HEAD_DIM ** -0.5
    def body(m, p, c):
        rows = pl.ds(pl.multiple_of(m * z.length, 128), z.length)
        at = lambda part: pl.ds(pl.multiple_of(part * z.att + c, 128), 128)
        q, k, v = join[rows, at(0)], join[rows, at(1)], join[rows, at(2)]
        s = mm_nt(halves(q), k) * factor + jnp.concatenate([bias[2 * p], bias[2 * p + 1]], 0)
        e = jnp.exp(s - jnp.max(s, -1, keepdims=True))
        soft = e * (1.0 / jnp.sum(e, -1, keepdims=True))
        ps[m, p] = soft
        att[rows, at(0)] = joined(mm(soft.astype(BF), v)).astype(BF)
    yield from head_parts(z.MB, 4, body)


def fwd_cross(z, cq, ckv, times, pc, c_out):
    factor = HEAD_DIM ** -0.5
    for m in range(z.MB):
        c_out[m * z.length:m * z.length + low_row] = jnp.zeros((low_row, z.att), BF)
    def body(m, p, c):
        rows = pl.ds(pl.multiple_of(m * z.length + low_row, 16), z.win)
        keys = pl.ds(pl.multiple_of(m * z.keys, 128), z.keys)
        at = lambda part: pl.ds(pl.multiple_of(part * z.att + c, 128), 128)
        q, k, v = cq[rows, at(0)], ckv[keys, at(0)], ckv[keys, at(1)]
        cnt = times[m]
        cnt = jnp.concatenate([cnt, cnt], 0)
        s = jnp.where(cnt > 0, mm_nt(halves(q), k) * factor, masked_score)
        e = jnp.exp(s - jnp.max(s, -1, keepdims=True))
        total = jnp.sum(e * cnt, -1, keepdims=True)
        soft = e * (1.0 / jnp.where(total > 0, total, 1.0))
        for k in range(z.keys // NL):
            pc[m, p, k] = soft[:, k * NL:(k + 1) * NL]
        c_out[rows, at(0)] = joined(mm((soft.astype(BF).astype(F32) * cnt).astype(BF), v)).astype(BF)
    yield from head_parts(z.MB, 4, body)


def gelu_parts(u):
    k = 0.7978845608028654
    t = jnp.tanh(k * (u + 0.044715 * u * u * u))
    half = 0.5 * (1.0 + t)
    return u * half, half + 0.5 * u * (1.0 - t * t) * k * (1.0 + 3 * 0.044715 * u * u)


def fwd_up(z, n3, up, upb, gl, slope, at):
    u = mm(n3[...], up[:, at]) + upb[:, at]
    value, d = gelu_parts(u)
    gl[:, at] = value.astype(BF)
    slope[:, at] = d


def project(left, weight, out, size=tile):
    for i in range(out.shape[1] // size):
        at = slice(i * size, (i + 1) * size)
        out[:, at] = mm(left[...], weight[:, at]).astype(out.dtype)
        yield


def project_nt(left, weight, out, size=tile):
    for i in range(out.shape[1] // size):
        at = slice(i * size, (i + 1) * size)
        out[:, at] = mm_nt(left[...], weight[at, :]).astype(out.dtype)
        yield


def outer(left, right, out, lo, hi, size=256):
    for i in range(out.shape[0] // size):
        at = slice(i * size, (i + 1) * size)
        out[at, lo:hi] = mm_tn(left[:, at], right[:, lo:hi]).astype(out.dtype)
        yield


def bwd_self(z, join, ps, da, dq, table_sum):
    factor = HEAD_DIM ** -0.5
    def body(m, p, c):
        rows = pl.ds(pl.multiple_of(m * z.length, 128), z.length)
        at = lambda part: pl.ds(pl.multiple_of(part * z.att + c, 128), 128)
        q, k, v = join[rows, at(0)], join[rows, at(1)], join[rows, at(2)]
        d = halves(da[rows, at(0)])
        soft = ps[m, p]
        dp = mm_nt(d, v)
        ds = (soft * (dp - jnp.sum(dp * soft, -1, keepdims=True))).astype(BF)
        dq[rows, at(0)] = (joined(mm(ds, k)) * factor).astype(BF)
        dq[rows, at(1)] = (mm_tn(ds, halves(q)) * factor).astype(BF)
        dq[rows, at(2)] = mm_tn(soft.astype(BF), d).astype(BF)
        wide = ds.astype(F32)
        for k in range(2):
            heads = pl.ds(pl.multiple_of((2 * p + k) * z.length, 128), z.length)
            table_sum[:, heads] += wide[k * z.length:(k + 1) * z.length]
    yield from head_parts(z.MB, 4, body)


def bwd_cross(z, cq, ckv, times, pc, dc, dcq, dckv):
    factor = HEAD_DIM ** -0.5
    for m in range(z.MB):
        dcq[m * z.length:m * z.length + low_row] = jnp.zeros((low_row, z.att), BF)
    def body(m, p, c):
        rows = pl.ds(pl.multiple_of(m * z.length + low_row, 16), z.win)
        keys = pl.ds(pl.multiple_of(m * z.keys, 128), z.keys)
        at = lambda part: pl.ds(pl.multiple_of(part * z.att + c, 128), 128)
        q, k, v = cq[rows, at(0)], ckv[keys, at(0)], ckv[keys, at(1)]
        d = halves(dc[rows, at(0)])
        cnt = times[m]
        cnt = jnp.concatenate([cnt, cnt], 0)
        soft = jnp.concatenate([pc[m, p, k] for k in range(z.keys // NL)], 1)
        dp = mm_nt(d, v)
        ds = (soft * (dp - jnp.sum(dp * soft * cnt, -1, keepdims=True))).astype(BF)
        ds = (ds.astype(F32) * cnt).astype(BF)
        pb = (soft.astype(BF).astype(F32) * cnt).astype(BF)
        dcq[rows, at(0)] = (joined(mm(ds, k)) * factor).astype(BF)
        dckv[keys, at(0)] = (mm_tn(ds, halves(q)) * factor).astype(BF)
        dckv[keys, at(1)] = mm_tn(pb, d).astype(BF)
    yield from head_parts(z.MB, 4, body)


def exact(a, b, dims):
    return lax.dot_general(a, b, (dims, ((), ())), precision=lax.Precision.HIGHEST, preferred_element_type=F32)


def table_grad(table_sum):
    length = table_sum.shape[0]
    flip = onehot(iota((length, length), 0) + iota((length, length), 1) == length - 1)
    hi, lo = split2(table_sum)
    flipped = mm(flip, hi) + mm(flip, lo)
    rows = []
    for h in range(HEADS):
        turned = pltpu.roll(flipped[:, h * length:(h + 1) * length], 0, 1, stride=1, stride_axis=0)
        rows.append(jnp.sum(turned, 0, keepdims=True))
    return jnp.concatenate(rows, 0)


WEIGHTS = (K_QKV, K_AO, K_CQ, K_KV, K_CO, K_UP, K_DN)


def forward_steps(z, ready, r):
    yield K_SMALL
    r.sp[...] = spread(z.width)
    r.spt[...] = gather_up(z.width)
    r.save(K_SPT)
    packed = ready(K_SMALL)[...]
    r.vec[...] = small_rows(packed, z.width)
    r.save(K_VEC)
    yield
    def upb(i):
        at = columns(i, tile)
        per = z.ff // GROUPS
        put = onehot(iota((128, tile), 0) == (iota((128, tile), 1) + i * tile) % per)
        placed = mm(packed, put)
        shape = (GROUPS * SMALLS, tile)
        mine = (iota(shape, 0) // SMALLS == (iota(shape, 1) + i * tile) // per) & (iota(shape, 0) % SMALLS == UPB)
        r.upb[:, at] = jnp.sum(jnp.where(mine, placed, 0.0), 0, keepdims=True)
    loop(z.ff // tile, upb)
    biases(table_rows(packed, z.length), r.bias)
    half = z.keys // 2
    for i in range(z.MB * 2):
        rows = slice(i * half, (i + 1) * half)
        r.ep[rows, :] = mm(r.pool[rows, :], r.sp[...]).astype(BF)
        yield
    r.save(K_EP)
    yield K_KV
    kv = ready(K_KV)
    yield from project(r.ep, kv, r.ckv, 256)
    r.save(K_CKV)
    yield K_TOK
    tok = ready(K_TOK)
    stream = tok.shape[1]
    for m in range(z.MB):
        rows = slice(m * z.length, (m + 1) * z.length)
        pick = onehot(r.wanted[rows, :1] == iota((z.length, stream), 1))
        r.x[rows] = mm(pick, tok[m])
    r.save(K_X)
    yield
    r.n1[...] = mm(norm(r.x[...], r.vec[G1:G1 + 1]), r.sp[...]).astype(BF)
    r.save(K_N1)
    yield K_QKV
    yield from project(r.n1, ready(K_QKV), r.join)
    r.save(K_JOIN)
    yield from fwd_self(z, r.join, r.bias, r.ps, r.a)
    r.save(K_PS)
    r.save(K_A)
    yield K_AO
    h1 = r.x[...] + (mm(r.a[...], ready(K_AO)[...]) + r.vec[BA:BA + 1])
    r.h1[...] = h1
    r.save(K_H1)
    r.n2[...] = mm(norm(h1, r.vec[G2:G2 + 1]), r.sp[...]).astype(BF)
    r.save(K_N2)
    yield K_CQ
    yield from project(r.n2, ready(K_CQ), r.cq)
    r.save(K_CQ)
    yield from fwd_cross(z, r.cq, r.ckv, r.times, r.pc, r.c)
    r.save(K_PC)
    r.save(K_C)
    yield K_CO
    h2 = r.h1[...] + (mm(r.c[...], ready(K_CO)[...]) + r.vec[BC:BC + 1])
    r.h2[...] = h2
    r.save(K_H2)
    r.n3[...] = mm(norm(h2, r.vec[G3:G3 + 1]), r.sp[...]).astype(BF)
    r.save(K_N3)
    yield K_CT
    ct = ready(K_CT)
    for m in range(z.MB):
        rows = slice(m * z.length, (m + 1) * z.length)
        pick = onehot(r.wanted[rows, :1] == iota((z.length, stream), 1))
        r.ct[rows] = mm(pick, ct[m]).astype(BF)
    r.save(K_CT)
    step = z.ff // 4
    for i in range(4):
        yield K_UP + str(i)
        cut = (step // 2 + 127) // 128 * 128
        for lo, hi in ((0, cut), (cut, step)):
            fwd_up(z, r.n3, ready(K_UP), r.upb, r.gl, r.slope, slice(i * step + lo, i * step + hi))
            yield
    r.save(K_GL)
    r.save(K_SLOPE)
    yield K_DN
    dn = ready(K_DN)
    out = mm(r.gl[...], dn[...])
    y = (r.h2[...] + (out + r.vec[BD:BD + 1])).astype(BF)
    for m in range(z.MB):
        rows = slice(m * z.length, (m + 1) * z.length)
        pick = onehot(r.wanted[rows, :1] == iota((z.length, stream), 1))
        r.back_y[m] = mm_tn(pick, y[rows]).astype(BF)
    r.save(K_BACK_Y)


def backward_steps(z, ready, r):
    vec, back = r.vec, r.spt
    small = {}
    ones = lambda v: jnp.sum(v.astype(F32), 0, keepdims=True)
    def pieces(name, left, right):
        out, count = ready(name), r.cuts[name]
        size = out.shape[1] // count
        for c in range(count):
            yield from outer(left, right, out, c * size, (c + 1) * size)
            yield K_GRAD, name, c
    yield K_SAVED, (K_CT,)
    dn = ready(K_DN)
    small[BD] = ones(r.ct[...])
    step = z.ff // 4
    for i in range(4):
        at = slice(i * step, (i + 1) * step)
        yield K_TILE, i
        du = (mm_nt(r.ct[...], dn[at, :]) * r.slope_tile(i)).astype(BF)
        r.du[:, at] = du
        r.upb_sum[:, at] = ones(du)
    yield K_SAVED, (K_GL,)
    yield from outer(r.gl, r.ct, ready(K_DN), 0, z.width)
    yield K_GRAD, K_DN, 0
    yield K_GRAD, K_DN, 1
    yield K_SAVED, (K_SPT, K_VEC, K_H2, K_N3)
    yield K_WEIGHT, K_UP
    dn3 = dense(mm_nt(r.du[...], ready(K_UP)[...]), back[...])
    dw, small[G3] = norm_back(r.h2[...], vec[G3:G3 + 1], dn3)
    dh = r.ct[...].astype(F32) + dw
    r.dh[...] = dh
    r.e[...] = dh.astype(BF)
    small[BC] = ones(dh.astype(BF))
    yield
    yield from pieces(K_UP, r.n3, r.du)
    yield K_WEIGHT, K_CO
    yield from project_nt(r.e, ready(K_CO), r.dc)
    yield K_SAVED, (K_C,)
    yield from pieces(K_CO, r.c, r.e)
    yield K_SAVED, (K_CQ, K_CKV, K_PC)
    yield from bwd_cross(z, r.cq, r.ckv, r.times, r.pc, r.dc, r.dcq, r.dckv)
    yield K_SAVED, (K_EP,)
    yield from pieces(K_KV, r.ep, r.dckv)
    yield K_WEIGHT, K_CQ
    yield K_SAVED, (K_H1, K_N2)
    dn2 = dense(mm_nt(r.dcq[...], ready(K_CQ)[...]), back[...])
    dw, small[G2] = norm_back(r.h1[...], vec[G2:G2 + 1], dn2)
    dh = r.dh[...] + dw
    r.dh[...] = dh
    r.e[...] = dh.astype(BF)
    small[BA] = ones(dh.astype(BF))
    yield
    yield from pieces(K_CQ, r.n2, r.dcq)
    yield K_WEIGHT, K_AO
    yield from project_nt(r.e, ready(K_AO), r.dc)
    yield K_SAVED, (K_A,)
    yield from pieces(K_AO, r.a, r.e)
    yield K_SAVED, (K_JOIN, K_PS)
    r.table[...] = jnp.zeros(r.table.shape, F32)
    yield from bwd_self(z, r.join, r.ps, r.dc, r.dq, r.table)
    yield K_WEIGHT, K_QKV
    yield K_SAVED, (K_X, K_N1)
    dn1 = dense(mm_nt(r.dq[...], ready(K_QKV)[...]), back[...])
    dw, small[G1] = norm_back(r.x[...], vec[G1:G1 + 1], dn1)
    dx = (r.dh[...] + dw).astype(BF)
    stream = r.back_x.shape[1]
    for m in range(z.MB):
        rows = slice(m * z.length, (m + 1) * z.length)
        pick = onehot(r.wanted[rows, :1] == iota((z.length, stream), 1))
        r.back_x[m] = mm_tn(pick, dx[rows]).astype(BF)
    yield K_GRAD, K_X, 0
    pack_smalls(z, small, r)
    yield K_GRAD, K_SMALL, 0
    yield from pieces(K_QKV, r.n1, r.dq)


def pool_steps(z, ready, r):
    yield K_WEIGHT, K_KV
    kv = ready(K_KV)
    size = z.wide // 4
    for i in range(4):
        at = slice(i * size, (i + 1) * size)
        r.pool_hi[:, at], r.pool_lo[:, at] = split2(mm_nt(r.dckv[...], kv[at, :]))
        yield
    part = z.keys // 2
    for i in range(z.MB * 2):
        rows = slice(i * part, (i + 1) * part)
        r.put_pool(i, mm(r.pool_hi[rows, :], r.spt[...]) + mm(r.pool_lo[rows, :], r.spt[...]))
        yield


def pack_smalls(z, small, r):
    vecs = jnp.concatenate([small.get(i, jnp.zeros((1, z.width), F32)) for i in range(8)], 0)
    per = z.width // GROUPS
    shape = (GROUPS * 8, z.width)
    mine = iota(shape, 0) // 8 == iota(shape, 1) // per
    take = onehot(iota((GROUPS * 8, 8), 0) % 8 == iota((GROUPS * 8, 8), 1))
    put = onehot(iota((z.width, 128), 0) % per == iota((z.width, 128), 1))
    total = jnp.zeros((GROUPS * 8, 128), F32)
    for v in split2(vecs):
        total += mm(jnp.where(mine, mm(take, v), 0.0).astype(BF), put)
    per = z.ff // GROUPS
    bias = jnp.zeros((GROUPS, 128), F32)
    for i in range(z.ff // tile):
        shape = (GROUPS, tile)
        mine = iota(shape, 0) == (iota(shape, 1) + i * tile) // per
        put = onehot((iota((tile, 128), 0) + i * tile) % per == iota((tile, 128), 1))
        for v in split2(r.upb_sum[:, i * tile:(i + 1) * tile]):
            bias += mm(jnp.where(mine, jnp.broadcast_to(v.astype(F32), shape), 0.0).astype(BF), put)
    width = z.length // NB
    per = NB // GROUPS
    shape = (GROUPS, z.length)
    table = jnp.zeros((GROUPS, 128), F32)
    for v in split2(table_grad(r.table[...])):
        for k in range(per):
            mine = onehot((z.length - 1 - iota(shape, 1)) // width == iota(shape, 0) * per + k)
            put = onehot(iota((HEADS, 128), 0) + k * HEADS == iota((HEADS, 128), 1))
            table += mm(mm_nt(mine, v).astype(BF), put)
    for which, v in ((UPB, bias), (REL, table)):
        take = onehot(iota((GROUPS * 8, GROUPS), 0) == iota((GROUPS * 8, GROUPS), 1) * 8 + which)
        for part in split2(v):
            total += mm(take, part)
    r.small_grad[...] = total


class Refs:
    def __init__(self, names, refs):
        for n, ref in zip(names, refs): setattr(self, n, ref)


def weight_shapes(z):
    return {K_QKV: (z.wide, 3 * z.att), K_AO: (z.att, z.width), K_CQ: (z.wide, z.att), K_KV: (z.wide, 2 * z.att),
            K_CO: (z.att, z.width), K_UP: (z.wide, z.ff), K_DN: (z.ff, z.width)}


def saved_shapes(z):
    R = z.rows
    S = jax.ShapeDtypeStruct
    pairs = HEADS // 2
    return {K_SPT: S((z.wide, z.width), BF), K_VEC: S((SMALLS, z.width), F32), K_EP: S((z.MB * z.keys, z.wide), BF),
            K_CKV: S((z.MB * z.keys, 2 * z.att), BF), K_X: S((R, z.width), F32), K_N1: S((R, z.wide), BF),
            K_JOIN: S((R, 3 * z.att), BF), K_PS: S((z.MB, pairs, 2 * z.length, z.length), F32), K_A: S((R, z.att), BF),
            K_H1: S((R, z.width), F32), K_N2: S((R, z.wide), BF), K_CQ: S((R, z.att), BF),
            K_PC: S((z.MB, pairs, z.keys // NL, 2 * z.win, NL), F32), K_C: S((R, z.att), BF), K_H2: S((R, z.width), F32),
            K_N3: S((R, z.wide), BF), K_GL: S((R, z.ff), BF), K_SLOPE: S((R, z.ff), F32), K_CT: S((R, z.width), BF)}


def forward_plain(z, gathered, wanted, times, pool):
    names = list(gathered)
    saved = saved_shapes(z)
    outs = {**saved, K_BACK_Y: jax.ShapeDtypeStruct(gathered[K_TOK].shape, BF)}
    share = {K_UP: K_QKV, K_CT: K_TOK}
    room = {k: gathered[k].shape for k in names if k not in share}
    room[K_QKV] = gathered[K_UP].shape
    def kernel(*refs):
        n = len(names)
        held = dict(zip(names, refs[:n]))
        r = Refs([K_WANTED, K_TIMES, K_POOL], refs[n:n + 3])
        r.__dict__.update(zip(outs, refs[n + 3:n + 3 + len(outs)]))
        scratch = refs[n + 3 + len(outs):]
        sems, r.bias, r.upb, r.sp = scratch[:4]
        bufs = dict(zip(room, scratch[4:]))
        def view(k):
            return bufs[K_QKV].at[:, :gathered[k].shape[1]] if k in (K_QKV, K_UP) else bufs[share.get(k, k)]
        def copy(k):
            return pltpu.make_async_copy(held[k], view(k), sems.at[names.index(k)])
        for k in room:
            copy(k).start()
        r.save = lambda k: None
        for k in forward_steps(z, view, r):
            if k in (K_UP0, K_CT):
                copy(k.rstrip(K_0)).start()
            if k == K_UP0 or k in names:
                copy(k.rstrip(K_0)).wait()
    V = pl.BlockSpec(memory_space=pltpu.VMEM)
    A = pl.BlockSpec(memory_space=pl.ANY)
    return dict(zip(outs, pl.pallas_call(kernel, name="layer_forward", out_shape=list(outs.values()),
        in_specs=[A] * len(names) + [V] * 3, out_specs=[V] * len(outs),
        scratch_shapes=[pltpu.SemaphoreType.DMA((len(names),)), pltpu.VMEM((HEADS, z.length, z.length), F32), pltpu.VMEM((1, z.ff), F32), pltpu.VMEM((z.width, z.wide), BF)]
            + [pltpu.VMEM(v, BF) for v in room.values()],
        compiler_params=pltpu.CompilerParams(vmem_limit_bytes=63 * MIB))(*gathered.values(), wanted, times, pool)))


def backward_plain(z, weights, saved, wanted, times):
    names = list(WEIGHTS)
    shapes = weight_shapes(z)
    ins = list(saved)
    S = jax.ShapeDtypeStruct
    outs = {K_POOL_GRAD: S((z.MB * z.keys, z.width), F32), K_BACK_X: S((z.MB, z.stream, z.width), BF), K_SMALL_GRAD: S((GROUPS * 8, 128), F32)}
    part = z.keys // 2
    local = {K_DU: ((z.rows, z.ff), BF), K_UPB_SUM: ((1, z.ff), F32), K_DH: ((z.rows, z.width), F32), K_E: ((z.rows, z.width), BF),
             K_DC: ((z.rows, z.att), BF), "dcq": ((z.rows, z.att), BF), "dckv": ((z.MB * z.keys, 2 * z.att), BF),
             K_TABLE: ((z.length, HEADS * z.length), F32), K_TILES: ((2, max(z.rows, part), z.ff // 4), F32)}
    kept = [k for k in names if k != K_QKV]

    def kernel(*refs):
        refs = list(refs)
        take = lambda k: [refs.pop(0) for _ in range(k)]
        held = dict(zip(names, take(len(names))))
        r = Refs(ins + [K_WANTED, K_TIMES], take(len(ins) + 2))
        grads = dict(zip(names, take(len(names))))
        r.__dict__.update(zip(outs, take(len(outs))))
        sems, gsem, tsem, psem = take(4)
        bufs = dict(zip(kept, take(len(kept))))
        bufs[K_QKV] = bufs[K_UP].at[:, :shapes[K_QKV][1]]
        r.__dict__.update(zip(local, take(len(local))))
        r.dq = r.du.at[:, :3 * z.att]
        load = lambda k: pltpu.make_async_copy(held[k], bufs[k], sems.at[names.index(k)])
        store = lambda k: pltpu.make_async_copy(bufs[k], grads[k], gsem.at[names.index(k)])
        step = z.ff // 4
        r.slope_tiles, r.pool_tiles = r.tiles.at[:, :z.rows], r.tiles.at[:, :part, :z.width]
        r.pool_hi, r.pool_lo = r.ep, bufs[K_UP].at[:z.MB * z.keys, :z.wide]
        slope = lambda i: pltpu.make_async_copy(r.slope.at[:, i * step:(i + 1) * step], r.slope_tiles.at[i % 2], tsem.at[i % 2])
        slope(0).start()
        for k in (K_DN, K_UP, K_CO, K_CQ, K_AO):
            load(k).start()
        def slope_tile(i):
            if i + 1 < 4:
                slope(i + 1).start()
            slope(i).wait()
            return r.slope_tiles[i % 2]
        pool_copy = lambda i: pltpu.make_async_copy(r.pool_tiles.at[i % 2], r.pool_grad.at[i * part:(i + 1) * part], psem.at[i % 2])
        def put_pool(i, value):
            if i >= 2:
                pool_copy(i - 2).wait()
            r.pool_tiles[i % 2] = value
            pool_copy(i).start()
        r.slope_tile, r.put_pool = slope_tile, put_pool
        r.cuts = dict.fromkeys(names, 1)
        load(K_DN).wait()
        for event in backward_steps(z, lambda k: bufs[k], r):
            kind, k = (event or (None, None))[:2]
            if kind == K_WEIGHT:
                load(k).wait()
            if kind == K_GRAD and k in names and event[2] == int(k == K_DN):
                store(k).start()
                if k == K_CO:
                    store(K_UP).wait()
                    load(K_QKV).start()
        store(K_KV).wait()
        store(K_QKV).wait()
        load(K_KV).start()
        for event in pool_steps(z, lambda k: bufs[k], r):
            if event:
                load(K_KV).wait()
        for k in names:
            if k not in (K_UP, K_KV, K_QKV):
                store(k).wait()
        for i in (z.MB * 2 - 2, z.MB * 2 - 1):
            pool_copy(i).wait()
    V = pl.BlockSpec(memory_space=pltpu.VMEM)
    A = pl.BlockSpec(memory_space=pl.ANY)
    D = pltpu.SemaphoreType.DMA
    res = pl.pallas_call(kernel, name="layer_backward", out_shape=[S(shapes[k], BF) for k in names] + list(outs.values()),
        in_specs=[A] * len(names) + [A if k == K_SLOPE else V for k in ins] + [V] * 2, out_specs=[A] * (len(names) + 1) + [V] * 2,
        scratch_shapes=[D((len(names),)), D((len(names),)), D((2,)), D((2,))] + [pltpu.VMEM(shapes[k], BF) for k in kept]
            + [pltpu.VMEM(*v) for v in local.values()],
        compiler_params=pltpu.CompilerParams(vmem_limit_bytes=63 * MIB))(*[weights[k] for k in names], *saved.values(), wanted, times)
    return dict(zip(names, res)), dict(zip(outs, res[len(names):]))


MESH = pl.DeviceIdType.MESH

def when(pred, fn):
    if pred is None: fn()
    else: pl.when(pred)(fn)

def both(a, b):
    if a is None: return b
    if b is None: return a
    return jnp.logical_and(a, b)

class Place:
    def __init__(self, nz):
        dp, fs = lax.axis_index(K_DP), lax.axis_index(K_FSDP)
        self.nz = nz
        self.y, self.x = dp // 2, lax.rem(dp, 2)
        self.z, self.c = fs // 2, lax.rem(fs, 2)
        y, x, z, c = self.y, self.x, self.z, self.c
        self.y1, self.x1 = y + c * (1 - 2 * y), x + (1 - c) * (1 - 2 * x)
        self.y2, self.x2 = y + (1 - c) * (1 - 2 * y), x + c * (1 - 2 * x)
        self.yo, self.xo = 1 - y, 1 - x
        self.first = {K_DP: self.y1 * 2 + self.x1, K_FSDP: fs}
        self.second = {K_DP: self.y2 * 2 + self.x2, K_FSDP: fs}
        self.pair = {K_DP: dp, K_FSDP: z * 2 + 1 - c}
        self.up = {K_DP: dp, K_FSDP: fs + 2}
        self.down = {K_DP: dp, K_FSDP: fs - 2}
        self.has_up, self.has_down = z < nz - 1, z > 0

    def barrier(self):
        bar = pltpu.get_barrier_semaphore()
        ways = [(None, self.pair), (None, self.first), (None, self.second), (self.has_up, self.up), (self.has_down, self.down)]
        for pred, dev in ways:
            when(pred, lambda dev=dev: pl.semaphore_signal(bar, inc=1, device_id=dev, device_id_type=MESH))
        pl.semaphore_wait(bar, 3 + jnp.minimum(self.z, 1) + jnp.minimum(self.nz - 1 - self.z, 1))

class Gather:
    def __init__(self, at, block, out, sems, line_only=False):
        self.at, self.block, self.out, self.line_only = at, block, out, line_only
        self.zs, self.zr, self.ps, self.pr, self.own = sems
        self.late = []

    def cell(self, z, c):
        p = self.at
        return self.out.at[:, z, c] if self.line_only else self.out.at[p.y, p.x, z, c]
    def line(self, y, x, c):
        return self.out.at[:, :, c] if self.line_only else self.out.at[y, x, :, c]
    def copy(self, src, dst, s, r, dev):
        return pltpu.make_async_remote_copy(src_ref=src, dst_ref=dst, send_sem=s, recv_sem=r, device_id=dev, device_id_type=MESH)
    def send(self, pred, src, dst, s, r, dev):
        def go():
            self.copy(src, dst, s, r, dev).start()
        when(pred, go)
        def done():
            self.copy(src, dst, s, r, dev).wait_send()
        self.late.append((pred, done))
    def arrived(self, pred, ref, s, r):
        when(pred, lambda: self.copy(ref, ref, s, r, self.at.pair).wait_recv())

    def across(self, pred, ref, block=None):
        p = self.at
        src = ref if block is None else block
        if not self.line_only:
            for k, dev in ((4, p.first), (5, p.second)):
                when(pred, lambda k=k, dev=dev: self.copy(src, ref, self.ps.at[k], self.pr.at[k], dev).start())
    def start(self):
        p = self.at
        mine = self.cell(p.z, p.c)
        self.send(p.has_up, self.block, mine, self.zs.at[0, 0], self.zr.at[0, 0], p.up)
        self.send(p.has_down, self.block, mine, self.zs.at[1, 0], self.zr.at[1, 0], p.down)
        self.across(None, mine, self.block)
        pltpu.make_async_copy(self.block, mine, self.own).start()
    def hop(self, j):
        p = self.at
        for way, pred, more, ref, dev in ((0, p.z >= j, p.has_up, self.cell(p.z - j, p.c), p.up),
                                          (1, p.z < p.nz - j, p.has_down, self.cell(p.z + j, p.c), p.down)):
            self.arrived(pred, ref, self.zs.at[way, j - 1], self.zr.at[way, j - 1])
            if j < p.nz - 1:
                self.send(both(pred, more), ref, ref, self.zs.at[way, j], self.zr.at[way, j], dev)
            self.across(pred, ref)
    def z_done(self):
        p = self.at
        pltpu.make_async_copy(self.block, self.cell(p.z, p.c), self.own).wait()
        mine = self.line(p.y, p.x, p.c)
        self.send(None, mine, mine, self.ps.at[0], self.pr.at[0], p.pair)
        if not self.line_only:
            for k in (4, 5):
                self.late.append((None, lambda k=k: self.copy(mine, mine, self.ps.at[k], self.pr.at[k], p.pair).wait_send()))
    def after_first(self):
        p = self.at
        if self.line_only: return
        got = self.line(p.y1, p.x1, p.c)
        self.arrived(None, got, self.ps.at[4], self.pr.at[4])
        self.send(None, got, got, self.ps.at[6], self.pr.at[6], p.second)
        self.send(None, got, got, self.ps.at[1], self.pr.at[1], p.pair)
    def after_second(self):
        p = self.at
        if self.line_only: return
        for k, (y, x) in enumerate(((p.y2, p.x2), (p.yo, p.xo))):
            got = self.line(y, x, p.c)
            self.arrived(None, got, self.ps.at[5 + k], self.pr.at[5 + k])
            self.send(None, got, got, self.ps.at[2 + k], self.pr.at[2 + k], p.pair)
    def whole(self):
        p = self.at
        lines = [(p.y, p.x)] if self.line_only else [(p.y, p.x), (p.y2, p.x2), (p.y1, p.x1), (p.yo, p.xo)]
        for k, (y, x) in enumerate(lines):
            self.arrived(None, self.line(y, x, 1 - p.c), self.ps.at[k], self.pr.at[k])
    def drain(self):
        for pred, done in self.late:
            when(pred, done)

def sem_shapes(n, nz):
    D = pltpu.SemaphoreType.DMA
    return [D((n, 2, nz)), D((n, 2, nz)), D((n, 8)), D((n, 8)), D((n,))]


def pad16(r):
    return (r + 15) // 16 * 16


PIECES = ((K_SMALL, 0), (K_KV, 0), (K_TOK, 0), (K_KV, 1), (K_TOK, 1), (K_QKV, 0), (K_QKV, 1), (K_QKV, 2), (K_AO, 0), (K_CT, 0), (K_CQ, 0),
          (K_CO, 0), (K_CT, 1), (K_UP, 0), (K_UP, 1), (K_UP, 2), (K_UP, 3), (K_DN, 0), (K_DN, 1))
lines_only = (K_TOK, K_CT)
first_lag, second_lag, whole_lag, send_ahead, units_per_step = 3, 5, 6, 2, 4


def piece(ref, name, c):
    cut = sum(k == name for k, _ in PIECES)
    if cut == 1:
        return ref
    if name in lines_only:
        return ref.at[c:c + 1]
    lead = (slice(None),) * (len(ref.shape) - 2)
    if name == K_DN:
        tiles = ref.shape[-2] // 16
        return ref.at[lead + (slice(tiles * c // cut * 16, tiles * (c + 1) // cut * 16),)]
    cols = ref.shape[-1] // cut
    return ref.at[lead + (slice(None), slice(c * cols, (c + 1) * cols))]


def forward_gather(z, arrays, wanted, times, pool, nz):
    names = list(arrays)
    S = jax.ShapeDtypeStruct
    whole, stages = {}, []
    for k, b in arrays.items():
        if k in lines_only:
            whole[k] = S((b.shape[0], nz, 2) + b.shape[1:], b.dtype)
            stages.append(pltpu.VMEM(b.shape, b.dtype))
        else:
            r = pad16(b.shape[0])
            whole[k] = S((2, 2, nz, 2, r, b.shape[1]), b.dtype)
            stages.append(pltpu.VMEM((r, b.shape[1]), b.dtype))
    saved = {**saved_shapes(z), K_BACK_Y: S((z.MB, z.stream, z.width), BF)}
    share = {K_UP: K_QKV, K_CT: K_TOK}
    room = {k: whole[k] for k in names if k not in share}
    room[K_QKV] = whole[K_UP]
    count = len(PIECES)

    def kernel(*refs):
        refs = list(refs)
        take = lambda k: [refs.pop(0) for _ in range(k)]
        blocks = dict(zip(names, take(len(names))))
        r = Refs([K_WANTED, K_TIMES, K_POOL], take(3))
        landed = dict(zip(names, take(len(names))))
        kept = dict(zip(saved, take(len(saved))))
        stage = dict(zip(names, take(len(names))))
        r.__dict__.update(zip(saved, take(len(saved))))
        bufs = dict(zip(room, take(len(room))))
        r.bias, r.upb, r.sp, loads, saves = take(5)
        sems = take(5)
        at = Place(nz)
        for k in names:
            b, s = blocks[k], stage[k]
            if s.shape == b.shape:
                s[...] = b[...]
            else:
                s[...] = jnp.zeros(s.shape, s.dtype)
                s[:b.shape[0], :] = b[...]
        at.barrier()
        gs = [Gather(at, piece(stage[k], k, c), piece(landed[k], k, c), [s.at[j] for s in sems], k in lines_only)
              for j, (k, c) in enumerate(PIECES)]

        def save(k):
            pltpu.make_async_copy(getattr(r, k), kept[k], saves.at[list(saved).index(k)]).start()
        r.save = save
        def buffer(k):
            if k in (K_QKV, K_UP):
                return bufs[K_QKV].at[:, :, :, :, :, :whole[k].shape[-1]]
            return bufs[share.get(k, k)]
        def load(j):
            k, c = PIECES[j]
            return pltpu.make_async_copy(piece(landed[k], k, c), piece(buffer(k), k, c), loads.at[j])
        def ready(k):
            b = bufs[share.get(k, k)]
            if k in lines_only:
                return b.reshape(z.MB, z.stream, z.width)
            flat = b.reshape(GROUPS * b.shape[-2], b.shape[-1])
            return flat.at[:, :whole[k].shape[-1]] if k in (K_QKV, K_UP) else flat

        there, started, waited = set(), set(), set()
        free = set(room)
        work = forward_steps(z, ready, r)
        state = {K_NEED: next(work), K_DONE: False}
        def start_loads():
            for j in sorted(there - started):
                if PIECES[j][0] in free:
                    load(j).start()
                    started.add(j)
        def advance(units):
            while units and not state[K_DONE]:
                need = state[K_NEED]
                if need:
                    if need == K_AO:
                        free.add(K_UP)
                    if need == K_QKV:
                        free.add(K_CT)
                    start_loads()
                    ask = {j for j, (k, c) in enumerate(PIECES) if k == need or k + str(c) == need}
                    if not ask <= started:
                        return
                    for j in sorted(ask - waited):
                        load(j).wait()
                    waited.update(ask)
                try:
                    state[K_NEED] = next(work)
                except StopIteration:
                    state[K_DONE] = True
                units -= 1

        for g in gs[:send_ahead]:
            g.start()
        for t in range(count + whole_lag):
            def stage_of(lag):
                return gs[t - lag] if 0 <= t - lag < count else None
            if t + send_ahead < count:
                gs[t + send_ahead].start()
            for j in range(1, nz):
                if g := stage_of(j - 1):
                    g.hop(j)
            if g := stage_of(nz - 2):
                g.z_done()
            if g := stage_of(first_lag):
                g.after_first()
            if g := stage_of(second_lag):
                g.after_second()
            if g := stage_of(whole_lag):
                g.whole()
                there.add(t - whole_lag)
                start_loads()
            advance(units_per_step if t < count + whole_lag - 1 else 1 << 20)
        for g in gs:
            g.drain()
        for i, k in enumerate(saved):
            pltpu.make_async_copy(getattr(r, k), kept[k], saves.at[i]).wait()

    V = pl.BlockSpec(memory_space=pltpu.VMEM)
    A = pl.BlockSpec(memory_space=pl.ANY)
    D = pltpu.SemaphoreType.DMA
    got = pl.pallas_call(kernel, name="gather_forward", out_shape=list(whole.values()) + list(saved.values()),
        in_specs=[V] * (len(names) + 3), out_specs=[A] * (len(names) + len(saved)),
        scratch_shapes=stages + [pltpu.VMEM(s.shape, s.dtype) for s in saved.values()] + [pltpu.VMEM(s.shape, s.dtype) for s in room.values()]
            + [pltpu.VMEM((HEADS, z.length, z.length), F32), pltpu.VMEM((1, z.ff), F32), pltpu.VMEM((z.width, z.wide), BF), D((count,)), D((len(saved),))] + sem_shapes(count, nz),
        compiler_params=pltpu.CompilerParams(collective_id=1, has_side_effects=True, vmem_limit_bytes=63 * MIB))(*arrays.values(), wanted, times, pool)
    flat = lambda k, v: v.reshape(-1, v.shape[-1])
    return {k: flat(k, v) for k, v in zip(names, got) if k in WEIGHTS}, dict(zip(saved, got[len(names):]))


CUTS = {K_DN: 2, K_UP: 4, K_CO: 1, K_KV: 2, K_CQ: 1, K_AO: 1, K_QKV: 6}
SUMS = tuple((k, c) for k in (K_Y, K_DN, K_UP, K_CO, K_KV, K_CQ, K_AO, K_X, K_SMALL, K_QKV) for c in range(CUTS.get(k, 1)))
early_lags, late_lags, late_pieces = (1, 3, 5, 7), (1, 2, 3, 4), 4


def lags_of(i, nz):
    pair, second, first, along = early_lags if i < len(SUMS) - late_pieces else late_lags
    return {K_PAIR: pair, K_SECOND: second, K_FIRST: first, **{h: along + h - 1 for h in range(1, nz)}, K_FINISH: along + nz - 1}


class Sum:
    def __init__(self, at, held, landing, out, sems, line_only, stages):
        self.at, self.held, self.out, self.line_only, self.stages = at, held, out, line_only, stages
        if line_only:
            self.rc, self.ru, self.rd = landing
        else:
            self.rc, self.r2, self.r1, self.ru, self.rd = landing
        self.ps, self.pr, self.us, self.ur, self.ds, self.dr = sems
        self.late = []
    def copy(self, src, dst, s, r, dev):
        return pltpu.make_async_remote_copy(src_ref=src, dst_ref=dst, send_sem=s, recv_sem=r, device_id=dev, device_id_type=MESH)
    def send(self, pred, src, dst, s, r, dev):
        when(pred, lambda: self.copy(src, dst, s, r, dev).start())
        self.late.append((pred, lambda: self.copy(src, dst, s, r, dev).wait_send()))
    def fetch(self, pred, ref, s, r):
        stage, sem = self.stages.room(ref)
        def go():
            self.copy(ref, ref, s, r, self.at.pair).wait_recv()
            pltpu.make_async_copy(ref, stage, sem).start()
        when(pred, go)
        def add(mine):
            def body():
                pltpu.make_async_copy(ref, stage, sem).wait()
                mine[...] = mine[...] + stage[...]
            when(pred, body)
        return add
    def line(self, y, x):
        return self.held.at[y, x, :, self.at.c]
    def cell(self, z):
        return self.held.at[:, z, self.at.c] if self.line_only else self.held.at[self.at.y, self.at.x, z, self.at.c]
    def start(self):
        p = self.at
        other = self.held.at[:, :, 1 - p.c] if self.line_only else self.held.at[:, :, :, 1 - p.c]
        self.send(None, other, self.rc, self.ps.at[0], self.pr.at[0], p.pair)
    def after_pair(self):
        p = self.at
        if self.line_only:
            add = self.fetch(None, self.rc, self.ps.at[0], self.pr.at[0])
            return [lambda: add(self.held.at[:, :, p.c])]
        stage, sem = self.stages.room(self.rc)
        self.copy(self.rc, self.rc, self.ps.at[0], self.pr.at[0], p.pair).wait_recv()
        fetch = pltpu.make_async_copy(self.rc, stage, sem)
        fetch.start()
        def adds():
            fetch.wait()
            def plus(y, x):
                mine = self.line(y, x)
                mine[...] = mine[...] + stage[y, x]
            for k, (y, x) in enumerate(((p.y2, p.x2), (p.yo, p.xo))):
                plus(y, x)
                self.send(None, self.line(y, x), self.r2.at[k], self.ps.at[1 + k], self.pr.at[1 + k], p.second)
            plus(p.y1, p.x1)
            plus(p.y, p.x)
        return [adds]
    def after_second(self):
        p = self.at
        if self.line_only:
            return []
        far = self.fetch(None, self.r2.at[1], self.ps.at[2], self.pr.at[2])
        near = self.fetch(None, self.r2.at[0], self.ps.at[1], self.pr.at[1])
        def adds():
            far(self.line(p.y1, p.x1))
            self.send(None, self.line(p.y1, p.x1), self.r1, self.ps.at[3], self.pr.at[3], p.first)
            near(self.line(p.y, p.x))
        return [adds]
    def after_first(self):
        if self.line_only:
            return []
        add = self.fetch(None, self.r1, self.ps.at[3], self.pr.at[3])
        return [lambda: add(self.line(self.at.y, self.at.x))]
    def z_step(self, h):
        p, nz = self.at, self.at.nz
        todo = []
        for j in range(nz - h, 0, -1):
            for here, goal, land, s, r, dev in ((p.z == h - 1, h - 1 + j, self.ru, self.us, self.ur, p.up),
                                                (p.z == nz - h, nz - h - j, self.rd, self.ds, self.dr, p.down)):
                add = self.fetch(here, land.at[j], s.at[j + 1], r.at[j]) if h > 1 else None
                def go(add=add, here=here, goal=goal, land=land, s=s, r=r, dev=dev, j=j):
                    if add:
                        add(self.cell(goal))
                    self.send(here, self.cell(goal), land.at[j - 1], s.at[j], r.at[j - 1], dev)
                todo.append(go)
        return todo
    def finish(self):
        p = self.at
        up = self.fetch(p.has_down, self.ru.at[0], self.us.at[1], self.ur.at[0])
        down = self.fetch(p.has_up, self.rd.at[0], self.ds.at[1], self.dr.at[0])
        def go():
            mine = self.cell(p.z)
            up(mine)
            down(mine)
            if self.line_only:
                self.out[...] = mine[...]
            else:
                self.out[...] = mine[...][:self.out.shape[0]].astype(self.out.dtype)
        return [go]
    def drain(self):
        for pred, done in self.late:
            when(pred, done)


class Stages:
    def __init__(self, pools, sems):
        self.pools, self.sems = pools, sems
        self.reset()
    def reset(self):
        self.used, self.count = {}, 0
    def room(self, ref):
        lead = ref.shape[:-1]
        n = 1
        for k in lead:
            n *= k
        key = (ref.shape[-1], jnp.dtype(ref.dtype).name)
        off = self.used.get(key, 0)
        self.used[key] = off + n
        sem = self.sems.at[self.count]
        self.count += 1
        return self.pools[key].at[off:off + n].reshape(ref.shape), sem


def landing_shapes(shape, line_only, nz):
    if line_only:
        m, _, _, r, n = shape
        return [(m, nz, r, n), (nz - 1, m, r, n), (nz - 1, m, r, n)]
    r, n = shape[-2:]
    return [(2, 2, nz, r, n), (2, nz, r, n), (nz, r, n), (nz - 1, r, n), (nz - 1, r, n)]


def sum_piece_shape(whole, name, c):
    cut = sum(k == name for k, _ in SUMS)
    r, n = whole[-2:]
    rows, cols = slice(0, r), slice(0, n)
    if name == K_DN:
        rows = slice(r // 16 * c // cut * 16, r // 16 * (c + 1) // cut * 16)
    elif cut > 1:
        cols = slice(n // cut * c, n // cut * (c + 1))
    return whole[:-2] + (rows.stop - rows.start, cols.stop - cols.start), rows, cols


def backward_scatter(z, weights, saved, back_y, wanted, times, shards, nz):
    names = list(WEIGHTS)
    shapes = weight_shapes(z)
    S = jax.ShapeDtypeStruct
    tok = z.length // 2
    blocked = {k: (2, 2, nz, 2, shapes[k][0] // GROUPS, shapes[k][1]) for k in names}
    blocked[K_SMALL] = (2, 2, nz, 2, 8, 128)
    blocked[K_Y] = blocked[K_X] = (z.MB, nz, 2, tok, z.width)
    kinds = {k: F32 if k == K_SMALL else BF for k in blocked}
    lines = (K_Y, K_X)
    placed = [sum_piece_shape(blocked[k], k, c) for k, c in SUMS]
    landings = [S(s, kinds[k]) for (k, c), (shape, _, _) in zip(SUMS, placed) for s in landing_shapes(shape, k in lines, nz)]
    outs = {K_POOL_GRAD: S((z.MB * z.keys, z.width), F32)}
    for k in names:
        outs[k] = S(shards[k].shape, F32)
    outs.update(small=S((8, 128), F32), y=S((z.MB, tok, z.width), BF), x=S((z.MB, tok, z.width), BF))
    part = z.keys // 2
    share = {K_H1: K_H2, K_X: K_H2, K_N2: K_N3, K_N1: K_N3, K_A: K_C, K_JOIN: K_GL, K_PS: K_PC}
    after = {(K_TILE, 0): (K_GL,), (K_TILE, 1): ("w up",), (K_TILE, 2): (K_SPT, K_VEC, K_H2, K_N3), (K_TILE, 3): (K_C, "w co"),
             (K_GRAD, K_DN, CUTS[K_DN] - 1): (K_JOIN, K_CQ, K_CKV), (K_GRAD, K_UP, 0): (K_PC, K_EP),
             (K_GRAD, K_UP, CUTS[K_UP] - 1): (K_H1, K_N2, "w cq"), (K_GRAD, K_CO, 0): (K_A, "w ao", "w qkv"),
             (K_GRAD, K_KV, 0): (K_PS,), (K_GRAD, K_CQ, 0): (K_X, K_N1)}
    room = {k: saved[k] for k in saved if k not in share and k != K_SLOPE}
    local = {K_DU: ((z.rows, z.ff), BF), K_UPB_SUM: ((1, z.ff), F32), K_DH: ((z.rows, z.width), F32), K_E: ((z.rows, z.width), BF),
             K_DC: ((z.rows, z.att), BF), K_TABLE: ((z.length, HEADS * z.length), F32),
             K_TILES: ((2, max(z.rows, part), max(z.ff // 4, z.width)), F32), K_SMALL_GRAD: ((2, 2, nz, 2, 8, 128), F32), "line": ((z.MB, nz, 2, tok, z.width), BF)}
    steps = max(i + max(lags_of(i, nz).values()) for i in range(len(SUMS))) + 1
    plan = {}
    most = [0]

    def schedule(t):
        return [(i, name) for i in range(len(SUMS)) for name, lag in lags_of(i, nz).items() if i + lag == t]
    def asks(i, name):
        (k, c), (shape, _, _) = SUMS[i], placed[i]
        got = landing_shapes(shape, k in lines, nz)
        if name == K_PAIR:
            return [got[0]]
        if name in (K_SECOND, K_FIRST):
            return [] if k in lines else [got[1][1:]] * 2 if name == K_SECOND else [got[2]]
        z_block = got[-1][1:]
        return [z_block] * 2 if name == K_FINISH else [z_block] * (2 * (nz - name) if name > 1 else 0)
    for t in range(steps):
        need, count = {}, 0
        for i, name in schedule(t):
            for s in asks(i, name):
                n = 1
                for d in s[:-1]:
                    n *= d
                key = (s[-1], jnp.dtype(kinds[SUMS[i][0]]).name)
                need[key] = need.get(key, 0) + n
                count += 1
        for key, n in need.items():
            plan[key] = max(plan.get(key, 0), n)
        most[0] = max(most[0], count)

    def kernel(*refs):
        refs = list(refs)
        take = lambda k: [refs.pop(0) for _ in range(k)]
        stored = dict(zip(names, take(len(names))))
        kept = dict(zip(saved, take(len(saved))))
        y_in = take(1)[0]
        r = Refs([K_WANTED, K_TIMES], take(2))
        result = dict(zip(outs, take(len(outs))))
        land = take(len(landings))
        bufs = dict(zip(names, take(len(names))))
        slots = dict(zip(room, take(len(room))))
        r.__dict__.update(zip(local, take(len(local))))
        pools = dict(zip(plan, take(len(plan))))
        wsem, ssem, tsem, psem, ysem, dsem, stage_sem = take(7)
        sems = take(6)
        at = Place(nz)
        def slot(k):
            ref = slots[share.get(k, k)]
            if k == K_JOIN:
                return ref.at[:, :3 * z.att]
            if k == K_PS:
                return ref.reshape(z.MB, HEADS // 2, 2 * z.win * z.pool, NL).at[:, :, :2 * z.length]
            return ref
        for k in saved:
            if k != K_SLOPE:
                setattr(r, k, slot(k))
        small_held = r.small_grad
        r.small_grad = small_held.reshape(GROUPS * 8, 128)
        r.dq, r.dcq, r.dckv = r.join, r.cq, r.ckv
        r.back_x = r.line.reshape(z.MB, z.stream, z.width)
        step = z.ff // 4
        slope_tiles, r.pool_tiles = r.tiles.at[:, :z.rows, :step], r.tiles.at[:, :part, :z.width]
        r.pool_hi, r.pool_lo = r.ep, bufs[K_UP].reshape(shapes[K_UP]).at[:z.MB * z.keys, 2 * z.att:2 * z.att + z.wide]
        held = {**bufs, K_SMALL: small_held, K_Y: r.line, K_X: r.line}
        load = lambda k: pltpu.make_async_copy(stored[k], bufs[k], wsem.at[names.index(k)])
        get = lambda k: pltpu.make_async_copy(kept[k], slot(k), ssem.at[list(saved).index(k)])
        slope = lambda i: pltpu.make_async_copy(kept[K_SLOPE].at[:, i * step:(i + 1) * step], slope_tiles.at[i % 2], tsem.at[i % 2])
        y_load = pltpu.make_async_copy(y_in, r.line, ysem)
        dn_load = lambda i: pltpu.make_async_copy(stored[K_DN].at[i // 2, i % 2], bufs[K_DN].at[i // 2, i % 2], dsem.at[i])
        get(K_CT).start()
        for i in range(4):
            dn_load(i).start()
            if i < 2:
                slope(i).start()
        y_load.start()
        begin = lambda k: load(k[2:]).start() if k[:2] == "w " else get(k).start()
        at.barrier()
        def slope_tile(i):
            slope(i).wait()
            return slope_tiles[i % 2]
        pool_copy = lambda i: pltpu.make_async_copy(r.pool_tiles.at[i % 2], result[K_POOL_GRAD].at[i * part:(i + 1) * part], psem.at[i % 2])
        def put_pool(i, value):
            if i >= 2:
                pool_copy(i - 2).wait()
            r.pool_tiles[i % 2] = value
            pool_copy(i).start()
        r.slope_tile, r.put_pool, r.cuts = slope_tile, put_pool, CUTS
        ready = lambda k: bufs[k].reshape(shapes[k])

        stages = Stages(pools, stage_sem)
        sums, spot = [], 0
        for i, ((k, c), (shape, rows, cols)) in enumerate(zip(SUMS, placed)):
            n = len(landing_shapes(shape, k in lines, nz))
            out = result[k]
            if k in names:
                lead = (slice(None),) * 4
                part_of = held[k].at[lead + (rows, cols)]
                last = min(rows.stop, out.shape[0])
                out = out.at[rows.start:last, cols]
            else:
                part_of = held[k]
            sums.append(Sum(at, part_of, land[spot:spot + n], out, [s.at[i] for s in sems], k in lines, stages))
            spot += n

        work = backward_steps(z, ready, r)
        made = set()
        def until(piece):
            if piece == (K_Y, 0):
                y_load.wait()
                return
            if piece == (K_X, 0):
                sums[0].drain()
                sums[0].late = []
            while piece not in made:
                event = next(work)
                kind = event and event[0]
                if kind == K_WEIGHT:
                    load(event[1]).wait()
                if kind == K_SAVED:
                    for k in event[1]:
                        get(k).wait()
                if kind == K_GRAD:
                    made.add(event[1:])
                if kind == K_TILE:
                    i = event[1]
                    dn_load(i).wait()
                    if 1 <= i <= 2:
                        slope(i + 1).start()
                for k in after.get(event, ()):
                    begin(k)

        spare = bufs[K_UP].at[:, :, :, :, :, :shapes[K_KV][1]]
        again = pltpu.make_async_copy(stored[K_KV], spare, wsem.at[names.index(K_KV)])
        pool_work = pool_steps(z, lambda k: bufs[K_UP].reshape(shapes[K_UP]).at[:, :shapes[K_KV][1]], r)
        def idle():
            event = next(pool_work, K_DONE)
            if event and event != K_DONE:
                again.wait()
                event = next(pool_work)
            return event != K_DONE

        for t in range(steps):
            if t < len(SUMS):
                until(SUMS[t])
                sums[t].start()
                if t + 1 == len(SUMS):
                    for i, (k, _) in enumerate(SUMS):
                        if k == K_UP:
                            sums[i].drain()
                            sums[i].late = []
                    again.start()
            for part_of_step in ((K_PAIR, K_SECOND, K_FIRST), None):
                todo = []
                stages.reset()
                for i, name in schedule(t):
                    s = sums[i]
                    if (part_of_step is None) == (name in (K_PAIR, K_SECOND, K_FIRST)):
                        continue
                    if name == K_FINISH:
                        todo += s.finish()
                    elif name == K_PAIR:
                        todo += s.after_pair()
                    elif name == K_SECOND:
                        todo += s.after_second()
                    elif name == K_FIRST:
                        todo += s.after_first()
                    else:
                        todo += s.z_step(name)
                if t >= len(SUMS):
                    idle()
                for go in todo:
                    go()
        while idle():
            pass
        for s in sums:
            s.drain()
        for i in (z.MB * 2 - 2, z.MB * 2 - 1):
            pool_copy(i).wait()

    V = pl.BlockSpec(memory_space=pltpu.VMEM)
    A = pl.BlockSpec(memory_space=pl.ANY)
    D = pltpu.SemaphoreType.DMA
    n = len(SUMS)
    got = pl.pallas_call(kernel, name="backward_scatter", out_shape=list(outs.values()) + landings,
        in_specs=[A] * (len(names) + len(saved) + 1) + [V] * 2,
        out_specs=[A] + [V] * (len(outs) - 1) + [A] * len(landings),
        scratch_shapes=[pltpu.VMEM(blocked[k], BF) for k in names] + [pltpu.VMEM(v.shape, v.dtype) for v in room.values()]
            + [pltpu.VMEM(*v) for v in local.values()] + [pltpu.VMEM((rows, key[0]), jnp.dtype(key[1])) for key, rows in plan.items()]
            + [D((len(names),)), D((len(saved),)), D((2,)), D((2,)), D, D((4,)), D((most[0],))]
            + [D((n, 4)), D((n, 4)), D((n, nz + 1)), D((n, nz + 1)), D((n, nz + 1)), D((n, nz + 1))],
        compiler_params=pltpu.CompilerParams(collective_id=2, has_side_effects=True, vmem_limit_bytes=63 * MIB),
    )(*[weights[k].reshape(blocked[k]) for k in names], *saved.values(), back_y.reshape(blocked[K_Y]), wanted, times)
    return dict(zip(outs, got))


def vectors(norm1_gain, norm2_gain, norm3_gain, attn_out_bias, cca_out_bias, ffw_down_bias, rel_table, ffw_up_bias):
    return [norm1_gain, norm2_gain, norm3_gain, attn_out_bias, cca_out_bias, ffw_down_bias, rel_table, ffw_up_bias]


def to_groups(v):
    small = v.shape[0] // GROUPS
    big = (small + 15) // 16 * 16
    return jnp.pad(v.reshape(GROUPS, small, -1), ((0, 0), (0, big - small), (0, 0))).reshape(GROUPS * big, -1)


def from_groups(v, rows):
    return v.reshape(GROUPS, v.shape[0] // GROUPS, -1)[:, :rows // GROUPS].reshape(rows, -1)


def body(tokens, cotangent, lengths, deal, pool, neighbour_ids, norm1_gain, attn_qkv, attn_out, attn_out_bias, rel_table,
         norm2_gain, cca_query, cca_kv, cca_out, cca_out_bias, norm3_gain, ffw_up, ffw_up_bias, ffw_down, ffw_down_bias):
    members, member = lax.axis_size(K_FSDP), lax.axis_index(K_FSDP)
    devices = members * lax.axis_size(K_DP)
    MB, tok_rows, width = tokens.shape
    length = 2 * tok_rows
    z = Sizes(MB, length, width, HEADS * HEAD_DIM, ffw_up.shape[1], pool.shape[1])
    z.stream = members * tok_rows
    shards = {K_QKV: attn_qkv, K_AO: attn_out, K_CQ: cca_query, K_KV: cca_kv, K_CO: cca_out, K_UP: ffw_up, K_DN: ffw_down}
    vecs = vectors(norm1_gain, norm2_gain, norm3_gain, attn_out_bias, cca_out_bias, ffw_down_bias, rel_table, ffw_up_bias)

    ids = jnp.arange(members, dtype=jnp.int32)
    lens, dealt = lengths[:, 0], deal[:, 0]
    starts = jnp.sum(jnp.where(ids[None, :, None] > ids[None, None, :], lens[:, None, :], 0), 2)
    mine = dealt == member
    own_start = jnp.sum(jnp.where(mine, starts, 0), 1)
    own_len = jnp.sum(jnp.where(mine, lens, 0), 1)
    place = jnp.arange(length, dtype=jnp.int32)
    wanted = jnp.where(place[None] < own_len[:, None], own_start[:, None] + place[None], -1).reshape(-1)
    wanted = jnp.broadcast_to(wanted[:, None], (MB * length, 128))
    spans = length // CH
    ids3 = neighbour_ids.reshape(MB, spans, K_NB)
    held = jnp.sum((ids3[..., None] == jnp.arange(z.pool, dtype=jnp.int32)).astype(F32), 2)
    row = jnp.arange(low_row, length, dtype=jnp.int32)
    in_span = ((row[:, None] - (CH - 1)) // CH == jnp.arange(spans, dtype=jnp.int32)) & (row[:, None] >= CH - 1)
    times = jnp.sum(jnp.where(in_span[None, :, :, None], held[:, None], 0.0), 2)
    times = jnp.broadcast_to(times[..., None], times.shape + (NL,)).reshape(MB, z.win, z.keys)
    neighbours = pool.reshape(MB * z.keys, width)

    direct = lax.axis_size(K_DP) == 4 and members % 2 == 0 and devices == GROUPS
    nz = members // 2
    if direct:
        packed = jnp.concatenate([w for v in vecs for w in (v, jnp.zeros((128 - v.shape[0],), BF))] + [jnp.zeros(((SMALLS - 8) * 128,), BF)])
        packed = packed.reshape(SMALLS, 128)
        weights, saved = forward_gather(z, {K_SMALL: packed, K_TOK: tokens, K_CT: cotangent, **shards}, wanted, times, neighbours, nz)
        back_y = saved.pop(K_BACK_Y)
        outs = backward_scatter(z, weights, saved, back_y, wanted, times, shards, nz)
        act, dx, small, mine = outs[K_Y], outs[K_X], outs[K_SMALL], outs
        parts = [small[i, :v.shape[0]] for i, v in enumerate(vecs)]
    else:
        whole = lambda v: lax.all_gather(v, (K_DP, K_FSDP), axis=0, tiled=True)
        rows = [jnp.pad(w, ((0, 0), (0, 128 - w.shape[1])))[:, None] for w in [whole(v).reshape(GROUPS, -1) for v in vecs]]
        packed = jnp.concatenate(rows + [jnp.zeros((GROUPS, SMALLS - 8, 128), BF)], 1).reshape(GROUPS * SMALLS, 128)
        gathered = {K_SMALL: packed, **{k: to_groups(whole(v)) for k, v in shards.items()},
                    K_TOK: lax.all_gather(tokens, K_FSDP, axis=1, tiled=True), K_CT: lax.all_gather(cotangent, K_FSDP, axis=1, tiled=True)}
        weights = {k: gathered[k] for k in WEIGHTS}
        saved = forward_plain(z, gathered, wanted, times, neighbours)
        back_y = saved.pop(K_BACK_Y)
        grads, outs = backward_plain(z, weights, saved, wanted, times)
        back_x, small = outs[K_BACK_X], outs[K_SMALL_GRAD]
        down = lambda v: lax.psum_scatter(v.astype(F32), (K_DP, K_FSDP), scatter_dimension=0, tiled=True)
        line = lambda v: lax.psum_scatter(v, K_FSDP, scatter_dimension=1, tiled=True)
        act, dx = line(back_y), line(back_x)
        mine = {k: down(from_groups(grads[k], shards[k].shape[0] * devices)) for k in shards}
        small = small.reshape(GROUPS, 8, 128)
        parts = [down(small[:, i, :v.shape[0] * devices // GROUPS].reshape(-1)) for i, v in enumerate(vecs)]
    g1, g2, g3, ba, bc, bd, rel, upb = parts
    return (act, dx, outs[K_POOL_GRAD].reshape(pool.shape), g1, mine[K_QKV], mine[K_AO], ba, rel, g2, mine[K_CQ], mine[K_KV],
            mine[K_CO], bc, g3, mine[K_UP], upb, mine[K_DN], bd)


def solution(mesh):
    everywhere = (K_DP, K_FSDP)
    rows, vec = P(everywhere, None), P(everywhere)
    slots = P(None, everywhere, None)
    return jax.shard_map(
        body,
        mesh=mesh,
        in_specs=(slots, slots, P(None, K_DP, None), P(None, K_DP, None), P(None, everywhere, None, None), slots,
                  vec, rows, rows, vec, vec, vec, rows, rows, rows, vec, vec, rows, vec, rows, vec),
        out_specs=(slots, slots, P(None, everywhere, None, None), vec, rows, rows, vec, vec, vec, rows, rows, rows, vec, vec,
                   rows, vec, rows, vec),
        check_vma=False,
    )
```
